32 devices in a mesh: groups: 2 (over y), tile: 4 (over z), tm: 4 (over x, core).
Axes of the slice: x: 2, y: 2, z: 4, core: 2. Of those that a mesh axis runs over, the one named last changes fastest.
Arguments:
- multiplier: float32 [8, 8, 64, 512], P(('groups', 'tm'), None, 'tile'), parts along dimension 0, may hold values from -6 to 6
- increment: float32 [8, 8, 64, 512], P(('groups', 'tm'), None, 'tile'), parts along dimension 0, may hold values from -6 to 6
- obs_dual: float32 [8, 2048], P(('groups', 'tm'), 'tile'), parts along dimension 0, may hold values from -6 to 6
- rhs_model: float32 [8, 8, 64, 512], P(('groups', 'tm'), None, 'tile'), parts along dimension 0, may hold values from -6 to 6
- rhs_obs: float32 [8, 2048], P(('groups', 'tm'), 'tile'), parts along dimension 0, may hold values from -6 to 6
- model_err: float32 [8, 8, 64, 512], P(('groups', 'tm'), None, 'tile'), parts along dimension 0, may hold values from 0.2 to 2
- obs_err: float32 [8, 2048], P(('groups', 'tm'), 'tile'), parts along dimension 0, may hold values from 0.25 to 4
- drift_east: float32 [8, 8, 64, 512], P(('groups', 'tm'), None, 'tile'), parts along dimension 0, may hold values from -0.1 to 0.1
- drift_north: float32 [8, 8, 64, 512], P(('groups', 'tm'), None, 'tile'), parts along dimension 0, may hold values from -0.1 to 0.1
- diffusion: float32 [8, 8, 64, 512], P(('groups', 'tm'), None, 'tile'), parts along dimension 0, may hold values from 0.02 to 0.12
- obs_cell: int32 [8, 2048], P(('groups', 'tm'), 'tile'), parts along dimension 0, may hold values from 0 to 65535
- obs_count: int32 [8, 4], P(('groups', 'tm'), 'tile'), parts along dimension 0, may hold values from 256 to 512, as said below
Outputs:
- new_multiplier: float32 [8, 8, 64, 512], P(('groups', 'tm'), None, 'tile'), parts along dimension 0
- new_increment: float32 [8, 8, 64, 512], P(('groups', 'tm'), None, 'tile'), parts along dimension 0
- new_obs_dual: float32 [8, 2048], P(('groups', 'tm'), 'tile'), parts along dimension 0
The draws below stay inside these ranges and needn't reach their ends.
There are 2 independent parts, one for each index of `groups`. The reference program is written for one: setup_inputs(seed, part) draws one part's arguments, and reference() takes and returns one part's arrays. A program takes and returns all parts, laid end to end along the dimension named above; each array names one. Nothing has to cross between parts.
Inputs may be any that keep to these rules, and one draw needn't show every extreme that they name: `obs_count`: every tile and sub-window has between 256 and 512 live slots; the live ones come first; some tile and sub-window has all 512 live.
All inputs are finite; a program needn't handle non-finite values.
Results may differ from the reference program's by a relative error of at most 0.000027.
Values sent between devices are 32-bit elements; how exact they have to be, the bound alone decides.
No kernel may reach another device: no remote copies, remote signals or barrier semaphores. Data moves between devices by JAX's collectives and lax.ppermute only.
A program may use at most 64 MiB of HBM per device.

```python
import math
import jax
import jax.numpy as jnp

LEV = 8
CX = 16
NY = 512
OBS = 512
NSUB = 4
NX = 64
CELLS = 65536
N_TILE = 4


def draw_obs_count(key, part):
    key = jax.random.fold_in(key, 7)
    first_key, second_key = jax.random.split(key)
    counts = jax.random.randint(first_key, (NSUB * N_TILE,), OBS // 2, OBS + 1).astype(jnp.int32)
    chosen = jax.random.randint(second_key, (), 0, NSUB * N_TILE).astype(jnp.int32)
    counts = jnp.where(jnp.arange(NSUB * N_TILE, dtype=jnp.int32) == chosen, OBS, counts)
    return counts.reshape(NSUB, N_TILE).astype(jnp.int32)


def set_ends(entries, own_key, low, high):
    shape = entries.shape
    index_at = [jax.random.randint(jax.random.fold_in(own_key, axis), (), 0, shape[axis]) for axis in range(len(shape))]
    entries = entries.at[tuple(index_at)].set(low)
    longest = shape.index(max(shape))
    index_at[longest] = (index_at[longest] + 1) % shape[longest]
    return entries.at[tuple(index_at)].set(high)


def steps_of(stream_key, extent, cuts, low, high):
    def one(axis_at, parts):
        draws = jax.random.uniform(jax.random.fold_in(jax.random.fold_in(stream_key, 6), axis_at), (parts,), jnp.float32, low / len(cuts), high / len(cuts))
        return jnp.repeat(jnp.exp(draws), extent[axis_at] // parts).reshape((-1,) + (1,) * (len(extent) - axis_at - 1))

    loudness = one(*cuts[0])
    for cut in cuts[1:]:
        loudness = loudness * one(*cut)
    return loudness


def normal_values(rng, shape, scale, bound, shards=(), held_as=jnp.bfloat16):
    level = steps_of(rng, shape, shards, -0.22, 0.18) if shards else 1.0
    array = jax.random.normal(rng, shape, jnp.float32) * scale * level
    return jnp.minimum(jnp.maximum(array, -bound), bound).astype(held_as)


def setup_inputs(seed: int = 0, part: int = 0) -> dict:
    streams_of = jax.random.split(jax.random.key(seed), 13)
    part_splits = jax.random.split(jax.random.fold_in(streams_of[12], part), 13)
    multiplier = normal_values(part_splits[0], (NSUB, LEV, NX, NY), 1.0, 6.0, ((0, 4), (2, 4)), jnp.float32)
    increment = normal_values(part_splits[1], (NSUB, LEV, NX, NY), 1.0, 6.0, ((0, 4), (2, 4)), jnp.float32)
    obs_dual = normal_values(part_splits[2], (NSUB, N_TILE * OBS), 1.0, 6.0, ((0, 4), (1, 4)), jnp.float32)
    rhs_model = normal_values(part_splits[3], (NSUB, LEV, NX, NY), 1.0, 6.0, ((0, 4), (2, 4)), jnp.float32)
    rhs_obs = normal_values(part_splits[4], (NSUB, N_TILE * OBS), 1.0, 6.0, ((0, 4), (1, 4)), jnp.float32)
    model_err = jnp.clip(jnp.exp(math.log(2.0) - 2.3025851 * jax.random.uniform(part_splits[5], (NSUB, LEV, NX, NY), jnp.float32) ** steps_of(part_splits[5], (NSUB, LEV, NX, NY), ((0, 4), (2, 4)), -0.2, 0.2)), 0.2, 2.0)
    obs_err = jnp.clip(jnp.exp(math.log(4.0) - 2.7725887 * jax.random.uniform(part_splits[6], (NSUB, N_TILE * OBS), jnp.float32) ** steps_of(part_splits[6], (NSUB, N_TILE * OBS), ((0, 4), (1, 4)), -0.2, 0.2)), 0.25, 4.0)
    drift_east = jnp.clip(jax.random.uniform(part_splits[7], (NSUB, LEV, NX, NY), jnp.float32, -0.1, 0.1) * steps_of(part_splits[7], (NSUB, LEV, NX, NY), ((0, 4), (2, 4)), -0.4, 0.0), -0.1, 0.1)
    drift_north = jnp.clip(jax.random.uniform(part_splits[8], (NSUB, LEV, NX, NY), jnp.float32, -0.1, 0.1) * steps_of(part_splits[8], (NSUB, LEV, NX, NY), ((0, 4), (2, 4)), -0.4, 0.0), -0.1, 0.1)
    diffusion = jnp.clip(0.02 + 0.09999999776482582 * jax.random.uniform(part_splits[9], (NSUB, LEV, NX, NY), jnp.float32) ** steps_of(part_splits[9], (NSUB, LEV, NX, NY), ((0, 4), (2, 4)), -0.2, 0.2), 0.02, 0.12)
    obs_cell = set_ends(jax.random.randint(part_splits[10], (NSUB, N_TILE * OBS), 0, CELLS), jax.random.fold_in(part_splits[10], 1), 0, CELLS - 1).astype(jnp.int32)
    obs_count = draw_obs_count(jax.random.fold_in(jax.random.fold_in(streams_of[12], part), 71), part)
    return {"multiplier": multiplier, "increment": increment, "obs_dual": obs_dual, "rhs_model": rhs_model, "rhs_obs": rhs_obs, "model_err": model_err, "obs_err": obs_err, "drift_east": drift_east, "drift_north": drift_north, "diffusion": diffusion, "obs_cell": obs_cell, "obs_count": obs_count}


def pad_axis(field, axis, before, after):
    widths = [(0, 0)] * field.ndim
    widths[axis] = (before, after)
    return jnp.pad(field, widths)


def forward_step(state, drift_e, drift_n, diffuse):
    along_x = pad_axis(state, 2, 1, 1)
    along_y = pad_axis(state, 3, 1, 1)
    return ((1.0 - 4.0 * diffuse) * state + (diffuse - drift_e) * along_x[:, :, 2:, :]
            + (diffuse + drift_e) * along_x[:, :, :-2, :] + (diffuse - drift_n) * along_y[:, :, :, 2:]
            + (diffuse + drift_n) * along_y[:, :, :, :-2])


def adjoint_step(state, drift_e, drift_n, diffuse):
    plus_x = pad_axis((diffuse - drift_e) * state, 2, 1, 0)[:, :, :-1, :]
    minus_x = pad_axis((diffuse + drift_e) * state, 2, 0, 1)[:, :, 1:, :]
    plus_y = pad_axis((diffuse - drift_n) * state, 3, 1, 0)[:, :, :, :-1]
    minus_y = pad_axis((diffuse + drift_n) * state, 3, 0, 1)[:, :, :, 1:]
    return (1.0 - 4.0 * diffuse) * state + plus_x + minus_x + plus_y + minus_y


def to_tiles(field):
    blocks = field.reshape(NSUB, LEV, N_TILE, CX, NY).transpose(0, 2, 1, 3, 4)
    return blocks.reshape(NSUB, N_TILE, LEV * CX * NY)


def from_tiles(flat):
    blocks = flat.reshape(NSUB, N_TILE, LEV, CX, NY).transpose(0, 2, 1, 3, 4)
    return blocks.reshape(NSUB, LEV, NX, NY)


def reference(multiplier, increment, obs_dual, rhs_model, rhs_obs, model_err, obs_err,
              drift_east, drift_north, diffusion, obs_cell, obs_count):
    slots = obs_cell.reshape(NSUB, N_TILE, OBS).astype(jnp.int32)
    valid = (jnp.arange(OBS, dtype=jnp.int32)[None, None, :] < obs_count[:, :, None]).astype(jnp.float32)
    hx = (jnp.take_along_axis(to_tiles(increment), slots, axis=2) * valid).reshape(NSUB, N_TILE * OBS)
    owner = (jnp.arange(NSUB * N_TILE, dtype=jnp.int32).reshape(NSUB, N_TILE, 1) * (LEV * CX * NY) + slots).reshape(-1)
    weights = (valid * obs_dual.reshape(NSUB, N_TILE, OBS)).reshape(-1)
    spread = jnp.zeros((NSUB * N_TILE * LEV * CX * NY,), jnp.float32).at[owner].add(weights)
    ht = from_tiles(spread.reshape(NSUB, N_TILE, LEV * CX * NY))
    coeffs = (drift_east, drift_north, diffusion)
    moved = forward_step(forward_step(increment, *coeffs), *coeffs)
    lx = increment - jnp.concatenate([jnp.zeros_like(moved[:1]), moved[:-1]], axis=0)
    later = jnp.concatenate([multiplier[1:], jnp.zeros_like(multiplier[:1])], axis=0)
    lt = multiplier - adjoint_step(adjoint_step(later, *coeffs), *coeffs)
    valid_flat = valid.reshape(NSUB, N_TILE * OBS)
    res_model = rhs_model - (model_err * multiplier + lx)
    res_obs = valid_flat * (rhs_obs - (obs_err * obs_dual + hx))
    res_incr = -(lt + ht)
    dir_model = jnp.cumsum(res_model, axis=0)
    dir_incr = jnp.flip(jnp.cumsum(jnp.flip(res_incr, 0), axis=0), 0)
    dir_obs = res_obs / obs_err
    numer = jnp.sum(res_model * dir_model) + jnp.sum(res_incr * dir_incr) + jnp.sum(res_obs * dir_obs)
    denom = jnp.sum(dir_model * dir_model) + jnp.sum(dir_incr * dir_incr) + jnp.sum(dir_obs * dir_obs)
    step_size = numer / denom
    return (multiplier + step_size * dir_model, increment + step_size * dir_incr,
            obs_dual + step_size * dir_obs)
```

```python
import jax
import jax.numpy as jnp
from jax import lax
from jax.experimental import pallas as pl
from jax.experimental.pallas import tpu as pltpu
from jax.sharding import PartitionSpec as P

F32 = jnp.float32
VMEM = pltpu.VMEM
GRANT = 24 * 1024 * 1024


def kernel_call(body, name, inputs, outputs):
    arrays, in_specs = [], []
    for array, home in inputs:
        if home == "scalar":
            in_specs.append(pl.BlockSpec(memory_space=pltpu.SMEM))
        else:
            in_specs.append(pl.BlockSpec(memory_space=VMEM))
            if home == "near":
                array = pltpu.with_memory_space_constraint(array, VMEM)
        arrays.append(array)
    out_shape = [
        VMEM(shape, F32) if home == "near" else jax.ShapeDtypeStruct(shape, F32)
        for shape, home in outputs
    ]
    return pl.pallas_call(
        body,
        name=name,
        out_shape=out_shape,
        in_specs=in_specs,
        out_specs=[pl.BlockSpec(memory_space=VMEM)] * len(outputs),
        compiler_params=pltpu.CompilerParams(vmem_limit_bytes=GRANT),
    )(*arrays)


def iotas(shape):
    return (
        lax.broadcasted_iota(jnp.int32, shape, 0),
        lax.broadcasted_iota(jnp.int32, shape, 1),
    )


def up(field, axis):
    return pltpu.roll(field, field.shape[axis] - 1, axis)


def down(field, axis):
    return pltpu.roll(field, 1, axis)


def taps(a, b, c):
    i, y = iotas(a.shape)
    rows, cols = a.shape
    return (
        1.0 - 4.0 * c,
        jnp.where(i < rows - 1, c - a, 0.0),
        jnp.where(i > 0, c + a, 0.0),
        jnp.where(y < cols - 1, c - b, 0.0),
        jnp.where(y > 0, c + b, 0.0),
    )


def forward(state, coeffs):
    mid, east, west, north, south = coeffs
    return (
        mid * state
        + east * up(state, 0)
        + west * down(state, 0)
        + north * up(state, 1)
        + south * down(state, 1)
    )


def adjoint(state, coeffs):
    mid, east, west, north, south = coeffs
    return (
        mid * state
        + down(east * state, 0)
        + up(west * state, 0)
        + down(north * state, 1)
        + up(south * state, 1)
    )


EDGE = ("mid_low", "mid_high", "north_low", "north_high", "south_low", "south_high")
EDGE += ("west_low", "west_next", "east_high", "east_next", "east_low", "west_high")


def forward_body(s_ref, a_ref, b_ref, c_ref, moved_ref, high_ref, low_ref, edge_ref):
    levels, rows, _ = s_ref.shape
    last = rows - 1
    for lev in range(levels):
        s, a, b, c = s_ref[lev], a_ref[lev], b_ref[lev], c_ref[lev]
        coeffs = taps(a, b, c)
        once = forward(s, coeffs)
        moved_ref[lev] = forward(once, coeffs)
        mid, east, west, north, south = coeffs
        at = pl.ds(lev, 1)
        open_east = c[last : last + 1] - a[last : last + 1]
        open_west = c[0:1] + a[0:1]
        high_ref[0, at] = s[last : last + 1]
        high_ref[1, at] = once[last : last + 1]
        high_ref[2, at] = open_east
        low_ref[0, at] = s[0:1]
        low_ref[1, at] = once[0:1]
        low_ref[2, at] = open_west
        rows_of = {
            "mid_low": mid[0:1],
            "mid_high": mid[last : last + 1],
            "north_low": north[0:1],
            "north_high": north[last : last + 1],
            "south_low": south[0:1],
            "south_high": south[last : last + 1],
            "west_low": open_west,
            "west_next": west[1:2],
            "east_high": open_east,
            "east_next": east[last - 1 : last],
            "east_low": east[0:1],
            "west_high": west[last : last + 1],
        }
        for n, key in enumerate(EDGE):
            edge_ref[n, at] = rows_of[key]


def adjoint_body(
    a_ref, b_ref, c_ref, inner_ref, outer_ref, high_ref, low_ref, back_ref, first_ref, second_ref
):
    levels, rows, _ = a_ref.shape
    last = rows - 1
    position, peers = lax.axis_index("tm"), lax.axis_size("tm")
    odd = lax.rem(lax.axis_index("tile"), 2)
    for n in range(3):
        first_ref[n] = jnp.where(odd == 0, high_ref[n], low_ref[n])
        second_ref[n] = jnp.where(odd == 0, low_ref[n], high_ref[n])
    for lev in range(levels):
        a, b, c = a_ref[lev], b_ref[lev], c_ref[lev]
        later = jnp.where(lax.rem(position, 2) == 0, inner_ref[lev], outer_ref[lev])
        later = jnp.where(position < peers - 1, later, 0.0)
        coeffs = taps(a, b, c)
        once = adjoint(later, coeffs)
        back_ref[lev] = adjoint(once, coeffs)
        at = pl.ds(lev, 1)
        east = c[last : last + 1] - a[last : last + 1]
        west = c[0:1] + a[0:1]
        highs = (east * later[last : last + 1], east * once[last : last + 1])
        lows = (west * later[0:1], west * once[0:1])
        for n in range(2):
            first_ref[3 + n, at] = jnp.where(odd == 0, highs[n], lows[n])
            second_ref[3 + n, at] = jnp.where(odd == 0, lows[n], highs[n])


def edges_body(
    first_ref, second_ref, got_first_ref, got_second_ref, edge_ref, moved_ref, back_ref
):
    tile, tiles = lax.axis_index("tile"), lax.axis_size("tile")
    odd = lax.rem(tile, 2)
    has_low, has_high = tile > 0, tile < tiles - 1

    def sides(n):
        below = jnp.where(odd == 0, got_second_ref[n], got_first_ref[n])
        above = jnp.where(odd == 0, got_first_ref[n], got_second_ref[n])
        return jnp.where(has_low, below, 0.0), jnp.where(has_high, above, 0.0)

    def own(n):
        one, two = first_ref[n], second_ref[n]
        return jnp.where(odd == 0, two, one), jnp.where(odd == 0, one, two)

    k = {key: edge_ref[n] for n, key in enumerate(EDGE)}
    (s_low, s_high), (w_low, w_high), (east_below, west_above) = sides(0), sides(1), sides(2)
    (p_low, p_high), (q_low, q_high) = sides(3), sides(4)
    (my_s_low, my_s_high), (my_p_low, my_p_high) = own(0), own(3)

    def along(x, mid, north, south):
        return mid * x + north * up(x, 1) + south * down(x, 1)

    def across(x, mid, north, south):
        return mid * x + down(north * x, 1) + up(south * x, 1)

    new_low = k["west_low"] * s_low
    new_high = k["east_high"] * s_high
    low = (k["mid_low"], k["north_low"], k["south_low"])
    high = (k["mid_high"], k["north_high"], k["south_high"])
    moved_ref[0] = along(new_low, *low) + k["west_low"] * (w_low + east_below * my_s_low)
    moved_ref[1] = k["west_next"] * new_low
    moved_ref[2] = k["east_next"] * new_high
    moved_ref[3] = along(new_high, *high) + k["east_high"] * (w_high + west_above * my_s_high)
    back_ref[0] = across(p_low, *low) + (q_low + east_below * my_p_low)
    back_ref[1] = k["east_low"] * p_low
    back_ref[2] = k["west_high"] * p_high
    back_ref[3] = across(p_high, *high) + (q_high + west_above * my_p_high)


def thirds(x):
    one = x.astype(jnp.bfloat16)
    rest = x - one.astype(F32)
    two = rest.astype(jnp.bfloat16)
    return one, two, (rest - two.astype(F32)).astype(jnp.bfloat16)


def observe_body(
    incr_ref, mult_ref, rhs_ref, err_ref, cell_ref, dual_ref, want_ref, var_ref, count_ref,
    local_ref, held_ref, dir_ref, sums_ref,
):
    levels, rows, cols = incr_ref.shape
    slots = cell_ref.shape[1]
    lines = levels * rows
    cell = cell_ref[...]
    _, slot = iotas(cell.shape)
    valid = jnp.where(slot < count_ref[0, 0], 1.0, 0.0)
    dual = dual_ref[...]
    line, col = cell // cols, lax.rem(cell, cols)
    at_line = iotas((lines, slots))[0] == line
    at_col = jnp.where(iotas((cols, slots))[0] == col, 1.0, 0.0).astype(jnp.bfloat16)
    weights = thirds(jnp.where(at_line, valid * dual, 0.0))
    spread = lax.dot_general(
        jnp.concatenate(weights, 0), at_col, (((1,), (1,)), ((), ())), preferred_element_type=F32
    )
    fields = thirds(incr_ref[...].reshape(lines, cols))
    picked = jnp.dot(jnp.concatenate(fields, 0), at_col, preferred_element_type=F32)
    picked = picked[:lines] + picked[lines : 2 * lines] + picked[2 * lines :]
    hx = jnp.sum(jnp.where(at_line, picked, 0.0), axis=0, keepdims=True) * valid
    var = var_ref[...]
    res = valid * (want_ref[...] - (var * dual + hx))
    direction = res / var
    dir_ref[...] = direction
    sums_ref[0] = res * direction
    sums_ref[1] = direction * direction
    ht = spread[:lines] + spread[lines : 2 * lines] + spread[2 * lines :]
    mult = mult_ref[...]
    held_ref[...] = mult + ht.reshape(levels, rows, cols)
    local_ref[...] = rhs_ref[...] - (err_ref[...] * mult + incr_ref[...])


def share_body(local_ref, moved_ref, held_ref, back_ref, out_ref):
    half = out_ref.shape[1]
    away = pl.ds((1 - lax.rem(lax.axis_index("tm"), 2)) * half, half)
    out_ref[0] = local_ref[away]
    out_ref[1] = moved_ref[away]
    out_ref[2] = held_ref[away] - back_ref[away]


def corrected(field, fix):
    rows = field.shape[0]
    i, _ = iotas(field.shape)
    for n, row in enumerate((0, 1, rows - 2, rows - 1)):
        field = field + jnp.where(i == row, fix[n], 0.0)
    return field


def pairs_body(
    local_ref, moved_ref, held_ref, back_ref, fix_ref, got_ref, got_fix_ref, terms_ref, send_ref
):
    half = got_ref.shape[1]
    position = lax.axis_index("tm")
    side = lax.rem(position, 2)
    low_pair = position < 2

    def pick(i, lev):
        fix_m = [fix_ref[0, n, pl.ds(lev, 1)] for n in range(4)]
        fix_b = [fix_ref[1, n, pl.ds(lev, 1)] for n in range(4)]
        got_m = [got_fix_ref[0, n, pl.ds(lev, 1)] for n in range(4)]
        got_b = [got_fix_ref[1, n, pl.ds(lev, 1)] for n in range(4)]
        mine = (
            local_ref[lev],
            corrected(moved_ref[lev], fix_m),
            corrected(held_ref[lev] - back_ref[lev], [-x for x in fix_b]),
        )
        other = (
            got_ref[0, i],
            corrected(got_ref[1, i], got_m),
            corrected(got_ref[2, i], [-x for x in got_b]),
        )
        even = [jnp.where(side == 0, x, y) for x, y in zip(mine, other)]
        odd = [jnp.where(side == 0, y, x) for x, y in zip(mine, other)]
        return even, odd

    for i in range(half):
        (l0, m0, t0), (l1, m1, t1) = pick(i, side * half + i)
        model1 = l1 + m0
        terms_ref[0, i] = jnp.where(low_pair, l0, t1)
        terms_ref[1, i] = jnp.where(low_pair, model1, t0)
        terms_ref[2, i] = jnp.where(low_pair, t1, l0)
        terms_ref[3, i] = jnp.where(low_pair, t0, model1)
        send_ref[0, i] = jnp.where(low_pair, l0 + model1, t1 + t0)
        send_ref[1, i] = jnp.where(low_pair, m1, 0.0)


def dots_body(terms_ref, got_ref, obs_ref, keep_ref, send_ref, sums_ref):
    half, rows, cols = terms_ref.shape[1:]
    position = lax.axis_index("tm")
    low_pair = position < 2
    inner = (position == 1) | (position == 2)
    numer, denom = jnp.zeros((8, 128), F32), jnp.zeros((8, 128), F32)

    def folded(x):
        total = None
        for r in range(0, rows, 8):
            for col in range(0, cols, 128):
                part = x[r : r + 8, col : col + 128]
                total = part if total is None else total + part
        return total

    for i in range(half):
        y0, y1, z0, z1 = (terms_ref[n, i] for n in range(4))
        z0 = z0 + got_ref[1, i]
        one = y0 + y1
        two = got_ref[0, i] + z0
        three = two + z1
        numer = numer + folded(y0 * y0 + y1 * one + z0 * two + z1 * three)
        denom = denom + folded(y0 * y0 + one * one + two * two + three * three)
        here = (jnp.where(inner, one, y0), jnp.where(inner, two, three))
        there = (jnp.where(inner, y0, one), jnp.where(inner, three, two))
        for ref, (own_side, far_side) in ((keep_ref, here), (send_ref, there)):
            ref[0, i] = jnp.where(low_pair, own_side, far_side)
            ref[1, i] = jnp.where(low_pair, far_side, own_side)
    slots = obs_ref.shape[2]
    for n, total in enumerate((numer, denom)):
        obs = obs_ref[n]
        row = obs[:, 0:128]
        for col in range(128, slots, 128):
            row = row + obs[:, col : col + 128]
        sums_ref[n] = total
        sums_ref[n, 0:1] = total[0:1] + row


def update_body(
    mult_ref, incr_ref, dual_ref, dir_ref, keep_ref, got_ref, sums_ref, new_m_ref, new_i_ref, new_o_ref
):
    half = keep_ref.shape[1]
    side = lax.rem(lax.axis_index("tm"), 2)
    total = [
        jnp.sum(jnp.sum(sums_ref[n], axis=0, keepdims=True), axis=1, keepdims=True)
        for n in range(2)
    ]
    step = total[0] / total[1]
    for i in range(half):
        for ref, place in ((keep_ref, side), (got_ref, 1 - side)):
            lev = place * half + i
            new_m_ref[lev] = mult_ref[lev] + step * ref[0, i]
            new_i_ref[lev] = incr_ref[lev] - step * ref[1, i]
    new_o_ref[...] = dual_ref[...] + step * dir_ref[...]


def flat_pairs(tiles, peers, partner):
    pairs = []
    for t in range(tiles):
        for k in range(peers):
            to_t, to_k = partner(t, k)
            pairs.append((t * peers + k, to_t * peers + to_k))
    return pairs


def swap(value, axis, distance):
    return lax.ppermute(value, axis, [(i, i ^ distance) for i in range(lax.axis_size(axis))])


def shifted(value, steps):
    count = lax.axis_size("tm")
    pairs = [(i, i + steps) for i in range(count) if 0 <= i + steps < count]
    return lax.ppermute(value, "tm", pairs)


def scanned(value, direction):
    reach = 1
    while reach < lax.axis_size("tm"):
        value = value + shifted(value, direction * reach)
        reach *= 2
    return value


def shards(
    multiplier, increment, obs_dual, rhs_model, rhs_obs, model_err, obs_err,
    drift_east, drift_north, diffusion, obs_cell, obs_count,
):
    tiles, peers = lax.axis_size("tile"), lax.axis_size("tm")
    mult, incr = multiplier[0], increment[0]
    coeffs = [drift_east[0], drift_north[0], diffusion[0]]
    levels, rows, cols = mult.shape
    field, half = mult.shape, levels // 2
    both = ("tile", "tm")

    def across(t, k):
        if 0 < k < peers - 1:
            return t, (k - 1 if k % 2 == 0 else k + 1)
        return t ^ 1, k

    def second_side(t, k):
        if 0 < t < tiles - 1:
            return (t - 1 if t % 2 == 0 else t + 1), k
        return t, k ^ 1

    outer = lax.ppermute(mult, both, flat_pairs(tiles, peers, across))
    inner = swap(mult, "tm", 1)
    moved, high, low, edge = kernel_call(
        forward_body,
        "forward",
        [(x, "far") for x in (incr, *coeffs)],
        [(field, "near")] + [((3, levels, cols), "near")] * 2 + [((len(EDGE), levels, cols), "near")],
    )
    back, first, second = kernel_call(
        adjoint_body,
        "adjoint",
        [(x, "far") for x in coeffs] + [(x, "near") for x in (inner, outer, high, low)],
        [(field, "near")] + [((5, levels, cols), "near")] * 2,
    )
    got_first = swap(first, "tile", 1)
    got_second = lax.ppermute(second, both, flat_pairs(tiles, peers, second_side))
    local, held, dir_obs, obs_sums = kernel_call(
        observe_body,
        "observe",
        [(x, "far") for x in (incr, mult, rhs_model[0], model_err[0])]
        + [(x, "far") for x in (obs_cell, obs_dual, rhs_obs, obs_err)]
        + [(obs_count, "scalar")],
        [(field, "near")] * 2 + [(obs_dual.shape, "near"), ((2, *obs_dual.shape), "near")],
    )
    near = lambda *arrays: [(x, "near") for x in arrays]
    fix_shape = ((4, levels, cols), "near")
    fix_moved, fix_back = kernel_call(
        edges_body, "edges", near(first, second, got_first, got_second, edge), [fix_shape] * 2
    )
    fix = jnp.stack([fix_moved, fix_back])
    if peers != 4:
        return scan_path(
            multiplier, increment, obs_dual, local, moved, held, back, fix, dir_obs, obs_sums
        )
    share = kernel_call(
        share_body, "share", near(local, moved, held, back), [((3, half, rows, cols), "near")]
    )[0]
    got_share = swap(share, "tm", 1)
    got_fix = swap(fix, "tm", 1)
    part = (half, rows, cols)
    terms, send = kernel_call(
        pairs_body,
        "pairs",
        near(local, moved, held, back, fix, got_share, got_fix),
        [((4, *part), "near"), ((2, *part), "near")],
    )
    got = swap(send, "tm", 2)
    keep, give, sums = kernel_call(
        dots_body,
        "dots",
        near(terms, got, obs_sums),
        [((2, *part), "near"), ((2, *part), "near"), ((2, 8, 128), "near")],
    )
    sums = sums + swap(sums, "tm", 1)
    got_dirs = swap(give, "tm", 1)
    sums = sums + swap(sums, "tm", 2)
    sums = reduced(sums, "tile")
    new_m, new_i, new_o = kernel_call(
        update_body,
        "update",
        [(mult, "near"), (incr, "near"), (obs_dual, "far")] + near(dir_obs, keep, got_dirs, sums),
        [(field, "far"), (field, "far"), (obs_dual.shape, "far")],
    )
    return new_m[None], new_i[None], new_o


def reduced(value, axis):
    distance = 1
    while distance < lax.axis_size(axis):
        value = value + swap(value, axis, distance)
        distance *= 2
    return value


def scan_path(multiplier, increment, obs_dual, local, moved, held, back, fix, dir_obs, obs_sums):
    rows = local.shape[1]
    fix = jnp.moveaxis(fix, 1, 2)
    at = jnp.array([0, 1, rows - 2, rows - 1])
    moved = moved.at[:, at].add(fix[0])
    res_incr = -(held - back.at[:, at].add(fix[1]))
    res_model = local + shifted(moved, 1)
    dir_model, dir_incr = scanned(res_model, 1), scanned(res_incr, -1)
    numer = jnp.sum(res_model * dir_model) + jnp.sum(res_incr * dir_incr) + jnp.sum(obs_sums[0])
    denom = jnp.sum(dir_model**2) + jnp.sum(dir_incr**2) + jnp.sum(obs_sums[1])
    sums = reduced(reduced(jnp.stack([numer, denom]), "tm"), "tile")
    step = sums[0] / sums[1]
    return (
        multiplier + step * dir_model[None],
        increment + step * dir_incr[None],
        obs_dual + step * dir_obs,
    )


def solution(mesh):
    grid = P(("groups", "tm"), None, "tile", None)
    line = P(("groups", "tm"), "tile")
    return jax.shard_map(
        shards,
        mesh=mesh,
        in_specs=(grid, grid, line, grid, line, grid, line, grid, grid, grid, line, line),
        out_specs=(grid, grid, line),
        check_vma=False,
    )
```

```python
import jax
import jax.numpy as jnp
from jax import lax
from jax.experimental import pallas as pl
from jax.experimental.pallas import tpu as pltpu
from jax.sharding import PartitionSpec as P

F32 = jnp.float32
VMEM = pltpu.VMEM
GRANT = 24 * 1024 * 1024


def kernel_call(body, name, inputs, outputs, scratch=()):
    arrays, in_specs = [], []
    for array, home in inputs:
        if home == "far":
            in_specs.append(pl.BlockSpec(memory_space=pltpu.HBM))
            array = pltpu.with_memory_space_constraint(array, pltpu.HBM)
        else:
            in_specs.append(pl.BlockSpec(memory_space=VMEM))
            array = pltpu.with_memory_space_constraint(array, VMEM)
        arrays.append(array)
    out_shape = []
    for shape, home, *dtype in outputs:
        dtype = dtype[0] if dtype else F32
        out_shape.append(
            VMEM(shape, dtype) if home == "near" else jax.ShapeDtypeStruct(shape, dtype)
        )
    return pl.pallas_call(
        body,
        name=name,
        out_shape=out_shape,
        in_specs=in_specs,
        out_specs=[pl.BlockSpec(memory_space=VMEM)] * len(outputs),
        scratch_shapes=list(scratch),
        cost_estimate=pl.CostEstimate(flops=1, bytes_accessed=1, transcendentals=0),
        compiler_params=pltpu.CompilerParams(vmem_limit_bytes=GRANT),
    )(*arrays)


def lanes(row):
    total = row[:, 0:128]
    for col in range(128, row.shape[1], 128):
        total = total + row[:, col : col + 128]
    return total


def iotas(shape):
    return (
        lax.broadcasted_iota(jnp.int32, shape, 0),
        lax.broadcasted_iota(jnp.int32, shape, 1),
    )


def up(field, axis):
    return pltpu.roll(field, field.shape[axis] - 1, axis)


def down(field, axis):
    return pltpu.roll(field, 1, axis)


def taps(a, b, c):
    i, y = iotas(a.shape)
    rows, cols = a.shape
    return (
        1.0 - 4.0 * c,
        jnp.where(i < rows - 1, c - a, 0.0),
        jnp.where(i > 0, c + a, 0.0),
        jnp.where(y < cols - 1, c - b, 0.0),
        jnp.where(y > 0, c + b, 0.0),
    )


def forward(state, coeffs):
    mid, east, west, north, south = coeffs
    return (
        mid * state
        + east * up(state, 0)
        + west * down(state, 0)
        + north * up(state, 1)
        + south * down(state, 1)
    )


def adjoint(state, coeffs):
    mid, east, west, north, south = coeffs
    return (
        mid * state
        + down(east * state, 0)
        + up(west * state, 0)
        + down(north * state, 1)
        + up(south * state, 1)
    )


EDGE = ("mid_low", "mid_high", "north_low", "north_high", "south_low", "south_high")
EDGE += ("west_low", "west_next", "east_high", "east_next", "east_low", "west_high")


def begin_body(count, *refs):
    sources, targets = refs[:count], refs[count : 2 * count]
    moved_ref, high_ref, low_ref, edge_ref, sems = refs[2 * count :]
    copies = [
        pltpu.make_async_copy(source, target, sems.at[n])
        for n, (source, target) in enumerate(zip(sources, targets))
    ]
    for copy in copies:
        copy.start()
    for copy in copies[:4]:
        copy.wait()
    s_ref, a_ref, b_ref, c_ref = targets[:4]
    levels, rows, _ = s_ref.shape
    last = rows - 1
    for lev in range(levels):
        s, a, b, c = s_ref[lev], a_ref[lev], b_ref[lev], c_ref[lev]
        coeffs = taps(a, b, c)
        once = forward(s, coeffs)
        moved_ref[lev] = forward(once, coeffs)
        mid, east, west, north, south = coeffs
        at = pl.ds(lev, 1)
        open_east = c[last : last + 1] - a[last : last + 1]
        open_west = c[0:1] + a[0:1]
        high_ref[0, at] = s[last : last + 1]
        high_ref[1, at] = once[last : last + 1]
        high_ref[2, at] = open_east
        low_ref[0, at] = s[0:1]
        low_ref[1, at] = once[0:1]
        low_ref[2, at] = open_west
        rows_of = {
            "mid_low": mid[0:1],
            "mid_high": mid[last : last + 1],
            "north_low": north[0:1],
            "north_high": north[last : last + 1],
            "south_low": south[0:1],
            "south_high": south[last : last + 1],
            "west_low": open_west,
            "west_next": west[1:2],
            "east_high": open_east,
            "east_next": east[last - 1 : last],
            "east_low": east[0:1],
            "west_high": west[last : last + 1],
        }
        for n, key in enumerate(EDGE):
            edge_ref[n, at] = rows_of[key]
    for copy in copies[4:]:
        copy.wait()


def adjoint_body(a_ref, b_ref, c_ref, later_ref, back_ref):
    for lev in range(a_ref.shape[0]):
        coeffs = taps(a_ref[lev], b_ref[lev], c_ref[lev])
        back_ref[lev] = adjoint(adjoint(later_ref[lev], coeffs), coeffs)


def outer_products(k, later):
    def once(side, at, beside):
        mid, north, south = k["mid_" + side], k["north_" + side], k["south_" + side]
        return mid * at + beside + down(north * at, 1) + up(south * at, 1)

    west, east = k["west_low"], k["east_high"]
    return (
        (west * later[0], west * once("low", later[0], k["west_next"] * later[1])),
        (east * later[3], east * once("high", later[3], k["east_next"] * later[2])),
    )


def outer_rows(ref, levels, wanted):
    rows = ref.shape[1]
    picked = []
    for row in (0, 1, rows - 2, rows - 1):
        value = jnp.concatenate([ref[lev, row : row + 1] for lev in range(levels)], 0)
        picked.append(jnp.where(wanted, value, 0.0))
    return picked


def rims_body(wanted, edge_ref, later_ref, high_ref, low_ref, first_ref, second_ref):
    odd = lax.rem(lax.axis_index("tile"), 2)
    k = {key: edge_ref[n] for n, key in enumerate(EDGE)}
    low, high = outer_products(k, outer_rows(later_ref, edge_ref.shape[1], wanted()))
    lows = [low_ref[n] for n in range(3)] + list(low)
    highs = [high_ref[n] for n in range(3)] + list(high)
    for n in range(5):
        first_ref[n] = jnp.where(odd == 0, highs[n], lows[n])
        second_ref[n] = jnp.where(odd == 0, lows[n], highs[n])


def late_rims_body(edge_ref, later_ref, first_ref, second_ref):
    odd = lax.rem(lax.axis_index("tile"), 2)
    k = {key: edge_ref[n] for n, key in enumerate(EDGE)}
    low, high = outer_products(k, outer_rows(later_ref, edge_ref.shape[1], lax.axis_index("tm") == 1))
    for n in range(2):
        first_ref[n] = jnp.where(odd == 0, high[n], low[n])
        second_ref[n] = jnp.where(odd == 0, low[n], high[n])


def sides(first, second):
    tile, tiles = lax.axis_index("tile"), lax.axis_size("tile")
    odd = lax.rem(tile, 2)
    below, above = jnp.where(odd == 0, second, first), jnp.where(odd == 0, first, second)
    return jnp.where(tile > 0, below, 0.0), jnp.where(tile < tiles - 1, above, 0.0)


def own_sides(first, second):
    odd = lax.rem(lax.axis_index("tile"), 2)
    return jnp.where(odd == 0, second, first), jnp.where(odd == 0, first, second)


def back_fix(k, product, stepped, own_product, toward):
    def across(x, side):
        mid, north, south = k["mid_" + side], k["north_" + side], k["south_" + side]
        return mid * x + down(north * x, 1) + up(south * x, 1)

    return (
        across(product[0], "low") + (stepped[0] + toward[0] * own_product[0]),
        k["east_low"] * product[0],
        k["west_high"] * product[1],
        across(product[1], "high") + (stepped[1] + toward[1] * own_product[1]),
    )


def edges_body(first_ref, second_ref, got_first_ref, got_second_ref, edge_ref, fix_ref):
    k = {key: edge_ref[n] for n, key in enumerate(EDGE)}
    state, stepped, toward, product, product_stepped = (
        sides(got_first_ref[n], got_second_ref[n]) for n in range(5)
    )
    own_state = own_sides(first_ref[0], second_ref[0])
    own_product = own_sides(first_ref[3], second_ref[3])

    def along(x, side):
        mid, north, south = k["mid_" + side], k["north_" + side], k["south_" + side]
        return mid * x + north * up(x, 1) + south * down(x, 1)

    new_low, new_high = k["west_low"] * state[0], k["east_high"] * state[1]
    fix_ref[0] = along(new_low, "low") + k["west_low"] * (stepped[0] + toward[0] * own_state[0])
    fix_ref[1] = k["west_next"] * new_low
    fix_ref[2] = k["east_next"] * new_high
    fix_ref[3] = along(new_high, "high") + k["east_high"] * (stepped[1] + toward[1] * own_state[1])
    for n, row in enumerate(back_fix(k, product, product_stepped, own_product, toward)):
        fix_ref[4 + n] = row


def late_edges_body(
    first_ref, second_ref, got_first_ref, got_second_ref, past_first_ref, past_second_ref,
    edge_ref, fix_ref,
):
    k = {key: edge_ref[n] for n, key in enumerate(EDGE)}
    product, stepped = (sides(got_first_ref[n], got_second_ref[n]) for n in range(2))
    toward = sides(past_first_ref[2], past_second_ref[2])
    own_product = own_sides(first_ref[0], second_ref[0])
    for n, row in enumerate(back_fix(k, product, stepped, own_product, toward)):
        fix_ref[n] = row


def thirds(x):
    one = x.astype(jnp.bfloat16)
    rest = x - one.astype(F32)
    two = rest.astype(jnp.bfloat16)
    return one, two, (rest - two.astype(F32)).astype(jnp.bfloat16)


def observe_body(
    incr_ref, mult_ref, rhs_ref, err_ref, cell_ref, dual_ref, want_ref, var_ref, valid_ref,
    local_ref, held_ref, dir_ref, sums_ref,
):
    levels, rows, cols = incr_ref.shape
    slots = cell_ref.shape[1]
    lines = levels * rows
    cell = cell_ref[...]
    valid = valid_ref[...]
    dual = dual_ref[...]
    line, col = cell // cols, lax.rem(cell, cols)
    at_line = iotas((lines, slots))[0] == line
    at_col = jnp.where(iotas((cols, slots))[0] == col, 1.0, 0.0).astype(jnp.bfloat16)
    weights = thirds(jnp.where(at_line, valid * dual, 0.0))
    spread = lax.dot_general(
        jnp.concatenate(weights, 0), at_col, (((1,), (1,)), ((), ())), preferred_element_type=F32
    )
    fields = thirds(incr_ref[...].reshape(lines, cols))
    picked = jnp.dot(jnp.concatenate(fields, 0), at_col, preferred_element_type=F32)
    picked = picked[:lines] + picked[lines : 2 * lines] + picked[2 * lines :]
    hx = jnp.sum(jnp.where(at_line, picked, 0.0), axis=0, keepdims=True) * valid
    var = var_ref[...]
    res = valid * (want_ref[...] - (var * dual + hx))
    direction = res / var
    dir_ref[...] = direction
    sums_ref[0] = res * direction
    sums_ref[1] = direction * direction
    ht = spread[:lines] + spread[lines : 2 * lines] + spread[2 * lines :]
    mult = mult_ref[...]
    held_ref[...] = mult + ht.reshape(levels, rows, cols)
    local_ref[...] = rhs_ref[...] - (err_ref[...] * mult + incr_ref[...])


def corrected(field, fix):
    rows = field.shape[0]
    i, _ = iotas(field.shape)
    for n, row in enumerate((0, 1, rows - 2, rows - 1)):
        field = field + jnp.where(i == row, fix[n], 0.0)
    return field


def fixes(ref, start, lev):
    return [ref[start + n, pl.ds(lev, 1)] for n in range(4)]


def minus(rows):
    return [-x for x in rows]


def share_body(
    a_ref, b_ref, c_ref, inner_ref, local_ref, moved_ref, held_ref, fix_ref, own_ref, urgent_ref
):
    position = lax.axis_index("tm")
    first, low_pair = lax.rem(position, 2) == 0, position < 2
    for lev in range(a_ref.shape[0]):
        coeffs = taps(a_ref[lev], b_ref[lev], c_ref[lev])
        back = adjoint(adjoint(inner_ref[lev], coeffs), coeffs)
        back = corrected(jnp.where(first, back, 0.0), fixes(fix_ref, 4, lev))
        moved = corrected(moved_ref[lev], fixes(fix_ref, 0, lev))
        local = local_ref[lev]
        residual = held_ref[lev] - back
        own_ref[0, lev] = local
        own_ref[1, lev] = moved
        own_ref[2, lev] = residual
        urgent_ref[lev] = jnp.where(low_pair, local + moved, residual)


def sends_body(own_ref, got_ref, fix_ref, send_ref):
    _, levels, rows, _ = own_ref.shape
    low_pair = lax.axis_index("tm") < 2
    for lev in range(levels):
        mine = jnp.where(low_pair, own_ref[0, lev], own_ref[2, lev])
        send_ref[lev * rows : (lev + 1) * rows] = mine + got_ref[lev]
    for n in range(4):
        start = levels * rows + n * levels
        send_ref[start : start + levels] = fix_ref[n]


def rest_body(own_ref, obs_ref, out_ref):
    levels = own_ref.shape[1]
    low_pair = lax.axis_index("tm") < 2
    for lev in range(levels):
        out_ref[lev] = own_ref[0, lev]
        out_ref[levels + lev] = jnp.where(low_pair, own_ref[2, lev], own_ref[1, lev])
    out_ref[2 * levels] = jnp.zeros(out_ref.shape[1:], F32)
    for n in range(2):
        out_ref[2 * levels, n : n + 1, 0:128] = lanes(obs_ref[n])


def terms_body(
    a_ref, b_ref, c_ref, cross_ref, own_ref, got_ref, rest_ref, fix_ref, terms_ref, known_ref
):
    low_pair = lax.axis_index("tm") < 2
    levels = own_ref.shape[1]
    for lev in range(levels):
        coeffs = taps(a_ref[lev], b_ref[lev], c_ref[lev])
        cross, got = cross_ref[lev], got_ref[lev]
        local, residual = own_ref[0, lev], own_ref[2, lev]
        back = corrected(adjoint(adjoint(cross, coeffs), coeffs), fixes(fix_ref, 0, lev))
        rest0, rest1 = rest_ref[lev], rest_ref[levels + lev]
        terms_ref[0, lev] = jnp.where(low_pair, rest0, residual)
        terms_ref[1, lev] = jnp.where(low_pair, local, residual) + got
        terms_ref[2, lev] = jnp.where(low_pair, residual - back, rest0 + cross)
        terms_ref[3, lev] = jnp.where(low_pair, rest1, local + rest1)
        known_ref[lev] = jnp.where(low_pair, local, residual + got)


def dots_body(terms_ref, got_ref, rest_ref, obs_ref, keep_ref, give_ref, sums_ref):
    _, levels, rows, cols = terms_ref.shape
    low_pair = lax.axis_index("tm") < 2
    numer, denom = jnp.zeros((8, 128), F32), jnp.zeros((8, 128), F32)

    def folded(x):
        total = None
        for r in range(0, rows, 8):
            part = lanes(x[r : r + 8])
            total = part if total is None else total + part
        return total

    for lev in range(levels):
        y0, one, z0, z1 = (terms_ref[n, lev] for n in range(4))
        late = []
        for n in range(4):
            at = levels * rows + n * levels + lev
            late.append(jnp.where(low_pair, 0.0, got_ref[at : at + 1]))
        z0 = corrected(z0, late)
        two = got_ref[lev * rows : (lev + 1) * rows] + z0
        three = two + z1
        numer = numer + folded(y0 * y0 + (one - y0) * one + z0 * two + z1 * three)
        denom = denom + folded(y0 * y0 + one * one + two * two + three * three)
        keep_ref[0, lev] = jnp.where(low_pair, one, three)
        keep_ref[1, lev] = jnp.where(low_pair, two, y0)
        give_ref[lev] = jnp.where(low_pair, three, two)
    for n, total in enumerate((numer, denom)):
        sums_ref[n] = total
        obs = lanes(obs_ref[n]) + rest_ref[2 * levels, n : n + 1, 0:128]
        sums_ref[n, 0:1] = total[0:1] + obs


def update_body(
    mult_ref, incr_ref, dual_ref, dir_ref, keep_ref, known_ref, got_ref, sums_ref,
    new_m_ref, new_i_ref, new_o_ref,
):
    position = lax.axis_index("tm")
    leads, low_pair = lax.rem(position, 2) == 1, position < 2
    total = [
        jnp.sum(jnp.sum(sums_ref[n], axis=0, keepdims=True), axis=1, keepdims=True)
        for n in range(2)
    ]
    step = total[0] / total[1]
    for lev in range(mult_ref.shape[0]):
        known, got = known_ref[lev], got_ref[lev]
        model = jnp.where(leads, keep_ref[0, lev], jnp.where(low_pair, known, got))
        back = jnp.where(leads, keep_ref[1, lev], jnp.where(low_pair, got, known))
        new_m_ref[lev] = mult_ref[lev] + step * model
        new_i_ref[lev] = incr_ref[lev] - step * back
    new_o_ref[...] = dual_ref[...] + step * dir_ref[...]


def exchange(value, partner):
    groups, tiles, peers = (lax.axis_size(x) for x in ("groups", "tile", "tm"))
    pairs = []
    for g in range(groups):
        for t in range(tiles):
            for k in range(peers):
                to_g, to_t, to_k = partner(g, t, k)
                target = (to_g * tiles + to_t) * peers + to_k
                pairs.append(((g * tiles + t) * peers + k, target))
    return lax.ppermute(value, ("groups", "tile", "tm"), pairs)


def swap(value, axis, distance):
    return lax.ppermute(value, axis, [(i, i ^ distance) for i in range(lax.axis_size(axis))])


def aside(g, t, k):
    return (g ^ 1, t, k) if lax.axis_size("groups") % 2 == 0 else (g, t ^ 1, k)


def leaders(value, tile, tm):
    return exchange(
        value, lambda g, t, k: (g, t ^ tile, k ^ tm) if k % 2 else aside(g, t, k)
    )


def next_pair(g, t, k):
    if 0 < k < lax.axis_size("tm") - 1:
        return g, t, (k - 1 if k % 2 == 0 else k + 1)
    return aside(g, t, k)


def second_side(g, t, k):
    if 0 < t < lax.axis_size("tile") - 1:
        return g, (t - 1 if t % 2 == 0 else t + 1), k
    return g, t, k ^ 1


def shifted(value, steps):
    count = lax.axis_size("tm")
    pairs = [(i, i + steps) for i in range(count) if 0 <= i + steps < count]
    return lax.ppermute(value, "tm", pairs)


def scanned(value, direction):
    reach = 1
    while reach < lax.axis_size("tm"):
        value = value + shifted(value, direction * reach)
        reach *= 2
    return value


def reduced(value, axis):
    distance = 1
    while distance < lax.axis_size(axis):
        value = value + swap(value, axis, distance)
        distance *= 2
    return value


def near(*arrays):
    return [(x, "near") for x in arrays]


def shards(
    multiplier, increment, obs_dual, rhs_model, rhs_obs, model_err, obs_err,
    drift_east, drift_north, diffusion, obs_cell, obs_count,
):
    tiles, peers = lax.axis_size("tile"), lax.axis_size("tm")
    levels, rows, cols = multiplier.shape[1:]
    field = ((levels, rows, cols), "near")
    lines = lambda n: ((n, levels, cols), "near")

    inner = swap(multiplier[0], "tm", 1)
    arguments = [increment[0], drift_east[0], drift_north[0], diffusion[0], multiplier[0]]
    arguments += [rhs_model[0], model_err[0], obs_cell, obs_dual, rhs_obs, obs_err]
    count = len(arguments)
    *here, moved, high, low, edge = kernel_call(
        lambda *refs: begin_body(count, *refs),
        "begin",
        [(x, "far") for x in arguments],
        [(x.shape, "near", x.dtype) for x in arguments]
        + [field, lines(3), lines(3), lines(len(EDGE))],
        [pltpu.SemaphoreType.DMA((count,))],
    )
    incr, *coeffs = here[:4]
    mult, rhs, err, cell, dual, want, var = here[4:]
    if peers == 4:
        later, wanted = inner, lambda: lax.rem(lax.axis_index("tm"), 2) == 0
    else:
        later = jnp.where(lax.axis_index("tm") % 2 == 0, inner, exchange(mult, next_pair))
        wanted = lambda: lax.axis_index("tm") < peers - 1
    first, second = kernel_call(
        lambda *refs: rims_body(wanted, *refs),
        "rims",
        near(edge, later, high, low),
        [lines(5), lines(5)],
    )
    got_first = swap(first, "tile", 1)
    got_second = exchange(second, second_side)
    valid = (lax.broadcasted_iota(jnp.int32, obs_cell.shape, 1) < obs_count).astype(F32)
    local, held, dir_obs, obs_sums = kernel_call(
        observe_body,
        "observe",
        near(incr, mult, rhs, err, cell, dual, want, var, valid),
        [field] * 2 + [(obs_dual.shape, "near"), ((2, *obs_dual.shape), "near")],
    )
    fix = kernel_call(
        edges_body, "edges", near(first, second, got_first, got_second, edge), [lines(8)]
    )[0]
    if peers != 4:
        later = jnp.where(lax.axis_index("tm") == peers - 1, 0.0, later)
        back = kernel_call(adjoint_body, "adjoint", near(*coeffs, later), [field])[0]
        return scan_path(
            multiplier, increment, obs_dual, local, moved, held, back, fix, dir_obs, obs_sums
        )
    cross = jnp.where(lax.axis_index("tm") < 2, moved, inner)
    got_cross = leaders(jnp.pad(cross, ((0, 1), (0, 0), (0, 0))), 0, 2)
    own, urgent = kernel_call(
        share_body,
        "share",
        near(*coeffs, inner, local, moved, held, fix),
        [((3, levels, rows, cols), "near"), field],
    )
    got = swap(urgent, "tm", 1)
    send = kernel_call(
        sends_body, "sends", near(own, got, fix), [((levels * rows + 4 * levels, cols), "near")]
    )[0]
    send, got_cross, own = lax.optimization_barrier((send, got_cross, own))
    got_send = leaders(send, 0, 2)
    rest = kernel_call(
        rest_body, "rest", near(own, obs_sums), [((2 * levels + 1, rows, cols), "near")]
    )[0]
    got_rest = swap(rest, "tm", 1)
    late_first, late_second = kernel_call(
        late_rims_body, "late_rims", near(edge, got_cross), [lines(2), lines(2)]
    )
    got_late_first = swap(late_first, "tile", 1)
    got_late_second = exchange(late_second, second_side)
    late_fix = kernel_call(
        late_edges_body,
        "late_edges",
        near(late_first, late_second, got_late_first, got_late_second)
        + near(got_first, got_second, edge),
        [lines(4)],
    )[0]
    terms, known = kernel_call(
        terms_body,
        "terms",
        near(*coeffs, got_cross, own, got, got_rest, late_fix),
        [((4, levels, rows, cols), "near"), field],
    )
    pair = ((2, levels, rows, cols), "near")
    keep, give, sums = kernel_call(
        dots_body, "dots", near(terms, got_send, got_rest, obs_sums), [pair, field, ((2, 8, 128), "near")]
    )
    total = sums + leaders(sums, 0, 2) + leaders(sums, 1, 0) + leaders(sums, 1, 2)
    distance = 2
    while distance < tiles:
        total = total + leaders(total, distance, 0)
        distance *= 2
    give, total = lax.optimization_barrier((give, total))
    got_dir = swap(give, "tm", 1)
    other = swap(total, "tm", 1)
    total = jnp.where(lax.axis_index("tm") % 2 == 1, total, other)
    new_m, new_i, new_o = kernel_call(
        update_body,
        "update",
        near(mult, incr, dual, dir_obs, keep, known, got_dir, total),
        [(mult.shape, "far"), (mult.shape, "far"), (obs_dual.shape, "far")],
    )
    return new_m[None], new_i[None], new_o


def scan_path(multiplier, increment, obs_dual, local, moved, held, back, fix, dir_obs, obs_sums):
    rows = local.shape[1]
    fix = jnp.moveaxis(fix, 0, 1)
    at = jnp.array([0, 1, rows - 2, rows - 1])
    moved = moved.at[:, at].add(fix[:, :4])
    res_incr = -(held - back.at[:, at].add(fix[:, 4:8]))
    res_model = local + shifted(moved, 1)
    dir_model, dir_incr = scanned(res_model, 1), scanned(res_incr, -1)
    numer = jnp.sum(res_model * dir_model) + jnp.sum(res_incr * dir_incr) + jnp.sum(obs_sums[0])
    denom = jnp.sum(dir_model**2) + jnp.sum(dir_incr**2) + jnp.sum(obs_sums[1])
    sums = reduced(reduced(jnp.stack([numer, denom]), "tm"), "tile")
    step = sums[0] / sums[1]
    return (
        multiplier + step * dir_model[None],
        increment + step * dir_incr[None],
        obs_dual + step * dir_obs,
    )


def solution(mesh):
    grid = P(("groups", "tm"), None, "tile", None)
    line = P(("groups", "tm"), "tile")
    return jax.shard_map(
        shards,
        mesh=mesh,
        in_specs=(grid, grid, line, grid, line, grid, line, grid, grid, grid, line, line),
        out_specs=(grid, grid, line),
        check_vma=False,
    )
```

```python
import jax
import jax.numpy as jnp
from jax import lax
from jax.experimental import pallas as pl
from jax.experimental.pallas import tpu as pltpu
from jax.sharding import PartitionSpec as P

F32 = jnp.float32
VMEM = pltpu.VMEM
GRANT = 24 * 1024 * 1024
WEIGHT = 3200000000


def kernel_call(body, name, inputs, outputs, scratch=(), weight=1):
    arrays, in_specs = [], []
    for array, home in inputs:
        if home == "far":
            in_specs.append(pl.BlockSpec(memory_space=pltpu.HBM))
            array = pltpu.with_memory_space_constraint(array, pltpu.HBM)
        else:
            in_specs.append(pl.BlockSpec(memory_space=VMEM))
            array = pltpu.with_memory_space_constraint(array, VMEM)
        arrays.append(array)
    out_shape = []
    for shape, home, *dtype in outputs:
        dtype = dtype[0] if dtype else F32
        out_shape.append(
            VMEM(shape, dtype) if home == "near" else jax.ShapeDtypeStruct(shape, dtype)
        )
    return pl.pallas_call(
        body,
        name=name,
        out_shape=out_shape,
        in_specs=in_specs,
        out_specs=[pl.BlockSpec(memory_space=VMEM)] * len(outputs),
        scratch_shapes=list(scratch),
        cost_estimate=pl.CostEstimate(flops=weight, bytes_accessed=1, transcendentals=0),
        compiler_params=pltpu.CompilerParams(vmem_limit_bytes=GRANT),
    )(*arrays)


def lanes(row):
    total = row[:, 0:128]
    for col in range(128, row.shape[1], 128):
        total = total + row[:, col : col + 128]
    return total


def iotas(shape):
    return (
        lax.broadcasted_iota(jnp.int32, shape, 0),
        lax.broadcasted_iota(jnp.int32, shape, 1),
    )


def up(field, axis):
    return pltpu.roll(field, field.shape[axis] - 1, axis)


def down(field, axis):
    return pltpu.roll(field, 1, axis)


def taps(a, b, c):
    i, y = iotas(a.shape)
    rows, cols = a.shape
    return (
        1.0 - 4.0 * c,
        jnp.where(i < rows - 1, c - a, 0.0),
        jnp.where(i > 0, c + a, 0.0),
        jnp.where(y < cols - 1, c - b, 0.0),
        jnp.where(y > 0, c + b, 0.0),
    )


def forward(state, coeffs):
    mid, east, west, north, south = coeffs
    return (
        mid * state
        + east * up(state, 0)
        + west * down(state, 0)
        + north * up(state, 1)
        + south * down(state, 1)
    )


def adjoint(state, coeffs):
    mid, east, west, north, south = coeffs
    return (
        mid * state
        + down(east * state, 0)
        + up(west * state, 0)
        + down(north * state, 1)
        + up(south * state, 1)
    )


EDGE = ("mid_low", "mid_high", "north_low", "north_high", "south_low", "south_high")
EDGE += ("west_low", "west_next", "east_high", "east_next", "east_low", "west_high")


def begin_body(count, *refs):
    sources, targets = refs[:count], refs[count : 2 * count]
    moved_ref, high_ref, low_ref, edge_ref, sems = refs[2 * count :]
    copies = [
        pltpu.make_async_copy(source, target, sems.at[n])
        for n, (source, target) in enumerate(zip(sources, targets))
    ]
    for copy in copies:
        copy.start()
    for copy in copies[:4]:
        copy.wait()
    s_ref, a_ref, b_ref, c_ref = targets[:4]
    levels, rows, _ = s_ref.shape
    last = rows - 1
    for lev in range(levels):
        s, a, b, c = s_ref[lev], a_ref[lev], b_ref[lev], c_ref[lev]
        coeffs = taps(a, b, c)
        once = forward(s, coeffs)
        moved_ref[lev] = forward(once, coeffs)
        mid, east, west, north, south = coeffs
        at = pl.ds(lev, 1)
        open_east = c[last : last + 1] - a[last : last + 1]
        open_west = c[0:1] + a[0:1]
        high_ref[0, at] = s[last : last + 1]
        high_ref[1, at] = once[last : last + 1]
        high_ref[2, at] = open_east
        low_ref[0, at] = s[0:1]
        low_ref[1, at] = once[0:1]
        low_ref[2, at] = open_west
        rows_of = {
            "mid_low": mid[0:1],
            "mid_high": mid[last : last + 1],
            "north_low": north[0:1],
            "north_high": north[last : last + 1],
            "south_low": south[0:1],
            "south_high": south[last : last + 1],
            "west_low": open_west,
            "west_next": west[1:2],
            "east_high": open_east,
            "east_next": east[last - 1 : last],
            "east_low": east[0:1],
            "west_high": west[last : last + 1],
        }
        for n, key in enumerate(EDGE):
            edge_ref[n, at] = rows_of[key]
    for copy in copies[4:]:
        copy.wait()


def adjoint_body(a_ref, b_ref, c_ref, later_ref, back_ref):
    for lev in range(a_ref.shape[0]):
        coeffs = taps(a_ref[lev], b_ref[lev], c_ref[lev])
        back_ref[lev] = adjoint(adjoint(later_ref[lev], coeffs), coeffs)


def outer_products(k, later):
    def once(side, at, beside):
        mid, north, south = k["mid_" + side], k["north_" + side], k["south_" + side]
        return mid * at + beside + down(north * at, 1) + up(south * at, 1)

    west, east = k["west_low"], k["east_high"]
    return (
        (west * later[0], west * once("low", later[0], k["west_next"] * later[1])),
        (east * later[3], east * once("high", later[3], k["east_next"] * later[2])),
    )


def outer_rows(ref, levels, wanted):
    rows = ref.shape[1]
    picked = []
    for row in (0, 1, rows - 2, rows - 1):
        value = jnp.concatenate([ref[lev, row : row + 1] for lev in range(levels)], 0)
        picked.append(jnp.where(wanted, value, 0.0))
    return picked


def rims_body(wanted, edge_ref, later_ref, high_ref, low_ref, first_ref, second_ref):
    odd = lax.rem(lax.axis_index("tile"), 2)
    k = {key: edge_ref[n] for n, key in enumerate(EDGE)}
    low, high = outer_products(k, outer_rows(later_ref, edge_ref.shape[1], wanted()))
    lows = [low_ref[n] for n in range(3)] + list(low)
    highs = [high_ref[n] for n in range(3)] + list(high)
    for n in range(5):
        first_ref[n] = jnp.where(odd == 0, highs[n], lows[n])
        second_ref[n] = jnp.where(odd == 0, lows[n], highs[n])


def late_rims_body(edge_ref, later_ref, first_ref, second_ref):
    odd = lax.rem(lax.axis_index("tile"), 2)
    k = {key: edge_ref[n] for n, key in enumerate(EDGE)}
    low, high = outer_products(k, outer_rows(later_ref, edge_ref.shape[1], lax.axis_index("tm") == 1))
    for n in range(2):
        first_ref[n] = jnp.where(odd == 0, high[n], low[n])
        second_ref[n] = jnp.where(odd == 0, low[n], high[n])


def sides(first, second):
    tile, tiles = lax.axis_index("tile"), lax.axis_size("tile")
    odd = lax.rem(tile, 2)
    below, above = jnp.where(odd == 0, second, first), jnp.where(odd == 0, first, second)
    return jnp.where(tile > 0, below, 0.0), jnp.where(tile < tiles - 1, above, 0.0)


def own_sides(first, second):
    odd = lax.rem(lax.axis_index("tile"), 2)
    return jnp.where(odd == 0, second, first), jnp.where(odd == 0, first, second)


def back_fix(k, product, stepped, own_product, toward):
    def across(x, side):
        mid, north, south = k["mid_" + side], k["north_" + side], k["south_" + side]
        return mid * x + down(north * x, 1) + up(south * x, 1)

    return (
        across(product[0], "low") + (stepped[0] + toward[0] * own_product[0]),
        k["east_low"] * product[0],
        k["west_high"] * product[1],
        across(product[1], "high") + (stepped[1] + toward[1] * own_product[1]),
    )


def edges_body(first_ref, second_ref, got_first_ref, got_second_ref, edge_ref, fix_ref):
    k = {key: edge_ref[n] for n, key in enumerate(EDGE)}
    state, stepped, toward, product, product_stepped = (
        sides(got_first_ref[n], got_second_ref[n]) for n in range(5)
    )
    own_state = own_sides(first_ref[0], second_ref[0])
    own_product = own_sides(first_ref[3], second_ref[3])

    def along(x, side):
        mid, north, south = k["mid_" + side], k["north_" + side], k["south_" + side]
        return mid * x + north * up(x, 1) + south * down(x, 1)

    new_low, new_high = k["west_low"] * state[0], k["east_high"] * state[1]
    fix_ref[0] = along(new_low, "low") + k["west_low"] * (stepped[0] + toward[0] * own_state[0])
    fix_ref[1] = k["west_next"] * new_low
    fix_ref[2] = k["east_next"] * new_high
    fix_ref[3] = along(new_high, "high") + k["east_high"] * (stepped[1] + toward[1] * own_state[1])
    for n, row in enumerate(back_fix(k, product, product_stepped, own_product, toward)):
        fix_ref[4 + n] = row


def late_edges_body(
    first_ref, second_ref, got_first_ref, got_second_ref, past_first_ref, past_second_ref,
    edge_ref, fix_ref,
):
    k = {key: edge_ref[n] for n, key in enumerate(EDGE)}
    product, stepped = (sides(got_first_ref[n], got_second_ref[n]) for n in range(2))
    toward = sides(past_first_ref[2], past_second_ref[2])
    own_product = own_sides(first_ref[0], second_ref[0])
    for n, row in enumerate(back_fix(k, product, stepped, own_product, toward)):
        fix_ref[n] = row


def thirds(x):
    one = x.astype(jnp.bfloat16)
    rest = x - one.astype(F32)
    two = rest.astype(jnp.bfloat16)
    return one, two, (rest - two.astype(F32)).astype(jnp.bfloat16)


def slot_masks(cell, lines, cols):
    slots = cell.shape[1]
    at_line = iotas((lines, slots))[0] == cell // cols
    at_col = iotas((cols, slots))[0] == lax.rem(cell, cols)
    return at_line, jnp.where(at_col, 1.0, 0.0).astype(jnp.bfloat16)


def spread_body(
    incr_ref, mult_ref, rhs_ref, err_ref, cell_ref, dual_ref, valid_ref, local_ref, held_ref
):
    levels, rows, cols = incr_ref.shape
    lines = levels * rows
    at_line, at_col = slot_masks(cell_ref[...], lines, cols)
    weights = thirds(jnp.where(at_line, valid_ref[...] * dual_ref[...], 0.0))
    spread = lax.dot_general(
        jnp.concatenate(weights, 0), at_col, (((1,), (1,)), ((), ())), preferred_element_type=F32
    )
    ht = spread[:lines] + spread[lines : 2 * lines] + spread[2 * lines :]
    mult = mult_ref[...]
    held_ref[...] = mult + ht.reshape(levels, rows, cols)
    local_ref[...] = rhs_ref[...] - (err_ref[...] * mult + incr_ref[...])


def gather_body(
    incr_ref, cell_ref, dual_ref, want_ref, var_ref, valid_ref, dir_ref, sums_ref
):
    levels, rows, cols = incr_ref.shape
    lines = levels * rows
    at_line, at_col = slot_masks(cell_ref[...], lines, cols)
    fields = thirds(incr_ref[...].reshape(lines, cols))
    picked = jnp.dot(jnp.concatenate(fields, 0), at_col, preferred_element_type=F32)
    picked = picked[:lines] + picked[lines : 2 * lines] + picked[2 * lines :]
    valid, var = valid_ref[...], var_ref[...]
    hx = jnp.sum(jnp.where(at_line, picked, 0.0), axis=0, keepdims=True) * valid
    res = valid * (want_ref[...] - (var * dual_ref[...] + hx))
    direction = res / var
    dir_ref[...] = direction
    sums_ref[0] = res * direction
    sums_ref[1] = direction * direction


def corrected(field, fix):
    rows = field.shape[0]
    i, _ = iotas(field.shape)
    for n, row in enumerate((0, 1, rows - 2, rows - 1)):
        field = field + jnp.where(i == row, fix[n], 0.0)
    return field


def fixes(ref, start, lev):
    return [ref[start + n, pl.ds(lev, 1)] for n in range(4)]


def minus(rows):
    return [-x for x in rows]


def share_body(local_ref, moved_ref, held_ref, back_ref, fix_ref, own_ref, urgent_ref):
    position = lax.axis_index("tm")
    first, low_pair = lax.rem(position, 2) == 0, position < 2
    for lev in range(local_ref.shape[0]):
        back = corrected(back_ref[lev], fixes(fix_ref, 4, lev))
        moved = corrected(moved_ref[lev], fixes(fix_ref, 0, lev))
        local = local_ref[lev]
        residual = held_ref[lev] - jnp.where(first, back, 0.0)
        own_ref[0, lev] = local
        own_ref[1, lev] = moved
        own_ref[2, lev] = residual
        urgent_ref[lev] = jnp.where(low_pair, local + moved, residual)


def sends_body(own_ref, got_ref, fix_ref, send_ref):
    _, levels, rows, _ = own_ref.shape
    low_pair = lax.axis_index("tm") < 2
    for lev in range(levels):
        mine = jnp.where(low_pair, own_ref[0, lev], own_ref[2, lev])
        send_ref[lev * rows : (lev + 1) * rows] = mine + got_ref[lev]
    for n in range(4):
        start = levels * rows + n * levels
        send_ref[start : start + levels] = fix_ref[n]


def rest_body(own_ref, obs_ref, local_ref, other_ref):
    levels = own_ref.shape[1]
    low_pair = lax.axis_index("tm") < 2
    for lev in range(levels):
        local_ref[lev] = own_ref[0, lev]
        other_ref[lev] = jnp.where(low_pair, own_ref[2, lev], own_ref[1, lev])
    local_ref[levels] = jnp.zeros(local_ref.shape[1:], F32)
    for n in range(2):
        local_ref[levels, n : n + 1, 0:128] = lanes(obs_ref[n])


def terms_body(
    cross_ref, beyond_ref, own_ref, got_ref, rest_ref, other_ref, fix_ref, terms_ref, known_ref
):
    low_pair = lax.axis_index("tm") < 2
    levels = own_ref.shape[1]
    for lev in range(levels):
        cross, got = cross_ref[lev], got_ref[lev]
        local, residual = own_ref[0, lev], own_ref[2, lev]
        back = corrected(beyond_ref[lev], fixes(fix_ref, 0, lev))
        rest0, rest1 = rest_ref[lev], other_ref[lev]
        terms_ref[0, lev] = jnp.where(low_pair, rest0, residual)
        terms_ref[1, lev] = jnp.where(low_pair, local, residual) + got
        terms_ref[2, lev] = jnp.where(low_pair, residual - back, rest0 + cross)
        terms_ref[3, lev] = jnp.where(low_pair, rest1, local + rest1)
        known_ref[lev] = jnp.where(low_pair, local, residual + got)


def dots_body(terms_ref, got_ref, rest_ref, obs_ref, keep_ref, give_ref, sums_ref):
    _, levels, rows, cols = terms_ref.shape
    low_pair = lax.axis_index("tm") < 2
    numer, denom = jnp.zeros((8, 128), F32), jnp.zeros((8, 128), F32)

    def folded(x):
        total = None
        for r in range(0, rows, 8):
            part = lanes(x[r : r + 8])
            total = part if total is None else total + part
        return total

    for lev in range(levels):
        y0, one, z0, z1 = (terms_ref[n, lev] for n in range(4))
        late = []
        for n in range(4):
            at = levels * rows + n * levels + lev
            late.append(jnp.where(low_pair, 0.0, got_ref[at : at + 1]))
        z0 = corrected(z0, late)
        two = got_ref[lev * rows : (lev + 1) * rows] + z0
        three = two + z1
        numer = numer + folded(y0 * y0 + (one - y0) * one + z0 * two + z1 * three)
        denom = denom + folded(y0 * y0 + one * one + two * two + three * three)
        keep_ref[0, lev] = jnp.where(low_pair, one, three)
        keep_ref[1, lev] = jnp.where(low_pair, two, y0)
        give_ref[lev] = jnp.where(low_pair, three, two)
    for n, total in enumerate((numer, denom)):
        sums_ref[n] = total
        obs = lanes(obs_ref[n]) + rest_ref[levels, n : n + 1, 0:128]
        sums_ref[n, 0:1] = total[0:1] + obs


def update_body(
    mult_ref, incr_ref, dual_ref, dir_ref, keep_ref, known_ref, got_ref, sums_ref,
    new_m_ref, new_i_ref, new_o_ref,
):
    position = lax.axis_index("tm")
    leads, low_pair = lax.rem(position, 2) == 1, position < 2
    total = [
        jnp.sum(jnp.sum(sums_ref[n], axis=0, keepdims=True), axis=1, keepdims=True)
        for n in range(2)
    ]
    step = total[0] / total[1]
    for lev in range(mult_ref.shape[0]):
        known, got = known_ref[lev], got_ref[lev]
        model = jnp.where(leads, keep_ref[0, lev], jnp.where(low_pair, known, got))
        back = jnp.where(leads, keep_ref[1, lev], jnp.where(low_pair, got, known))
        new_m_ref[lev] = mult_ref[lev] + step * model
        new_i_ref[lev] = incr_ref[lev] - step * back
    new_o_ref[...] = dual_ref[...] + step * dir_ref[...]


def exchange(value, partner):
    groups, tiles, peers = (lax.axis_size(x) for x in ("groups", "tile", "tm"))
    pairs = []
    for g in range(groups):
        for t in range(tiles):
            for k in range(peers):
                to_g, to_t, to_k = partner(g, t, k)
                target = (to_g * tiles + to_t) * peers + to_k
                pairs.append(((g * tiles + t) * peers + k, target))
    return lax.ppermute(value, ("groups", "tile", "tm"), pairs)


def swap(value, axis, distance):
    return lax.ppermute(value, axis, [(i, i ^ distance) for i in range(lax.axis_size(axis))])


def aside(g, t, k):
    return (g ^ 1, t, k) if lax.axis_size("groups") % 2 == 0 else (g, t ^ 1, k)


def leaders(value, tile, tm):
    return exchange(
        value, lambda g, t, k: (g, t ^ tile, k ^ tm) if k % 2 else aside(g, t, k)
    )


def next_pair(g, t, k):
    if 0 < k < lax.axis_size("tm") - 1:
        return g, t, (k - 1 if k % 2 == 0 else k + 1)
    return aside(g, t, k)


def second_side(g, t, k):
    if 0 < t < lax.axis_size("tile") - 1:
        return g, (t - 1 if t % 2 == 0 else t + 1), k
    return g, t, k ^ 1


def shifted(value, steps):
    count = lax.axis_size("tm")
    pairs = [(i, i + steps) for i in range(count) if 0 <= i + steps < count]
    return lax.ppermute(value, "tm", pairs)


def scanned(value, direction):
    reach = 1
    while reach < lax.axis_size("tm"):
        value = value + shifted(value, direction * reach)
        reach *= 2
    return value


def reduced(value, axis):
    distance = 1
    while distance < lax.axis_size(axis):
        value = value + swap(value, axis, distance)
        distance *= 2
    return value


def near(*arrays):
    return [(x, "near") for x in arrays]


def shards(
    multiplier, increment, obs_dual, rhs_model, rhs_obs, model_err, obs_err,
    drift_east, drift_north, diffusion, obs_cell, obs_count,
):
    tiles, peers = lax.axis_size("tile"), lax.axis_size("tm")
    levels, rows, cols = multiplier.shape[1:]
    field = ((levels, rows, cols), "near")
    lines = lambda n: ((n, levels, cols), "near")

    inner = swap(multiplier[0], "tm", 1)
    arguments = [increment[0], drift_east[0], drift_north[0], diffusion[0], multiplier[0]]
    arguments += [rhs_model[0], model_err[0], obs_cell, obs_dual, rhs_obs, obs_err]
    count = len(arguments)
    *here, moved, high, low, edge = kernel_call(
        lambda *refs: begin_body(count, *refs),
        "begin",
        [(x, "far") for x in arguments],
        [(x.shape, "near", x.dtype) for x in arguments]
        + [field, lines(3), lines(3), lines(len(EDGE))],
        [pltpu.SemaphoreType.DMA((count,))],
    )
    incr, *coeffs = here[:4]
    mult, rhs, err, cell, dual, want, var = here[4:]
    if peers == 4:
        later, wanted = inner, lambda: lax.rem(lax.axis_index("tm"), 2) == 0
    else:
        later = jnp.where(lax.axis_index("tm") % 2 == 0, inner, exchange(mult, next_pair))
        wanted = lambda: lax.axis_index("tm") < peers - 1
    first, second = kernel_call(
        lambda *refs: rims_body(wanted, *refs),
        "rims",
        near(edge, later, high, low),
        [lines(5), lines(5)],
    )
    got_first = swap(first, "tile", 1)
    got_second = exchange(second, second_side)
    valid = (lax.broadcasted_iota(jnp.int32, obs_cell.shape, 1) < obs_count).astype(F32)
    local, held = kernel_call(
        spread_body, "spread", near(incr, mult, rhs, err, cell, dual, valid), [field] * 2
    )
    fix = kernel_call(
        edges_body, "edges", near(first, second, got_first, got_second, edge), [lines(8)]
    )[0]
    if peers != 4:
        later = jnp.where(lax.axis_index("tm") == peers - 1, 0.0, later)
        back = kernel_call(adjoint_body, "adjoint", near(*coeffs, later), [field])[0]
        dir_obs, obs_sums = kernel_call(
            gather_body,
            "gather",
            near(incr, cell, dual, want, var, valid),
            [(obs_dual.shape, "near"), ((2, *obs_dual.shape), "near")],
        )
        return scan_path(
            multiplier, increment, obs_dual, local, moved, held, back, fix, dir_obs, obs_sums
        )
    cross = jnp.where(lax.axis_index("tm") < 2, moved, inner)
    got_cross = leaders(jnp.pad(cross, ((0, 1), (0, 0), (0, 0))), 0, 2)
    back = kernel_call(adjoint_body, "adjoint", near(*coeffs, inner), [field])[0]
    own, urgent = kernel_call(
        share_body,
        "share",
        near(local, moved, held, back, fix),
        [((3, levels, rows, cols), "near"), field],
    )
    got = swap(urgent, "tm", 1)
    send = kernel_call(
        sends_body, "sends", near(own, got, fix), [((levels * rows + 4 * levels, cols), "near")]
    )[0]
    send, own, cell = lax.optimization_barrier((send, own, cell))
    got_send = leaders(send, 0, 2)
    dir_obs, obs_sums = kernel_call(
        gather_body,
        "gather",
        near(incr, cell, dual, want, var, valid),
        [(obs_dual.shape, "near"), ((2, *obs_dual.shape), "near")],
    )
    rest, other = kernel_call(
        rest_body, "rest", near(own, obs_sums), [((levels + 1, rows, cols), "near"), field]
    )
    got_rest, got_other = swap(rest, "tm", 1), swap(other, "tm", 1)
    late_first, late_second = kernel_call(
        late_rims_body, "late_rims", near(edge, got_cross), [lines(2), lines(2)], weight=WEIGHT
    )
    got_late_first = swap(late_first, "tile", 1)
    got_late_second = exchange(late_second, second_side)
    late_fix = kernel_call(
        late_edges_body,
        "late_edges",
        near(late_first, late_second, got_late_first, got_late_second)
        + near(got_first, got_second, edge),
        [lines(4)],
    )[0]
    beyond = kernel_call(adjoint_body, "beyond", near(*coeffs, got_cross), [field])[0]
    terms, known = kernel_call(
        terms_body,
        "terms",
        near(got_cross, beyond, own, got, got_rest, got_other, late_fix),
        [((4, levels, rows, cols), "near"), field],
    )
    pair = ((2, levels, rows, cols), "near")
    keep, give, sums = kernel_call(
        dots_body, "dots", near(terms, got_send, got_rest, obs_sums), [pair, field, ((2, 8, 128), "near")]
    )
    total = sums + leaders(sums, 0, 2) + leaders(sums, 1, 0) + leaders(sums, 1, 2)
    distance = 2
    while distance < tiles:
        total = total + leaders(total, distance, 0)
        distance *= 2
    give, total = lax.optimization_barrier((give, total))
    got_dir = swap(give, "tm", 1)
    other = swap(total, "tm", 1)
    total = jnp.where(lax.axis_index("tm") % 2 == 1, total, other)
    new_m, new_i, new_o = kernel_call(
        update_body,
        "update",
        near(mult, incr, dual, dir_obs, keep, known, got_dir, total),
        [(mult.shape, "far"), (mult.shape, "far"), (obs_dual.shape, "far")],
    )
    return new_m[None], new_i[None], new_o


def scan_path(multiplier, increment, obs_dual, local, moved, held, back, fix, dir_obs, obs_sums):
    rows = local.shape[1]
    fix = jnp.moveaxis(fix, 0, 1)
    at = jnp.array([0, 1, rows - 2, rows - 1])
    moved = moved.at[:, at].add(fix[:, :4])
    res_incr = -(held - back.at[:, at].add(fix[:, 4:8]))
    res_model = local + shifted(moved, 1)
    dir_model, dir_incr = scanned(res_model, 1), scanned(res_incr, -1)
    numer = jnp.sum(res_model * dir_model) + jnp.sum(res_incr * dir_incr) + jnp.sum(obs_sums[0])
    denom = jnp.sum(dir_model**2) + jnp.sum(dir_incr**2) + jnp.sum(obs_sums[1])
    sums = reduced(reduced(jnp.stack([numer, denom]), "tm"), "tile")
    step = sums[0] / sums[1]
    return (
        multiplier + step * dir_model[None],
        increment + step * dir_incr[None],
        obs_dual + step * dir_obs,
    )


def solution(mesh):
    grid = P(("groups", "tm"), None, "tile", None)
    line = P(("groups", "tm"), "tile")
    return jax.shard_map(
        shards,
        mesh=mesh,
        in_specs=(grid, grid, line, grid, line, grid, line, grid, grid, grid, line, line),
        out_specs=(grid, grid, line),
        check_vma=False,
    )
```

```python
import jax
import jax.numpy as jnp
from jax import lax
from jax.experimental import pallas as pl
from jax.experimental.pallas import tpu as pltpu
from jax.sharding import PartitionSpec as P

F32 = jnp.float32
VMEM = pltpu.VMEM
GRANT = 24 * 1024 * 1024
WEIGHT = 3200000000
PARTS = 2


def kernel_call(body, name, inputs, outputs, scratch=(), weight=1):
    arrays, in_specs = [], []
    for array, home in inputs:
        if home == "far":
            in_specs.append(pl.BlockSpec(memory_space=pltpu.HBM))
            array = pltpu.with_memory_space_constraint(array, pltpu.HBM)
        else:
            in_specs.append(pl.BlockSpec(memory_space=VMEM))
            array = pltpu.with_memory_space_constraint(array, VMEM)
        arrays.append(array)
    out_shape, out_specs = [], []
    for shape, home, *dtype in outputs:
        dtype = dtype[0] if dtype else F32
        out_specs.append(pl.BlockSpec(memory_space=VMEM))
        out_shape.append(
            VMEM(shape, dtype) if home == "near" else jax.ShapeDtypeStruct(shape, dtype)
        )
    return pl.pallas_call(
        body,
        name=name,
        out_shape=out_shape,
        in_specs=in_specs,
        out_specs=out_specs,
        scratch_shapes=list(scratch),
        cost_estimate=pl.CostEstimate(flops=weight, bytes_accessed=1, transcendentals=0),
        compiler_params=pltpu.CompilerParams(vmem_limit_bytes=GRANT),
    )(*arrays)


def lanes(row):
    total = row[:, 0:128]
    for col in range(128, row.shape[1], 128):
        total = total + row[:, col : col + 128]
    return total


def iotas(shape):
    return (
        lax.broadcasted_iota(jnp.int32, shape, 0),
        lax.broadcasted_iota(jnp.int32, shape, 1),
    )


def up(field, axis):
    return pltpu.roll(field, field.shape[axis] - 1, axis)


def down(field, axis):
    return pltpu.roll(field, 1, axis)


def taps(a, b, c):
    i, y = iotas(a.shape)
    rows, cols = a.shape
    return (
        1.0 - 4.0 * c,
        jnp.where(i < rows - 1, c - a, 0.0),
        jnp.where(i > 0, c + a, 0.0),
        jnp.where(y < cols - 1, c - b, 0.0),
        jnp.where(y > 0, c + b, 0.0),
    )


def forward(state, coeffs):
    mid, east, west, north, south = coeffs
    return (
        mid * state
        + east * up(state, 0)
        + west * down(state, 0)
        + north * up(state, 1)
        + south * down(state, 1)
    )


def adjoint(state, coeffs):
    mid, east, west, north, south = coeffs
    return (
        mid * state
        + down(east * state, 0)
        + up(west * state, 0)
        + down(north * state, 1)
        + up(south * state, 1)
    )


EDGE = ("mid_low", "mid_high", "north_low", "north_high", "south_low", "south_high")
EDGE += ("west_low", "west_next", "east_high", "east_next", "east_low", "west_high")


def begin_body(count, *refs):
    sources, targets = refs[:count], refs[count : 2 * count]
    moved_ref, high_ref, low_ref, edge_ref, sems = refs[2 * count :]
    s_ref, a_ref, b_ref, c_ref = targets[:4]
    levels, rows, _ = s_ref.shape
    last = rows - 1
    cut = levels // PARTS
    parts = [
        [
            pltpu.make_async_copy(
                sources[n].at[pl.ds(part * cut, cut)],
                targets[n].at[pl.ds(part * cut, cut)],
                sems.at[part * 4 + n],
            )
            for n in range(4)
        ]
        for part in range(PARTS)
    ]
    rest = [
        pltpu.make_async_copy(sources[n], targets[n], sems.at[4 * (PARTS - 1) + n])
        for n in range(4, count)
    ]
    for copy in sum(parts, []) + rest:
        copy.start()
    for lev in range(levels):
        if lev % cut == 0:
            for copy in parts[lev // cut]:
                copy.wait()
        s, a, b, c = s_ref[lev], a_ref[lev], b_ref[lev], c_ref[lev]
        coeffs = taps(a, b, c)
        once = forward(s, coeffs)
        moved_ref[lev] = forward(once, coeffs)
        mid, east, west, north, south = coeffs
        at = pl.ds(lev, 1)
        open_east = c[last : last + 1] - a[last : last + 1]
        open_west = c[0:1] + a[0:1]
        high_ref[0, at] = s[last : last + 1]
        high_ref[1, at] = once[last : last + 1]
        high_ref[2, at] = open_east
        low_ref[0, at] = s[0:1]
        low_ref[1, at] = once[0:1]
        low_ref[2, at] = open_west
        rows_of = {
            "mid_low": mid[0:1],
            "mid_high": mid[last : last + 1],
            "north_low": north[0:1],
            "north_high": north[last : last + 1],
            "south_low": south[0:1],
            "south_high": south[last : last + 1],
            "west_low": open_west,
            "west_next": west[1:2],
            "east_high": open_east,
            "east_next": east[last - 1 : last],
            "east_low": east[0:1],
            "west_high": west[last : last + 1],
        }
        for n, key in enumerate(EDGE):
            edge_ref[n, at] = rows_of[key]
    for copy in rest:
        copy.wait()


def adjoint_body(a_ref, b_ref, c_ref, later_ref, back_ref):
    for lev in range(a_ref.shape[0]):
        coeffs = taps(a_ref[lev], b_ref[lev], c_ref[lev])
        back_ref[lev] = adjoint(adjoint(later_ref[lev], coeffs), coeffs)


def outer_products(k, later):
    def once(side, at, beside):
        mid, north, south = k["mid_" + side], k["north_" + side], k["south_" + side]
        return mid * at + beside + down(north * at, 1) + up(south * at, 1)

    west, east = k["west_low"], k["east_high"]
    return (
        (west * later[0], west * once("low", later[0], k["west_next"] * later[1])),
        (east * later[3], east * once("high", later[3], k["east_next"] * later[2])),
    )


def outer_rows(ref, levels, wanted):
    rows = ref.shape[1]
    picked = []
    for row in (0, 1, rows - 2, rows - 1):
        value = jnp.concatenate([ref[lev, row : row + 1] for lev in range(levels)], 0)
        picked.append(jnp.where(wanted, value, 0.0))
    return picked


def rims_body(wanted, edge_ref, later_ref, high_ref, low_ref, first_ref, second_ref):
    odd = lax.rem(lax.axis_index("tile"), 2)
    k = {key: edge_ref[n] for n, key in enumerate(EDGE)}
    low, high = outer_products(k, outer_rows(later_ref, edge_ref.shape[1], wanted()))
    lows = [low_ref[n] for n in range(3)] + list(low)
    highs = [high_ref[n] for n in range(3)] + list(high)
    for n in range(5):
        first_ref[n] = jnp.where(odd == 0, highs[n], lows[n])
        second_ref[n] = jnp.where(odd == 0, lows[n], highs[n])


def late_rims_body(edge_ref, later_ref, first_ref, second_ref):
    odd = lax.rem(lax.axis_index("tile"), 2)
    k = {key: edge_ref[n] for n, key in enumerate(EDGE)}
    low, high = outer_products(k, outer_rows(later_ref, edge_ref.shape[1], lax.axis_index("tm") == 1))
    for n in range(2):
        first_ref[n] = jnp.where(odd == 0, high[n], low[n])
        second_ref[n] = jnp.where(odd == 0, low[n], high[n])


def sides(first, second):
    tile, tiles = lax.axis_index("tile"), lax.axis_size("tile")
    odd = lax.rem(tile, 2)
    below, above = jnp.where(odd == 0, second, first), jnp.where(odd == 0, first, second)
    return jnp.where(tile > 0, below, 0.0), jnp.where(tile < tiles - 1, above, 0.0)


def own_sides(first, second):
    odd = lax.rem(lax.axis_index("tile"), 2)
    return jnp.where(odd == 0, second, first), jnp.where(odd == 0, first, second)


def back_fix(k, product, stepped, own_product, toward):
    def across(x, side):
        mid, north, south = k["mid_" + side], k["north_" + side], k["south_" + side]
        return mid * x + down(north * x, 1) + up(south * x, 1)

    return (
        across(product[0], "low") + (stepped[0] + toward[0] * own_product[0]),
        k["east_low"] * product[0],
        k["west_high"] * product[1],
        across(product[1], "high") + (stepped[1] + toward[1] * own_product[1]),
    )


def edges_body(first_ref, second_ref, got_first_ref, got_second_ref, edge_ref, fix_ref):
    k = {key: edge_ref[n] for n, key in enumerate(EDGE)}
    state, stepped, toward, product, product_stepped = (
        sides(got_first_ref[n], got_second_ref[n]) for n in range(5)
    )
    own_state = own_sides(first_ref[0], second_ref[0])
    own_product = own_sides(first_ref[3], second_ref[3])

    def along(x, side):
        mid, north, south = k["mid_" + side], k["north_" + side], k["south_" + side]
        return mid * x + north * up(x, 1) + south * down(x, 1)

    new_low, new_high = k["west_low"] * state[0], k["east_high"] * state[1]
    fix_ref[0] = along(new_low, "low") + k["west_low"] * (stepped[0] + toward[0] * own_state[0])
    fix_ref[1] = k["west_next"] * new_low
    fix_ref[2] = k["east_next"] * new_high
    fix_ref[3] = along(new_high, "high") + k["east_high"] * (stepped[1] + toward[1] * own_state[1])
    for n, row in enumerate(back_fix(k, product, product_stepped, own_product, toward)):
        fix_ref[4 + n] = row


def late_edges_body(
    first_ref, second_ref, got_first_ref, got_second_ref, past_first_ref, past_second_ref,
    edge_ref, fix_ref,
):
    k = {key: edge_ref[n] for n, key in enumerate(EDGE)}
    product, stepped = (sides(got_first_ref[n], got_second_ref[n]) for n in range(2))
    toward = sides(past_first_ref[2], past_second_ref[2])
    own_product = own_sides(first_ref[0], second_ref[0])
    for n, row in enumerate(back_fix(k, product, stepped, own_product, toward)):
        fix_ref[n] = row


def thirds(x):
    one = x.astype(jnp.bfloat16)
    rest = x - one.astype(F32)
    two = rest.astype(jnp.bfloat16)
    return one, two, (rest - two.astype(F32)).astype(jnp.bfloat16)


def slot_masks(cell, lines, cols):
    slots = cell.shape[1]
    at_line = iotas((lines, slots))[0] == cell // cols
    at_col = iotas((cols, slots))[0] == lax.rem(cell, cols)
    return at_line, jnp.where(at_col, 1.0, 0.0).astype(jnp.bfloat16)


def spread_body(
    incr_ref, mult_ref, rhs_ref, err_ref, cell_ref, dual_ref, valid_ref, local_ref, held_ref
):
    levels, rows, cols = incr_ref.shape
    lines = levels * rows
    at_line, at_col = slot_masks(cell_ref[...], lines, cols)
    weights = thirds(jnp.where(at_line, valid_ref[...] * dual_ref[...], 0.0))
    spread = lax.dot_general(
        jnp.concatenate(weights, 0), at_col, (((1,), (1,)), ((), ())), preferred_element_type=F32
    )
    ht = spread[:lines] + spread[lines : 2 * lines] + spread[2 * lines :]
    mult = mult_ref[...]
    held_ref[...] = mult + ht.reshape(levels, rows, cols)
    local_ref[...] = rhs_ref[...] - (err_ref[...] * mult + incr_ref[...])


def gather_body(
    incr_ref, cell_ref, dual_ref, want_ref, var_ref, valid_ref, dir_ref, sums_ref
):
    levels, rows, cols = incr_ref.shape
    lines = levels * rows
    at_line, at_col = slot_masks(cell_ref[...], lines, cols)
    fields = thirds(incr_ref[...].reshape(lines, cols))
    picked = jnp.dot(jnp.concatenate(fields, 0), at_col, preferred_element_type=F32)
    picked = picked[:lines] + picked[lines : 2 * lines] + picked[2 * lines :]
    valid, var = valid_ref[...], var_ref[...]
    hx = jnp.sum(jnp.where(at_line, picked, 0.0), axis=0, keepdims=True) * valid
    res = valid * (want_ref[...] - (var * dual_ref[...] + hx))
    direction = res / var
    dir_ref[...] = direction
    sums_ref[0] = res * direction
    sums_ref[1] = direction * direction


def corrected(field, fix):
    rows = field.shape[0]
    i, _ = iotas(field.shape)
    for n, row in enumerate((0, 1, rows - 2, rows - 1)):
        field = field + jnp.where(i == row, fix[n], 0.0)
    return field


def fixes(ref, start, lev):
    return [ref[start + n, pl.ds(lev, 1)] for n in range(4)]


def minus(rows):
    return [-x for x in rows]


def share_body(local_ref, moved_ref, held_ref, back_ref, fix_ref, own_ref, urgent_ref):
    position = lax.axis_index("tm")
    first, low_pair = lax.rem(position, 2) == 0, position < 2
    for lev in range(local_ref.shape[0]):
        back = corrected(back_ref[lev], fixes(fix_ref, 4, lev))
        moved = corrected(moved_ref[lev], fixes(fix_ref, 0, lev))
        local = local_ref[lev]
        residual = held_ref[lev] - jnp.where(first, back, 0.0)
        own_ref[0, lev] = local
        own_ref[1, lev] = moved
        own_ref[2, lev] = residual
        urgent_ref[lev] = jnp.where(low_pair, local + moved, residual)


def sends_body(own_ref, got_ref, fix_ref, send_ref):
    _, levels, rows, _ = own_ref.shape
    low_pair = lax.axis_index("tm") < 2
    for lev in range(levels):
        mine = jnp.where(low_pair, own_ref[0, lev], own_ref[2, lev])
        send_ref[lev * rows : (lev + 1) * rows] = mine + got_ref[lev]
    for n in range(4):
        start = levels * rows + n * levels
        send_ref[start : start + levels] = fix_ref[n]


def rest_body(own_ref, obs_ref, local_ref, other_ref):
    levels = own_ref.shape[1]
    low_pair = lax.axis_index("tm") < 2
    for lev in range(levels):
        local_ref[lev] = own_ref[0, lev]
        other_ref[lev] = jnp.where(low_pair, own_ref[2, lev], own_ref[1, lev])
    local_ref[levels] = jnp.zeros(local_ref.shape[1:], F32)
    for n in range(2):
        local_ref[levels, n : n + 1, 0:128] = lanes(obs_ref[n])


def terms_body(
    cross_ref, beyond_ref, own_ref, got_ref, rest_ref, other_ref, fix_ref, terms_ref, known_ref
):
    low_pair = lax.axis_index("tm") < 2
    levels = own_ref.shape[1]
    for lev in range(levels):
        cross, got = cross_ref[lev], got_ref[lev]
        local, residual = own_ref[0, lev], own_ref[2, lev]
        back = corrected(beyond_ref[lev], fixes(fix_ref, 0, lev))
        rest0, rest1 = rest_ref[lev], other_ref[lev]
        terms_ref[0, lev] = jnp.where(low_pair, rest0, residual)
        terms_ref[1, lev] = jnp.where(low_pair, local, residual) + got
        terms_ref[2, lev] = jnp.where(low_pair, residual - back, rest0 + cross)
        terms_ref[3, lev] = jnp.where(low_pair, rest1, local + rest1)
        known_ref[lev] = jnp.where(low_pair, local, residual + got)


def dots_body(terms_ref, got_ref, rest_ref, obs_ref, keep_ref, give_ref, sums_ref):
    _, levels, rows, cols = terms_ref.shape
    low_pair = lax.axis_index("tm") < 2
    numer, denom = jnp.zeros((8, 128), F32), jnp.zeros((8, 128), F32)

    def folded(x):
        total = None
        for r in range(0, rows, 8):
            part = lanes(x[r : r + 8])
            total = part if total is None else total + part
        return total

    for lev in range(levels):
        y0, one, z0, z1 = (terms_ref[n, lev] for n in range(4))
        late = []
        for n in range(4):
            at = levels * rows + n * levels + lev
            late.append(jnp.where(low_pair, 0.0, got_ref[at : at + 1]))
        z0 = corrected(z0, late)
        two = got_ref[lev * rows : (lev + 1) * rows] + z0
        three = two + z1
        numer = numer + folded(y0 * y0 + (one - y0) * one + z0 * two + z1 * three)
        denom = denom + folded(y0 * y0 + one * one + two * two + three * three)
        keep_ref[0, lev] = jnp.where(low_pair, one, three)
        keep_ref[1, lev] = jnp.where(low_pair, two, y0)
        give_ref[lev] = jnp.where(low_pair, three, two)
    for n, total in enumerate((numer, denom)):
        obs = lanes(obs_ref[n]) + rest_ref[levels, n : n + 1, 0:128]
        sums_ref[n : n + 1] = jnp.sum(total, axis=0, keepdims=True) + obs


def update_body(
    mult_ref, incr_ref, dual_ref, dir_ref, keep_ref, known_ref, got_ref, sums_ref,
    new_m_ref, new_i_ref, new_o_ref,
):
    position = lax.axis_index("tm")
    leads, low_pair = lax.rem(position, 2) == 1, position < 2
    total = jnp.sum(sums_ref[...], axis=1, keepdims=True)
    step = total[0:1] / total[1:2]
    for lev in range(mult_ref.shape[0]):
        known, got = known_ref[lev], got_ref[lev]
        model = jnp.where(leads, keep_ref[0, lev], jnp.where(low_pair, known, got))
        back = jnp.where(leads, keep_ref[1, lev], jnp.where(low_pair, got, known))
        new_m_ref[lev] = mult_ref[lev] + step * model
        new_i_ref[lev] = incr_ref[lev] - step * back
    new_o_ref[...] = dual_ref[...] + step * dir_ref[...]


def exchange(value, partner):
    groups, tiles, peers = (lax.axis_size(x) for x in ("groups", "tile", "tm"))
    pairs = []
    for g in range(groups):
        for t in range(tiles):
            for k in range(peers):
                to_g, to_t, to_k = partner(g, t, k)
                target = (to_g * tiles + to_t) * peers + to_k
                pairs.append(((g * tiles + t) * peers + k, target))
    return lax.ppermute(value, ("groups", "tile", "tm"), pairs)


def swap(value, axis, distance):
    return lax.ppermute(value, axis, [(i, i ^ distance) for i in range(lax.axis_size(axis))])


def aside(g, t, k):
    return (g ^ 1, t, k) if lax.axis_size("groups") % 2 == 0 else (g, t ^ 1, k)


def leaders(value, tile, tm):
    return exchange(
        value, lambda g, t, k: (g, t ^ tile, k ^ tm) if k % 2 else aside(g, t, k)
    )


def next_pair(g, t, k):
    if 0 < k < lax.axis_size("tm") - 1:
        return g, t, (k - 1 if k % 2 == 0 else k + 1)
    return aside(g, t, k)


def second_side(g, t, k):
    if 0 < t < lax.axis_size("tile") - 1:
        return g, (t - 1 if t % 2 == 0 else t + 1), k
    return g, t, k ^ 1


def shifted(value, steps):
    count = lax.axis_size("tm")
    pairs = [(i, i + steps) for i in range(count) if 0 <= i + steps < count]
    return lax.ppermute(value, "tm", pairs)


def scanned(value, direction):
    reach = 1
    while reach < lax.axis_size("tm"):
        value = value + shifted(value, direction * reach)
        reach *= 2
    return value


def reduced(value, axis):
    distance = 1
    while distance < lax.axis_size(axis):
        value = value + swap(value, axis, distance)
        distance *= 2
    return value


def near(*arrays):
    return [(x, "near") for x in arrays]


def shards(
    multiplier, increment, obs_dual, rhs_model, rhs_obs, model_err, obs_err,
    drift_east, drift_north, diffusion, obs_cell, obs_count,
):
    tiles, peers = lax.axis_size("tile"), lax.axis_size("tm")
    levels, rows, cols = multiplier.shape[1:]
    field = ((levels, rows, cols), "near")
    lines = lambda n: ((n, levels, cols), "near")

    inner = swap(multiplier[0], "tm", 1)
    arguments = [increment[0], drift_east[0], drift_north[0], diffusion[0], multiplier[0]]
    arguments += [rhs_model[0], model_err[0], obs_cell, obs_dual, rhs_obs, obs_err]
    count = len(arguments)
    *here, moved, high, low, edge = kernel_call(
        lambda *refs: begin_body(count, *refs),
        "begin",
        [(x, "far") for x in arguments],
        [(x.shape, "near", x.dtype) for x in arguments]
        + [field, lines(3), lines(3), lines(len(EDGE))],
        [pltpu.SemaphoreType.DMA((count + 4 * (PARTS - 1),))],
    )
    incr, *coeffs = here[:4]
    mult, rhs, err, cell, dual, want, var = here[4:]
    if peers == 4:
        later, wanted = inner, lambda: lax.rem(lax.axis_index("tm"), 2) == 0
    else:
        later = jnp.where(lax.axis_index("tm") % 2 == 0, inner, exchange(mult, next_pair))
        wanted = lambda: lax.axis_index("tm") < peers - 1
    first, second = kernel_call(
        lambda *refs: rims_body(wanted, *refs),
        "rims",
        near(edge, later, high, low),
        [lines(5), lines(5)],
    )
    got_first = swap(first, "tile", 1)
    got_second = exchange(second, second_side)
    valid = (lax.broadcasted_iota(jnp.int32, obs_cell.shape, 1) < obs_count).astype(F32)
    local, held = kernel_call(
        spread_body, "spread", near(incr, mult, rhs, err, cell, dual, valid), [field] * 2
    )
    fix = kernel_call(
        edges_body, "edges", near(first, second, got_first, got_second, edge), [lines(8)]
    )[0]
    if peers != 4:
        later = jnp.where(lax.axis_index("tm") == peers - 1, 0.0, later)
        back = kernel_call(adjoint_body, "adjoint", near(*coeffs, later), [field])[0]
        dir_obs, obs_sums = kernel_call(
            gather_body,
            "gather",
            near(incr, cell, dual, want, var, valid),
            [(obs_dual.shape, "near"), ((2, *obs_dual.shape), "near")],
        )
        return scan_path(
            multiplier, increment, obs_dual, local, moved, held, back, fix, dir_obs, obs_sums
        )
    cross = jnp.where(lax.axis_index("tm") < 2, moved, inner)
    got_cross = leaders(jnp.pad(cross, ((0, 1), (0, 0), (0, 0))), 0, 2)
    back = kernel_call(adjoint_body, "adjoint", near(*coeffs, inner), [field])[0]
    own, urgent = kernel_call(
        share_body,
        "share",
        near(local, moved, held, back, fix),
        [((3, levels, rows, cols), "near"), field],
    )
    got = swap(urgent, "tm", 1)
    dir_obs, obs_sums = kernel_call(
        gather_body,
        "gather",
        near(incr, cell, dual, want, var, valid),
        [(obs_dual.shape, "near"), ((2, *obs_dual.shape), "near")],
    )
    got, obs_sums = lax.optimization_barrier((got, obs_sums))
    send = kernel_call(
        sends_body, "sends", near(own, got, fix), [((levels * rows + 4 * levels, cols), "near")]
    )[0]
    send, own = lax.optimization_barrier((send, own))
    got_send = leaders(send, 0, 2)
    rest, other = kernel_call(
        rest_body, "rest", near(own, obs_sums), [((levels + 1, rows, cols), "near"), field]
    )
    got_rest, got_other = swap(rest, "tm", 1), swap(other, "tm", 1)
    late_first, late_second = kernel_call(
        late_rims_body, "late_rims", near(edge, got_cross), [lines(2), lines(2)], weight=WEIGHT
    )
    got_late_first = swap(late_first, "tile", 1)
    got_late_second = exchange(late_second, second_side)
    late_fix = kernel_call(
        late_edges_body,
        "late_edges",
        near(late_first, late_second, got_late_first, got_late_second)
        + near(got_first, got_second, edge),
        [lines(4)],
    )[0]
    beyond = kernel_call(adjoint_body, "beyond", near(*coeffs, got_cross), [field])[0]
    terms, known = kernel_call(
        terms_body,
        "terms",
        near(got_cross, beyond, own, got, got_rest, got_other, late_fix),
        [((4, levels, rows, cols), "near"), field],
    )
    pair = ((2, levels, rows, cols), "near")
    keep, give, sums = kernel_call(
        dots_body, "dots", near(terms, got_send, got_rest, obs_sums), [pair, field, ((2, 128), "near")]
    )
    total = sums + leaders(sums, 0, 2) + leaders(sums, 1, 0) + leaders(sums, 1, 2)
    distance = 2
    while distance < tiles:
        total = total + leaders(total, distance, 0)
        distance *= 2
    give, total = lax.optimization_barrier((give, total))
    got_dir = swap(give, "tm", 1)
    other = swap(total, "tm", 1)
    total = jnp.where(lax.axis_index("tm") % 2 == 1, total, other)
    new_m, new_i, new_o = kernel_call(
        update_body,
        "update",
        near(mult, incr, dual, dir_obs, keep, known, got_dir, total),
        [(mult.shape, "far"), (mult.shape, "far"), (obs_dual.shape, "far")],
    )
    return new_m[None], new_i[None], new_o


def scan_path(multiplier, increment, obs_dual, local, moved, held, back, fix, dir_obs, obs_sums):
    rows = local.shape[1]
    fix = jnp.moveaxis(fix, 0, 1)
    at = jnp.array([0, 1, rows - 2, rows - 1])
    moved = moved.at[:, at].add(fix[:, :4])
    res_incr = -(held - back.at[:, at].add(fix[:, 4:8]))
    res_model = local + shifted(moved, 1)
    dir_model, dir_incr = scanned(res_model, 1), scanned(res_incr, -1)
    numer = jnp.sum(res_model * dir_model) + jnp.sum(res_incr * dir_incr) + jnp.sum(obs_sums[0])
    denom = jnp.sum(dir_model**2) + jnp.sum(dir_incr**2) + jnp.sum(obs_sums[1])
    sums = reduced(reduced(jnp.stack([numer, denom]), "tm"), "tile")
    step = sums[0] / sums[1]
    return (
        multiplier + step * dir_model[None],
        increment + step * dir_incr[None],
        obs_dual + step * dir_obs,
    )


def solution(mesh):
    grid = P(("groups", "tm"), None, "tile", None)
    line = P(("groups", "tm"), "tile")
    return jax.shard_map(
        shards,
        mesh=mesh,
        in_specs=(grid, grid, line, grid, line, grid, line, grid, grid, grid, line, line),
        out_specs=(grid, grid, line),
        check_vma=False,
    )
```

```python
import jax
import jax.numpy as jnp
from jax import lax
from jax.experimental import pallas as pl
from jax.experimental.pallas import tpu as pltpu
from jax.sharding import PartitionSpec as P

F32 = jnp.float32
VMEM = pltpu.VMEM
GRANT = 24 * 1024 * 1024
WEIGHT = 2600000000
PARTS = 2


def kernel_call(body, name, inputs, outputs, scratch=(), weight=1):
    arrays, in_specs = [], []
    for array, home in inputs:
        if home == "far":
            in_specs.append(pl.BlockSpec(memory_space=pltpu.HBM))
            array = pltpu.with_memory_space_constraint(array, pltpu.HBM)
        else:
            in_specs.append(pl.BlockSpec(memory_space=VMEM))
            array = pltpu.with_memory_space_constraint(array, VMEM)
        arrays.append(array)
    out_shape, out_specs = [], []
    for shape, home, *dtype in outputs:
        dtype = dtype[0] if dtype else F32
        out_specs.append(pl.BlockSpec(memory_space=VMEM))
        out_shape.append(
            VMEM(shape, dtype) if home == "near" else jax.ShapeDtypeStruct(shape, dtype)
        )
    return pl.pallas_call(
        body,
        name=name,
        out_shape=out_shape,
        in_specs=in_specs,
        out_specs=out_specs,
        scratch_shapes=list(scratch),
        cost_estimate=pl.CostEstimate(flops=weight, bytes_accessed=1, transcendentals=0),
        compiler_params=pltpu.CompilerParams(vmem_limit_bytes=GRANT),
    )(*arrays)


def lanes(row):
    total = row[:, 0:128]
    for col in range(128, row.shape[1], 128):
        total = total + row[:, col : col + 128]
    return total


def iotas(shape):
    return (
        lax.broadcasted_iota(jnp.int32, shape, 0),
        lax.broadcasted_iota(jnp.int32, shape, 1),
    )


def up(field, axis):
    return pltpu.roll(field, field.shape[axis] - 1, axis)


def down(field, axis):
    return pltpu.roll(field, 1, axis)


def taps(a, b, c):
    i, y = iotas(a.shape)
    rows, cols = a.shape
    return (
        1.0 - 4.0 * c,
        jnp.where(i < rows - 1, c - a, 0.0),
        jnp.where(i > 0, c + a, 0.0),
        jnp.where(y < cols - 1, c - b, 0.0),
        jnp.where(y > 0, c + b, 0.0),
    )


def forward(state, coeffs):
    mid, east, west, north, south = coeffs
    return (
        mid * state
        + east * up(state, 0)
        + west * down(state, 0)
        + north * up(state, 1)
        + south * down(state, 1)
    )


def adjoint(state, coeffs):
    mid, east, west, north, south = coeffs
    return (
        mid * state
        + down(east * state, 0)
        + up(west * state, 0)
        + down(north * state, 1)
        + up(south * state, 1)
    )


EDGE = ("mid_low", "mid_high", "north_low", "north_high", "south_low", "south_high")
EDGE += ("west_low", "west_next", "east_high", "east_next", "east_low", "west_high")


def begin_body(count, *refs):
    sources, targets = refs[:count], refs[count : 2 * count]
    moved_ref, high_ref, low_ref, edge_ref, sems = refs[2 * count :]
    s_ref, a_ref, b_ref, c_ref = targets[:4]
    levels, rows, _ = s_ref.shape
    last = rows - 1
    cut = levels // PARTS
    parts = [
        [
            pltpu.make_async_copy(
                sources[n].at[pl.ds(part * cut, cut)],
                targets[n].at[pl.ds(part * cut, cut)],
                sems.at[part * 4 + n],
            )
            for n in range(4)
        ]
        for part in range(PARTS)
    ]
    rest = [
        pltpu.make_async_copy(sources[n], targets[n], sems.at[4 * (PARTS - 1) + n])
        for n in range(4, count)
    ]
    for copy in sum(parts, []) + rest:
        copy.start()
    for lev in range(levels):
        if lev % cut == 0:
            for copy in parts[lev // cut]:
                copy.wait()
        s, a, b, c = s_ref[lev], a_ref[lev], b_ref[lev], c_ref[lev]
        coeffs = taps(a, b, c)
        once = forward(s, coeffs)
        moved_ref[lev] = forward(once, coeffs)
        mid, east, west, north, south = coeffs
        at = pl.ds(lev, 1)
        open_east = c[last : last + 1] - a[last : last + 1]
        open_west = c[0:1] + a[0:1]
        high_ref[0, at] = s[last : last + 1]
        high_ref[1, at] = once[last : last + 1]
        high_ref[2, at] = open_east
        high_ref[3, at] = b[last : last + 1]
        high_ref[4, at] = c[last : last + 1]
        low_ref[0, at] = s[0:1]
        low_ref[1, at] = once[0:1]
        low_ref[2, at] = open_west
        low_ref[3, at] = b[0:1]
        low_ref[4, at] = c[0:1]
        rows_of = {
            "mid_low": mid[0:1],
            "mid_high": mid[last : last + 1],
            "north_low": north[0:1],
            "north_high": north[last : last + 1],
            "south_low": south[0:1],
            "south_high": south[last : last + 1],
            "west_low": open_west,
            "west_next": west[1:2],
            "east_high": open_east,
            "east_next": east[last - 1 : last],
            "east_low": east[0:1],
            "west_high": west[last : last + 1],
        }
        for n, key in enumerate(EDGE):
            edge_ref[n, at] = rows_of[key]
    for copy in rest:
        copy.wait()


def adjoint_body(a_ref, b_ref, c_ref, later_ref, back_ref):
    for lev in range(a_ref.shape[0]):
        coeffs = taps(a_ref[lev], b_ref[lev], c_ref[lev])
        back_ref[lev] = adjoint(adjoint(later_ref[lev], coeffs), coeffs)


def outer_products(k, later):
    def once(side, at, beside):
        mid, north, south = k["mid_" + side], k["north_" + side], k["south_" + side]
        return mid * at + beside + down(north * at, 1) + up(south * at, 1)

    west, east = k["west_low"], k["east_high"]
    return (
        (west * later[0], west * once("low", later[0], k["west_next"] * later[1])),
        (east * later[3], east * once("high", later[3], k["east_next"] * later[2])),
    )


def rims_body(four, edge_ref, later_ref, high_ref, low_ref, first_ref, second_ref):
    position, peers = lax.axis_index("tm"), lax.axis_size("tm")
    odd = lax.rem(lax.axis_index("tile"), 2)
    k = {key: edge_ref[n] for n, key in enumerate(EDGE)}
    levels, rows, _ = later_ref.shape
    later = [
        jnp.concatenate([later_ref[lev, row : row + 1] for lev in range(levels)], 0)
        for row in (0, 1, rows - 2, rows - 1)
    ]
    products = outer_products(k, later)
    zero = jnp.zeros(later[0].shape, F32)
    sent = []
    for ref, product, outer, inside, beside in (
        (low_ref, products[0], later[0], later[1], k["west_next"]),
        (high_ref, products[1], later[3], later[2], k["east_next"]),
    ):
        out = [ref[0], ref[1], ref[2], *product, zero]
        if four:
            second, final = position == 1, position == peers - 1
            out[0] = jnp.where(final, outer, out[0])
            out[1] = jnp.where(final, inside, out[1])
            out[3] = jnp.where(second, ref[3], out[3])
            out[4] = jnp.where(second, ref[4], out[4])
            out[5] = jnp.where(second, beside, zero)
        sent.append(out)
    for n, (low, high) in enumerate(zip(*sent)):
        first_ref[n] = jnp.where(odd == 0, high, low)
        second_ref[n] = jnp.where(odd == 0, low, high)


def sides(first, second):
    tile, tiles = lax.axis_index("tile"), lax.axis_size("tile")
    odd = lax.rem(tile, 2)
    below, above = jnp.where(odd == 0, second, first), jnp.where(odd == 0, first, second)
    return jnp.where(tile > 0, below, 0.0), jnp.where(tile < tiles - 1, above, 0.0)


def own_sides(first, second):
    odd = lax.rem(lax.axis_index("tile"), 2)
    return jnp.where(odd == 0, second, first), jnp.where(odd == 0, first, second)


def back_fix(k, product, stepped, own_product, toward):
    def across(x, side):
        mid, north, south = k["mid_" + side], k["north_" + side], k["south_" + side]
        return mid * x + down(north * x, 1) + up(south * x, 1)

    return (
        across(product[0], "low") + (stepped[0] + toward[0] * own_product[0]),
        k["east_low"] * product[0],
        k["west_high"] * product[1],
        across(product[1], "high") + (stepped[1] + toward[1] * own_product[1]),
    )


def edges_body(
    four, first_ref, second_ref, got_first_ref, got_second_ref, edge_ref, fix_ref, late_ref
):
    position, peers = lax.axis_index("tm"), lax.axis_size("tm")
    k = {key: edge_ref[n] for n, key in enumerate(EDGE)}
    state, stepped, toward, product, product_stepped = (
        sides(got_first_ref[n], got_second_ref[n]) for n in range(5)
    )
    own_state = own_sides(first_ref[0], second_ref[0])
    own_product = own_sides(first_ref[3], second_ref[3])
    wanted = lax.rem(position, 2) == 0 if four else position < peers - 1

    def along(x, side):
        mid, north, south = k["mid_" + side], k["north_" + side], k["south_" + side]
        return mid * x + north * up(x, 1) + south * down(x, 1)

    new_low, new_high = k["west_low"] * state[0], k["east_high"] * state[1]
    moved = (
        along(new_low, "low") + k["west_low"] * (stepped[0] + toward[0] * own_state[0]),
        k["west_next"] * new_low,
        k["east_next"] * new_high,
        along(new_high, "high") + k["east_high"] * (stepped[1] + toward[1] * own_state[1]),
    )
    back = back_fix(k, product, product_stepped, own_product, toward)
    beyond = (state[0], stepped[0], state[1], stepped[1])
    for n in range(4):
        fix_ref[n] = moved[n]
        fix_ref[4 + n] = jnp.where(wanted, back[n], 0.0)
        late_ref[n] = jnp.where(position < peers // 2, moved[n], beyond[n])


def late_body(rows, got_first_ref, got_second_ref, edge_ref, cross_ref, late_ref, fix_ref):
    k = {key: edge_ref[n] for n, key in enumerate(EDGE)}
    levels, cols = edge_ref.shape[1:]
    _, y = iotas((levels, cols))
    toward, drift, diffuse, beside = (
        sides(got_first_ref[n], got_second_ref[n]) for n in range(2, 6)
    )
    product, stepped, own = [], [], []
    for side in range(2):
        near_by, far_off = late_ref[2 * side], late_ref[2 * side + 1]
        b, c = drift[side], diffuse[side]
        north, south = jnp.where(y < cols - 1, c - b, 0.0), jnp.where(y > 0, c + b, 0.0)
        once = (1.0 - 4.0 * c) * near_by + beside[side] * far_off
        once = once + down(north * near_by, 1) + up(south * near_by, 1)
        product.append(toward[side] * near_by)
        stepped.append(toward[side] * once)
        row = side * (rows - 1)
        outer = [cross_ref[lev * rows + row : lev * rows + row + 1] for lev in range(levels)]
        own.append(k[("west_low", "east_high")[side]] * jnp.concatenate(outer, 0))
    for n, fix in enumerate(back_fix(k, product, stepped, own, toward)):
        fix_ref[n] = fix


def beyond_body(a_ref, b_ref, c_ref, cross_ref, back_ref):
    levels, rows, _ = a_ref.shape
    for lev in range(levels):
        coeffs = taps(a_ref[lev], b_ref[lev], c_ref[lev])
        cross = cross_ref[lev * rows : (lev + 1) * rows]
        back_ref[lev] = adjoint(adjoint(cross, coeffs), coeffs)


def thirds(x):
    one = x.astype(jnp.bfloat16)
    rest = x - one.astype(F32)
    two = rest.astype(jnp.bfloat16)
    return one, two, (rest - two.astype(F32)).astype(jnp.bfloat16)


def slot_masks(cell, lines, cols):
    slots = cell.shape[1]
    at_line = iotas((lines, slots))[0] == cell // cols
    at_col = iotas((cols, slots))[0] == lax.rem(cell, cols)
    return at_line, jnp.where(at_col, 1.0, 0.0).astype(jnp.bfloat16)


def spread_body(
    incr_ref, mult_ref, rhs_ref, err_ref, cell_ref, dual_ref, valid_ref, local_ref, held_ref
):
    levels, rows, cols = incr_ref.shape
    lines = levels * rows
    at_line, at_col = slot_masks(cell_ref[...], lines, cols)
    weights = thirds(jnp.where(at_line, valid_ref[...] * dual_ref[...], 0.0))
    spread = lax.dot_general(
        jnp.concatenate(weights, 0), at_col, (((1,), (1,)), ((), ())), preferred_element_type=F32
    )
    ht = spread[:lines] + spread[lines : 2 * lines] + spread[2 * lines :]
    mult = mult_ref[...]
    held_ref[...] = mult + ht.reshape(levels, rows, cols)
    local_ref[...] = rhs_ref[...] - (err_ref[...] * mult + incr_ref[...])


def gather_body(
    incr_ref, cell_ref, dual_ref, want_ref, var_ref, valid_ref, dir_ref, sums_ref
):
    levels, rows, cols = incr_ref.shape
    lines = levels * rows
    at_line, at_col = slot_masks(cell_ref[...], lines, cols)
    fields = thirds(incr_ref[...].reshape(lines, cols))
    picked = jnp.dot(jnp.concatenate(fields, 0), at_col, preferred_element_type=F32)
    picked = picked[:lines] + picked[lines : 2 * lines] + picked[2 * lines :]
    valid, var = valid_ref[...], var_ref[...]
    hx = jnp.sum(jnp.where(at_line, picked, 0.0), axis=0, keepdims=True) * valid
    res = valid * (want_ref[...] - (var * dual_ref[...] + hx))
    direction = res / var
    dir_ref[...] = direction
    sums_ref[0] = res * direction
    sums_ref[1] = direction * direction


def corrected(field, fix):
    rows = field.shape[0]
    i, _ = iotas(field.shape)
    for n, row in enumerate((0, 1, rows - 2, rows - 1)):
        field = field + jnp.where(i == row, fix[n], 0.0)
    return field


def fixes(ref, start, lev):
    return [ref[start + n, pl.ds(lev, 1)] for n in range(4)]


def minus(rows):
    return [-x for x in rows]


def share_body(local_ref, moved_ref, held_ref, back_ref, fix_ref, own_ref, urgent_ref):
    position = lax.axis_index("tm")
    first, low_pair = lax.rem(position, 2) == 0, position < 2
    for lev in range(local_ref.shape[0]):
        back = corrected(back_ref[lev], fixes(fix_ref, 4, lev))
        moved = corrected(moved_ref[lev], fixes(fix_ref, 0, lev))
        local = local_ref[lev]
        residual = held_ref[lev] - jnp.where(first, back, 0.0)
        own_ref[0, lev] = local
        own_ref[1, lev] = moved
        own_ref[2, lev] = residual
        urgent_ref[lev] = jnp.where(low_pair, local + moved, residual)


def sends_body(own_ref, got_ref, send_ref):
    low_pair = lax.axis_index("tm") < 2
    for lev in range(own_ref.shape[1]):
        mine = jnp.where(low_pair, own_ref[0, lev], own_ref[2, lev])
        send_ref[lev] = mine + got_ref[lev]


def rest_body(own_ref, obs_ref, *out_refs):
    levels = own_ref.shape[1]
    low_pair = lax.axis_index("tm") < 2
    blocks = [(ref, n) for ref in out_refs for n in range(ref.shape[0])]
    for lev in range(levels):
        ref, n = blocks[lev]
        ref[n] = own_ref[0, lev]
        ref, n = blocks[levels + lev]
        ref[n] = jnp.where(low_pair, own_ref[2, lev], own_ref[1, lev])
    ref, n = blocks[2 * levels]
    ref[n] = jnp.zeros(ref.shape[1:], F32)
    for i in range(2):
        ref[n, i : i + 1, 0:128] = lanes(obs_ref[i])


def terms_body(cross_ref, late_ref, beyond_ref, own_ref, got_ref, fix_ref, *refs):
    low_pair = lax.axis_index("tm") < 2
    _, levels, rows, _ = own_ref.shape
    *rest_refs, terms_ref, known_ref = refs
    blocks = [(ref, n) for ref in rest_refs for n in range(ref.shape[0])]
    for lev in range(levels):
        got = got_ref[lev]
        local, residual = own_ref[0, lev], own_ref[2, lev]
        back = corrected(beyond_ref[lev], fixes(fix_ref, 0, lev))
        moved = corrected(cross_ref[lev * rows : (lev + 1) * rows], fixes(late_ref, 0, lev))
        rest0, rest1 = (ref[n] for ref, n in (blocks[lev], blocks[levels + lev]))
        terms_ref[0, lev] = jnp.where(low_pair, rest0, residual)
        terms_ref[1, lev] = jnp.where(low_pair, local, residual) + got
        terms_ref[2, lev] = jnp.where(low_pair, residual - back, rest0 + moved)
        terms_ref[3, lev] = jnp.where(low_pair, rest1, local + rest1)
        known_ref[lev] = jnp.where(low_pair, local, residual + got)


def dots_body(terms_ref, got_ref, rest_ref, obs_ref, keep_ref, give_ref, sums_ref):
    _, levels, rows, cols = terms_ref.shape
    low_pair = lax.axis_index("tm") < 2
    numer, denom = jnp.zeros((8, 128), F32), jnp.zeros((8, 128), F32)

    def folded(x):
        total = None
        for r in range(0, rows, 8):
            part = lanes(x[r : r + 8])
            total = part if total is None else total + part
        return total

    for lev in range(levels):
        y0, one, z0, z1 = (terms_ref[n, lev] for n in range(4))
        two = got_ref[lev] + z0
        three = two + z1
        numer = numer + folded(y0 * y0 + (one - y0) * one + z0 * two + z1 * three)
        denom = denom + folded(y0 * y0 + one * one + two * two + three * three)
        keep_ref[0, lev] = jnp.where(low_pair, one, three)
        keep_ref[1, lev] = jnp.where(low_pair, two, y0)
        give_ref[lev] = jnp.where(low_pair, three, two)
    for n, total in enumerate((numer, denom)):
        obs = lanes(obs_ref[n]) + rest_ref[rest_ref.shape[0] - 1, n : n + 1, 0:128]
        sums_ref[n : n + 1] = jnp.sum(total, axis=0, keepdims=True) + obs


def update_body(
    mult_ref, incr_ref, dual_ref, dir_ref, keep_ref, known_ref, got_ref, sums_ref,
    new_m_ref, new_i_ref, new_o_ref,
):
    position = lax.axis_index("tm")
    leads, low_pair = lax.rem(position, 2) == 1, position < 2
    total = jnp.sum(sums_ref[...], axis=1, keepdims=True)
    step = total[0:1] / total[1:2]
    for lev in range(mult_ref.shape[0]):
        known, got = known_ref[lev], got_ref[lev]
        model = jnp.where(leads, keep_ref[0, lev], jnp.where(low_pair, known, got))
        back = jnp.where(leads, keep_ref[1, lev], jnp.where(low_pair, got, known))
        new_m_ref[lev] = mult_ref[lev] + step * model
        new_i_ref[lev] = incr_ref[lev] - step * back
    new_o_ref[...] = dual_ref[...] + step * dir_ref[...]


def exchange(value, partner):
    groups, tiles, peers = (lax.axis_size(x) for x in ("groups", "tile", "tm"))
    pairs = []
    for g in range(groups):
        for t in range(tiles):
            for k in range(peers):
                to_g, to_t, to_k = partner(g, t, k)
                target = (to_g * tiles + to_t) * peers + to_k
                pairs.append(((g * tiles + t) * peers + k, target))
    return lax.ppermute(value, ("groups", "tile", "tm"), pairs)


def swap(value, axis, distance):
    return lax.ppermute(value, axis, [(i, i ^ distance) for i in range(lax.axis_size(axis))])


def aside(g, t, k):
    return (g ^ 1, t, k) if lax.axis_size("groups") % 2 == 0 else (g, t ^ 1, k)


def leaders(value, tile, tm):
    return exchange(
        value, lambda g, t, k: (g, t ^ tile, k ^ tm) if k % 2 else aside(g, t, k)
    )


def next_pair(g, t, k):
    if 0 < k < lax.axis_size("tm") - 1:
        return g, t, (k - 1 if k % 2 == 0 else k + 1)
    return aside(g, t, k)


def second_side(g, t, k):
    if 0 < t < lax.axis_size("tile") - 1:
        return g, (t - 1 if t % 2 == 0 else t + 1), k
    return g, t, k ^ 1


def shifted(value, steps):
    count = lax.axis_size("tm")
    pairs = [(i, i + steps) for i in range(count) if 0 <= i + steps < count]
    return lax.ppermute(value, "tm", pairs)


def scanned(value, direction):
    reach = 1
    while reach < lax.axis_size("tm"):
        value = value + shifted(value, direction * reach)
        reach *= 2
    return value


def reduced(value, axis):
    distance = 1
    while distance < lax.axis_size(axis):
        value = value + swap(value, axis, distance)
        distance *= 2
    return value


def near(*arrays):
    return [(x, "near") for x in arrays]


def shards(
    multiplier, increment, obs_dual, rhs_model, rhs_obs, model_err, obs_err,
    drift_east, drift_north, diffusion, obs_cell, obs_count,
):
    tiles, peers = lax.axis_size("tile"), lax.axis_size("tm")
    levels, rows, cols = multiplier.shape[1:]
    field = ((levels, rows, cols), "near")
    lines = lambda n: ((n, levels, cols), "near")

    inner = swap(multiplier[0], "tm", 1)
    arguments = [increment[0], drift_east[0], drift_north[0], diffusion[0], multiplier[0]]
    arguments += [rhs_model[0], model_err[0], obs_cell, obs_dual, rhs_obs, obs_err]
    count = len(arguments)
    *here, moved, high, low, edge = kernel_call(
        lambda *refs: begin_body(count, *refs),
        "begin",
        [(x, "far") for x in arguments],
        [(x.shape, "near", x.dtype) for x in arguments]
        + [field, lines(5), lines(5), lines(len(EDGE))],
        [pltpu.SemaphoreType.DMA((count + 4 * (PARTS - 1),))],
    )
    incr, *coeffs = here[:4]
    mult, rhs, err, cell, dual, want, var = here[4:]
    four = peers == 4
    if four:
        later = inner
    else:
        later = jnp.where(lax.axis_index("tm") % 2 == 0, inner, exchange(mult, next_pair))
    first, second = kernel_call(
        lambda *refs: rims_body(four, *refs),
        "rims",
        near(edge, later, high, low),
        [lines(6), lines(6)],
    )
    got_first = swap(first, "tile", 1)
    got_second = exchange(second, second_side)
    valid = (lax.broadcasted_iota(jnp.int32, obs_cell.shape, 1) < obs_count).astype(F32)
    local, held = kernel_call(
        spread_body, "spread", near(incr, mult, rhs, err, cell, dual, valid), [field] * 2
    )
    fix, late = kernel_call(
        lambda *refs: edges_body(four, *refs),
        "edges",
        near(first, second, got_first, got_second, edge),
        [lines(8), lines(4)],
    )
    if not four:
        later = jnp.where(lax.axis_index("tm") == peers - 1, 0.0, later)
        back = kernel_call(adjoint_body, "adjoint", near(*coeffs, later), [field])[0]
        dir_obs, obs_sums = kernel_call(
            gather_body,
            "gather",
            near(incr, cell, dual, want, var, valid),
            [(obs_dual.shape, "near"), ((2, *obs_dual.shape), "near")],
        )
        return scan_path(
            multiplier, increment, obs_dual, local, moved, held, back, fix, dir_obs, obs_sums
        )
    cross = jnp.where(lax.axis_index("tm") < 2, moved, inner).reshape(levels * rows, cols)
    got_cross = leaders(jnp.pad(cross, ((0, rows), (0, 0))), 0, 2)
    got_late = leaders(late, 0, 2)
    back = kernel_call(adjoint_body, "adjoint", near(*coeffs, inner), [field])[0]
    own, urgent = kernel_call(
        share_body,
        "share",
        near(local, moved, held, back, fix),
        [((3, levels, rows, cols), "near"), field],
    )
    got = swap(urgent, "tm", 1)
    send = kernel_call(sends_body, "sends", near(own, got), [field])[0]
    send, own, cell = lax.optimization_barrier((send, own, cell))
    got_send = leaders(send, 0, 2)
    dir_obs, obs_sums = kernel_call(
        gather_body,
        "gather",
        near(incr, cell, dual, want, var, valid),
        [(obs_dual.shape, "near"), ((2, *obs_dual.shape), "near")],
    )
    parts = [-(-(2 * levels + 1) // 3)] * 2
    parts.append(2 * levels + 1 - sum(parts))
    rest = kernel_call(
        rest_body, "rest", near(own, obs_sums), [((n, rows, cols), "near") for n in parts]
    )
    got_rest = [swap(x, "tm", 1) for x in rest]
    late_fix = kernel_call(
        lambda *refs: late_body(rows, *refs),
        "late",
        near(got_first, got_second, edge, got_cross, got_late),
        [lines(4)],
        weight=WEIGHT,
    )[0]
    beyond = kernel_call(beyond_body, "beyond", near(*coeffs, got_cross), [field])[0]
    terms, known = kernel_call(
        terms_body,
        "terms",
        near(got_cross, got_late, beyond, own, got, late_fix, *got_rest),
        [((4, levels, rows, cols), "near"), field],
    )
    pair = ((2, levels, rows, cols), "near")
    keep, give, sums = kernel_call(
        dots_body, "dots", near(terms, got_send, got_rest[-1], obs_sums), [pair, field, ((2, 128), "near")]
    )
    total = sums + leaders(sums, 0, 2) + leaders(sums, 1, 0) + leaders(sums, 1, 2)
    distance = 2
    while distance < tiles:
        total = total + leaders(total, distance, 0)
        distance *= 2
    give, total = lax.optimization_barrier((give, total))
    got_dir = swap(give, "tm", 1)
    other = swap(total, "tm", 1)
    total = jnp.where(lax.axis_index("tm") % 2 == 1, total, other)
    new_m, new_i, new_o = kernel_call(
        update_body,
        "update",
        near(mult, incr, dual, dir_obs, keep, known, got_dir, total),
        [(mult.shape, "far"), (mult.shape, "far"), (obs_dual.shape, "far")],
    )
    return new_m[None], new_i[None], new_o


def scan_path(multiplier, increment, obs_dual, local, moved, held, back, fix, dir_obs, obs_sums):
    rows = local.shape[1]
    fix = jnp.moveaxis(fix, 0, 1)
    at = jnp.array([0, 1, rows - 2, rows - 1])
    moved = moved.at[:, at].add(fix[:, :4])
    res_incr = -(held - back.at[:, at].add(fix[:, 4:8]))
    res_model = local + shifted(moved, 1)
    dir_model, dir_incr = scanned(res_model, 1), scanned(res_incr, -1)
    numer = jnp.sum(res_model * dir_model) + jnp.sum(res_incr * dir_incr) + jnp.sum(obs_sums[0])
    denom = jnp.sum(dir_model**2) + jnp.sum(dir_incr**2) + jnp.sum(obs_sums[1])
    sums = reduced(reduced(jnp.stack([numer, denom]), "tm"), "tile")
    step = sums[0] / sums[1]
    return (
        multiplier + step * dir_model[None],
        increment + step * dir_incr[None],
        obs_dual + step * dir_obs,
    )


def solution(mesh):
    grid = P(("groups", "tm"), None, "tile", None)
    line = P(("groups", "tm"), "tile")
    return jax.shard_map(
        shards,
        mesh=mesh,
        in_specs=(grid, grid, line, grid, line, grid, line, grid, grid, grid, line, line),
        out_specs=(grid, grid, line),
        check_vma=False,
    )
```

```python
import jax
import jax.numpy as jnp
from jax import lax
from jax.experimental import pallas as pl
from jax.experimental.pallas import tpu as pltpu
from jax.sharding import PartitionSpec as P

F32 = jnp.float32
VMEM = pltpu.VMEM
GRANT = 24 * 1024 * 1024
WEIGHT = 2600000000
PARTS = 2


def kernel_call(body, name, inputs, outputs, scratch=(), weight=1):
    arrays, in_specs = [], []
    for array, home in inputs:
        if home == "far":
            in_specs.append(pl.BlockSpec(memory_space=pltpu.HBM))
            array = pltpu.with_memory_space_constraint(array, pltpu.HBM)
        else:
            in_specs.append(pl.BlockSpec(memory_space=VMEM))
            array = pltpu.with_memory_space_constraint(array, VMEM)
        arrays.append(array)
    out_shape, out_specs = [], []
    for shape, home, *dtype in outputs:
        dtype = dtype[0] if dtype else F32
        out_specs.append(pl.BlockSpec(memory_space=VMEM))
        out_shape.append(
            VMEM(shape, dtype) if home == "near" else jax.ShapeDtypeStruct(shape, dtype)
        )
    return pl.pallas_call(
        body,
        name=name,
        out_shape=out_shape,
        in_specs=in_specs,
        out_specs=out_specs,
        scratch_shapes=list(scratch),
        cost_estimate=pl.CostEstimate(flops=weight, bytes_accessed=1, transcendentals=0),
        compiler_params=pltpu.CompilerParams(vmem_limit_bytes=GRANT),
    )(*arrays)


def lanes(row):
    total = row[:, 0:128]
    for col in range(128, row.shape[1], 128):
        total = total + row[:, col : col + 128]
    return total


def iotas(shape):
    return (
        lax.broadcasted_iota(jnp.int32, shape, 0),
        lax.broadcasted_iota(jnp.int32, shape, 1),
    )


def up(field, axis):
    return pltpu.roll(field, field.shape[axis] - 1, axis)


def down(field, axis):
    return pltpu.roll(field, 1, axis)


def taps(a, b, c):
    i, y = iotas(a.shape)
    rows, cols = a.shape
    return (
        1.0 - 4.0 * c,
        jnp.where(i < rows - 1, c - a, 0.0),
        jnp.where(i > 0, c + a, 0.0),
        jnp.where(y < cols - 1, c - b, 0.0),
        jnp.where(y > 0, c + b, 0.0),
    )


def forward(state, coeffs):
    mid, east, west, north, south = coeffs
    return (
        mid * state
        + east * up(state, 0)
        + west * down(state, 0)
        + north * up(state, 1)
        + south * down(state, 1)
    )


def adjoint(state, coeffs):
    mid, east, west, north, south = coeffs
    return (
        mid * state
        + down(east * state, 0)
        + up(west * state, 0)
        + down(north * state, 1)
        + up(south * state, 1)
    )


EDGE = ("mid_low", "mid_high", "north_low", "north_high", "south_low", "south_high")
EDGE += ("west_low", "west_next", "east_high", "east_next", "east_low", "west_high")


def begin_body(count, *refs):
    sources, targets = refs[:count], refs[count : 2 * count]
    moved_ref, high_ref, low_ref, edge_ref, sems = refs[2 * count :]
    s_ref, a_ref, b_ref, c_ref = targets[:4]
    levels, rows, _ = s_ref.shape
    last = rows - 1
    cut = levels // PARTS
    parts = [
        [
            pltpu.make_async_copy(
                sources[n].at[pl.ds(part * cut, cut)],
                targets[n].at[pl.ds(part * cut, cut)],
                sems.at[part * 4 + n],
            )
            for n in range(4)
        ]
        for part in range(PARTS)
    ]
    rest = [
        pltpu.make_async_copy(sources[n], targets[n], sems.at[4 * (PARTS - 1) + n])
        for n in range(4, count)
    ]
    for copy in sum(parts, []) + rest:
        copy.start()
    for lev in range(levels):
        if lev % cut == 0:
            for copy in parts[lev // cut]:
                copy.wait()
        s, a, b, c = s_ref[lev], a_ref[lev], b_ref[lev], c_ref[lev]
        coeffs = taps(a, b, c)
        once = forward(s, coeffs)
        moved_ref[lev] = forward(once, coeffs)
        mid, east, west, north, south = coeffs
        at = pl.ds(lev, 1)
        open_east = c[last : last + 1] - a[last : last + 1]
        open_west = c[0:1] + a[0:1]
        high_ref[0, at] = s[last : last + 1]
        high_ref[1, at] = once[last : last + 1]
        high_ref[2, at] = open_east
        high_ref[3, at] = b[last : last + 1]
        high_ref[4, at] = c[last : last + 1]
        low_ref[0, at] = s[0:1]
        low_ref[1, at] = once[0:1]
        low_ref[2, at] = open_west
        low_ref[3, at] = b[0:1]
        low_ref[4, at] = c[0:1]
        rows_of = {
            "mid_low": mid[0:1],
            "mid_high": mid[last : last + 1],
            "north_low": north[0:1],
            "north_high": north[last : last + 1],
            "south_low": south[0:1],
            "south_high": south[last : last + 1],
            "west_low": open_west,
            "west_next": west[1:2],
            "east_high": open_east,
            "east_next": east[last - 1 : last],
            "east_low": east[0:1],
            "west_high": west[last : last + 1],
        }
        for n, key in enumerate(EDGE):
            edge_ref[n, at] = rows_of[key]
    for copy in rest:
        copy.wait()


def adjoint_body(a_ref, b_ref, c_ref, later_ref, back_ref):
    for lev in range(a_ref.shape[0]):
        coeffs = taps(a_ref[lev], b_ref[lev], c_ref[lev])
        back_ref[lev] = adjoint(adjoint(later_ref[lev], coeffs), coeffs)


def outer_products(k, later):
    def once(side, at, beside):
        mid, north, south = k["mid_" + side], k["north_" + side], k["south_" + side]
        return mid * at + beside + down(north * at, 1) + up(south * at, 1)

    west, east = k["west_low"], k["east_high"]
    return (
        (west * later[0], west * once("low", later[0], k["west_next"] * later[1])),
        (east * later[3], east * once("high", later[3], k["east_next"] * later[2])),
    )


def rims_body(four, edge_ref, later_ref, high_ref, low_ref, first_ref, second_ref):
    position, peers = lax.axis_index("tm"), lax.axis_size("tm")
    odd = lax.rem(lax.axis_index("tile"), 2)
    k = {key: edge_ref[n] for n, key in enumerate(EDGE)}
    levels, rows, _ = later_ref.shape
    later = [
        jnp.concatenate([later_ref[lev, row : row + 1] for lev in range(levels)], 0)
        for row in (0, 1, rows - 2, rows - 1)
    ]
    products = outer_products(k, later)
    zero = jnp.zeros(later[0].shape, F32)
    sent = []
    for ref, product, outer, inside, beside in (
        (low_ref, products[0], later[0], later[1], k["west_next"]),
        (high_ref, products[1], later[3], later[2], k["east_next"]),
    ):
        out = [ref[0], ref[1], ref[2], *product, zero]
        if four:
            second, final = position == 1, position == peers - 1
            out[0] = jnp.where(final, outer, out[0])
            out[1] = jnp.where(final, inside, out[1])
            out[3] = jnp.where(second, ref[3], out[3])
            out[4] = jnp.where(second, ref[4], out[4])
            out[5] = jnp.where(second, beside, zero)
        sent.append(out)
    for n, (low, high) in enumerate(zip(*sent)):
        first_ref[n] = jnp.where(odd == 0, high, low)
        second_ref[n] = jnp.where(odd == 0, low, high)


def sides(first, second):
    tile, tiles = lax.axis_index("tile"), lax.axis_size("tile")
    odd = lax.rem(tile, 2)
    below, above = jnp.where(odd == 0, second, first), jnp.where(odd == 0, first, second)
    return jnp.where(tile > 0, below, 0.0), jnp.where(tile < tiles - 1, above, 0.0)


def own_sides(first, second):
    odd = lax.rem(lax.axis_index("tile"), 2)
    return jnp.where(odd == 0, second, first), jnp.where(odd == 0, first, second)


def back_fix(k, product, stepped, own_product, toward):
    def across(x, side):
        mid, north, south = k["mid_" + side], k["north_" + side], k["south_" + side]
        return mid * x + down(north * x, 1) + up(south * x, 1)

    return (
        across(product[0], "low") + (stepped[0] + toward[0] * own_product[0]),
        k["east_low"] * product[0],
        k["west_high"] * product[1],
        across(product[1], "high") + (stepped[1] + toward[1] * own_product[1]),
    )


def edges_of(first_ref, second_ref, got_first_ref, got_second_ref, edge_ref):
    k = {key: edge_ref[n] for n, key in enumerate(EDGE)}
    state, stepped, toward, product, product_stepped = (
        sides(got_first_ref[n], got_second_ref[n]) for n in range(5)
    )
    own_state = own_sides(first_ref[0], second_ref[0])
    own_product = own_sides(first_ref[3], second_ref[3])

    def along(x, side):
        mid, north, south = k["mid_" + side], k["north_" + side], k["south_" + side]
        return mid * x + north * up(x, 1) + south * down(x, 1)

    new_low, new_high = k["west_low"] * state[0], k["east_high"] * state[1]
    moved = (
        along(new_low, "low") + k["west_low"] * (stepped[0] + toward[0] * own_state[0]),
        k["west_next"] * new_low,
        k["east_next"] * new_high,
        along(new_high, "high") + k["east_high"] * (stepped[1] + toward[1] * own_state[1]),
    )
    back = back_fix(k, product, product_stepped, own_product, toward)
    return moved, back, (state[0], stepped[0], state[1], stepped[1])


def edges_body(*refs):
    *in_refs, fix_ref = refs
    moved, back, _ = edges_of(*in_refs)
    wanted = lax.axis_index("tm") < lax.axis_size("tm") - 1
    for n in range(4):
        fix_ref[n] = moved[n]
        fix_ref[4 + n] = jnp.where(wanted, back[n], 0.0)


def late_body(rows, got_first_ref, got_second_ref, edge_ref, cross_ref, late_ref, fix_ref):
    k = {key: edge_ref[n] for n, key in enumerate(EDGE)}
    levels, cols = edge_ref.shape[1:]
    _, y = iotas((levels, cols))
    toward, drift, diffuse, beside = (
        sides(got_first_ref[n], got_second_ref[n]) for n in range(2, 6)
    )
    product, stepped, own = [], [], []
    for side in range(2):
        near_by, far_off = late_ref[2 * side], late_ref[2 * side + 1]
        b, c = drift[side], diffuse[side]
        north, south = jnp.where(y < cols - 1, c - b, 0.0), jnp.where(y > 0, c + b, 0.0)
        once = (1.0 - 4.0 * c) * near_by + beside[side] * far_off
        once = once + down(north * near_by, 1) + up(south * near_by, 1)
        product.append(toward[side] * near_by)
        stepped.append(toward[side] * once)
        row = side * (rows - 1)
        outer = [cross_ref[lev * rows + row : lev * rows + row + 1] for lev in range(levels)]
        own.append(k[("west_low", "east_high")[side]] * jnp.concatenate(outer, 0))
    for n, fix in enumerate(back_fix(k, product, stepped, own, toward)):
        fix_ref[n] = fix


def beyond_body(a_ref, b_ref, c_ref, cross_ref, back_ref):
    levels, rows, _ = a_ref.shape
    for lev in range(levels):
        coeffs = taps(a_ref[lev], b_ref[lev], c_ref[lev])
        cross = cross_ref[lev * rows : (lev + 1) * rows]
        back_ref[lev] = adjoint(adjoint(cross, coeffs), coeffs)


def thirds(x):
    one = x.astype(jnp.bfloat16)
    rest = x - one.astype(F32)
    two = rest.astype(jnp.bfloat16)
    return one, two, (rest - two.astype(F32)).astype(jnp.bfloat16)


def slot_masks(cell, lines, cols):
    slots = cell.shape[1]
    at_line = iotas((lines, slots))[0] == cell // cols
    at_col = iotas((cols, slots))[0] == lax.rem(cell, cols)
    return at_line, jnp.where(at_col, 1.0, 0.0).astype(jnp.bfloat16)


def spread_body(
    incr_ref, mult_ref, rhs_ref, err_ref, cell_ref, dual_ref, valid_ref, local_ref, held_ref
):
    levels, rows, cols = incr_ref.shape
    lines = levels * rows
    at_line, at_col = slot_masks(cell_ref[...], lines, cols)
    weights = thirds(jnp.where(at_line, valid_ref[...] * dual_ref[...], 0.0))
    spread = lax.dot_general(
        jnp.concatenate(weights, 0), at_col, (((1,), (1,)), ((), ())), preferred_element_type=F32
    )
    ht = spread[:lines] + spread[lines : 2 * lines] + spread[2 * lines :]
    mult = mult_ref[...]
    held_ref[...] = mult + ht.reshape(levels, rows, cols)
    local_ref[...] = rhs_ref[...] - (err_ref[...] * mult + incr_ref[...])


def gather_body(
    incr_ref, cell_ref, dual_ref, want_ref, var_ref, valid_ref, dir_ref, sums_ref
):
    levels, rows, cols = incr_ref.shape
    lines = levels * rows
    at_line, at_col = slot_masks(cell_ref[...], lines, cols)
    fields = thirds(incr_ref[...].reshape(lines, cols))
    picked = jnp.dot(jnp.concatenate(fields, 0), at_col, preferred_element_type=F32)
    picked = picked[:lines] + picked[lines : 2 * lines] + picked[2 * lines :]
    valid, var = valid_ref[...], var_ref[...]
    hx = jnp.sum(jnp.where(at_line, picked, 0.0), axis=0, keepdims=True) * valid
    res = valid * (want_ref[...] - (var * dual_ref[...] + hx))
    direction = res / var
    dir_ref[...] = direction
    sums_ref[0] = res * direction
    sums_ref[1] = direction * direction


def corrected(field, fix):
    rows = field.shape[0]
    i, _ = iotas(field.shape)
    for n, row in enumerate((0, 1, rows - 2, rows - 1)):
        field = field + jnp.where(i == row, fix[n], 0.0)
    return field


def fixes(ref, start, lev):
    return [ref[start + n, pl.ds(lev, 1)] for n in range(4)]


def minus(rows):
    return [-x for x in rows]


def share_body(
    first_ref, second_ref, got_first_ref, got_second_ref, edge_ref,
    local_ref, moved_ref, held_ref, back_ref, own_ref, urgent_ref, late_ref,
):
    position = lax.axis_index("tm")
    first, low_pair = lax.rem(position, 2) == 0, position < 2
    fix_moved, fix_back, beyond = edges_of(
        first_ref, second_ref, got_first_ref, got_second_ref, edge_ref
    )
    for n in range(4):
        late_ref[n] = jnp.where(low_pair, fix_moved[n], beyond[n])
    for lev in range(local_ref.shape[0]):
        back = corrected(back_ref[lev], [x[lev : lev + 1] for x in fix_back])
        moved = corrected(moved_ref[lev], [x[lev : lev + 1] for x in fix_moved])
        local = local_ref[lev]
        residual = held_ref[lev] - jnp.where(first, back, 0.0)
        own_ref[0, lev] = local
        own_ref[1, lev] = moved
        own_ref[2, lev] = residual
        urgent_ref[lev] = jnp.where(low_pair, local + moved, residual)


def sends_body(own_ref, got_ref, send_ref):
    low_pair = lax.axis_index("tm") < 2
    for lev in range(own_ref.shape[1]):
        mine = jnp.where(low_pair, own_ref[0, lev], own_ref[2, lev])
        send_ref[lev] = mine + got_ref[lev]


def rest_body(own_ref, obs_ref, *out_refs):
    levels = own_ref.shape[1]
    low_pair = lax.axis_index("tm") < 2
    blocks = [(ref, n) for ref in out_refs for n in range(ref.shape[0])]
    for lev in range(levels):
        ref, n = blocks[lev]
        ref[n] = own_ref[0, lev]
        ref, n = blocks[levels + lev]
        ref[n] = jnp.where(low_pair, own_ref[2, lev], own_ref[1, lev])
    ref, n = blocks[2 * levels]
    ref[n] = jnp.zeros(ref.shape[1:], F32)
    for i in range(2):
        ref[n, i : i + 1, 0:128] = lanes(obs_ref[i])


def terms_body(cross_ref, late_ref, beyond_ref, own_ref, got_ref, fix_ref, *refs):
    low_pair = lax.axis_index("tm") < 2
    _, levels, rows, _ = own_ref.shape
    *rest_refs, terms_ref, known_ref = refs
    blocks = [(ref, n) for ref in rest_refs for n in range(ref.shape[0])]
    for lev in range(levels):
        got = got_ref[lev]
        local, residual = own_ref[0, lev], own_ref[2, lev]
        back = corrected(beyond_ref[lev], fixes(fix_ref, 0, lev))
        moved = corrected(cross_ref[lev * rows : (lev + 1) * rows], fixes(late_ref, 0, lev))
        rest0, rest1 = (ref[n] for ref, n in (blocks[lev], blocks[levels + lev]))
        terms_ref[0, lev] = jnp.where(low_pair, rest0, residual)
        terms_ref[1, lev] = jnp.where(low_pair, local, residual) + got
        terms_ref[2, lev] = jnp.where(low_pair, residual - back, rest0 + moved)
        terms_ref[3, lev] = jnp.where(low_pair, rest1, local + rest1)
        known_ref[lev] = jnp.where(low_pair, local, residual + got)


def dots_body(terms_ref, got_ref, rest_ref, obs_ref, keep_ref, give_ref, sums_ref):
    _, levels, rows, cols = terms_ref.shape
    low_pair = lax.axis_index("tm") < 2
    numer, denom = jnp.zeros((8, 128), F32), jnp.zeros((8, 128), F32)

    def folded(x):
        total = None
        for r in range(0, rows, 8):
            part = lanes(x[r : r + 8])
            total = part if total is None else total + part
        return total

    for lev in range(levels):
        y0, one, z0, z1 = (terms_ref[n, lev] for n in range(4))
        two = got_ref[lev] + z0
        three = two + z1
        numer = numer + folded(y0 * y0 + (one - y0) * one + z0 * two + z1 * three)
        denom = denom + folded(y0 * y0 + one * one + two * two + three * three)
        keep_ref[0, lev] = jnp.where(low_pair, one, three)
        keep_ref[1, lev] = jnp.where(low_pair, two, y0)
        give_ref[lev] = jnp.where(low_pair, three, two)
    for n, total in enumerate((numer, denom)):
        obs = lanes(obs_ref[n]) + rest_ref[rest_ref.shape[0] - 1, n : n + 1, 0:128]
        sums_ref[n : n + 1] = jnp.sum(total, axis=0, keepdims=True) + obs


def update_body(
    mult_ref, incr_ref, dual_ref, dir_ref, keep_ref, known_ref, got_ref, sums_ref,
    new_m_ref, new_i_ref, new_o_ref,
):
    position = lax.axis_index("tm")
    leads, low_pair = lax.rem(position, 2) == 1, position < 2
    total = jnp.sum(sums_ref[...], axis=1, keepdims=True)
    step = total[0:1] / total[1:2]
    for lev in range(mult_ref.shape[0]):
        known, got = known_ref[lev], got_ref[lev]
        model = jnp.where(leads, keep_ref[0, lev], jnp.where(low_pair, known, got))
        back = jnp.where(leads, keep_ref[1, lev], jnp.where(low_pair, got, known))
        new_m_ref[lev] = mult_ref[lev] + step * model
        new_i_ref[lev] = incr_ref[lev] - step * back
    new_o_ref[...] = dual_ref[...] + step * dir_ref[...]


def exchange(value, partner):
    groups, tiles, peers = (lax.axis_size(x) for x in ("groups", "tile", "tm"))
    pairs = []
    for g in range(groups):
        for t in range(tiles):
            for k in range(peers):
                to_g, to_t, to_k = partner(g, t, k)
                target = (to_g * tiles + to_t) * peers + to_k
                pairs.append(((g * tiles + t) * peers + k, target))
    return lax.ppermute(value, ("groups", "tile", "tm"), pairs)


def swap(value, axis, distance):
    return lax.ppermute(value, axis, [(i, i ^ distance) for i in range(lax.axis_size(axis))])


def aside(g, t, k):
    return (g ^ 1, t, k) if lax.axis_size("groups") % 2 == 0 else (g, t ^ 1, k)


def leaders(value, tile, tm):
    return exchange(
        value, lambda g, t, k: (g, t ^ tile, k ^ tm) if k % 2 else aside(g, t, k)
    )


def next_pair(g, t, k):
    if 0 < k < lax.axis_size("tm") - 1:
        return g, t, (k - 1 if k % 2 == 0 else k + 1)
    return aside(g, t, k)


def second_side(g, t, k):
    if 0 < t < lax.axis_size("tile") - 1:
        return g, (t - 1 if t % 2 == 0 else t + 1), k
    return g, t, k ^ 1


def shifted(value, steps):
    count = lax.axis_size("tm")
    pairs = [(i, i + steps) for i in range(count) if 0 <= i + steps < count]
    return lax.ppermute(value, "tm", pairs)


def scanned(value, direction):
    reach = 1
    while reach < lax.axis_size("tm"):
        value = value + shifted(value, direction * reach)
        reach *= 2
    return value


def reduced(value, axis):
    distance = 1
    while distance < lax.axis_size(axis):
        value = value + swap(value, axis, distance)
        distance *= 2
    return value


def near(*arrays):
    return [(x, "near") for x in arrays]


def shards(
    multiplier, increment, obs_dual, rhs_model, rhs_obs, model_err, obs_err,
    drift_east, drift_north, diffusion, obs_cell, obs_count,
):
    tiles, peers = lax.axis_size("tile"), lax.axis_size("tm")
    levels, rows, cols = multiplier.shape[1:]
    field = ((levels, rows, cols), "near")
    lines = lambda n: ((n, levels, cols), "near")

    inner = swap(multiplier[0], "tm", 1)
    arguments = [increment[0], drift_east[0], drift_north[0], diffusion[0], multiplier[0]]
    arguments += [rhs_model[0], model_err[0], obs_cell, obs_dual, rhs_obs, obs_err]
    count = len(arguments)
    *here, moved, high, low, edge = kernel_call(
        lambda *refs: begin_body(count, *refs),
        "begin",
        [(x, "far") for x in arguments],
        [(x.shape, "near", x.dtype) for x in arguments]
        + [field, lines(5), lines(5), lines(len(EDGE))],
        [pltpu.SemaphoreType.DMA((count + 4 * (PARTS - 1),))],
    )
    incr, *coeffs = here[:4]
    mult, rhs, err, cell, dual, want, var = here[4:]
    four = peers == 4
    if four:
        later = inner
    else:
        later = jnp.where(lax.axis_index("tm") % 2 == 0, inner, exchange(mult, next_pair))
    first, second = kernel_call(
        lambda *refs: rims_body(four, *refs),
        "rims",
        near(edge, later, high, low),
        [lines(6), lines(6)],
    )
    got_first = swap(first, "tile", 1)
    got_second = exchange(second, second_side)
    valid = (lax.broadcasted_iota(jnp.int32, obs_cell.shape, 1) < obs_count).astype(F32)
    local, held = kernel_call(
        spread_body, "spread", near(incr, mult, rhs, err, cell, dual, valid), [field] * 2
    )
    rims = near(first, second, got_first, got_second, edge)
    if not four:
        fix = kernel_call(edges_body, "edges", rims, [lines(8)])[0]
        later = jnp.where(lax.axis_index("tm") == peers - 1, 0.0, later)
        back = kernel_call(adjoint_body, "adjoint", near(*coeffs, later), [field])[0]
        dir_obs, obs_sums = kernel_call(
            gather_body,
            "gather",
            near(incr, cell, dual, want, var, valid),
            [(obs_dual.shape, "near"), ((2, *obs_dual.shape), "near")],
        )
        return scan_path(
            multiplier, increment, obs_dual, local, moved, held, back, fix, dir_obs, obs_sums
        )
    cross = jnp.where(lax.axis_index("tm") < 2, moved, inner).reshape(levels * rows, cols)
    got_cross = leaders(jnp.pad(cross, ((0, rows), (0, 0))), 0, 2)
    back = kernel_call(adjoint_body, "adjoint", near(*coeffs, inner), [field])[0]
    own, urgent, late = kernel_call(
        share_body,
        "share",
        rims + near(local, moved, held, back),
        [((3, levels, rows, cols), "near"), field, lines(4)],
    )
    got_late = leaders(late, 0, 2)
    got = swap(urgent, "tm", 1)
    send = kernel_call(sends_body, "sends", near(own, got), [field])[0]
    send, own, cell = lax.optimization_barrier((send, own, cell))
    got_send = leaders(send, 0, 2)
    dir_obs, obs_sums = kernel_call(
        gather_body,
        "gather",
        near(incr, cell, dual, want, var, valid),
        [(obs_dual.shape, "near"), ((2, *obs_dual.shape), "near")],
    )
    parts = [-(-(2 * levels + 1) // 3)] * 2
    parts.append(2 * levels + 1 - sum(parts))
    rest = kernel_call(
        rest_body, "rest", near(own, obs_sums), [((n, rows, cols), "near") for n in parts]
    )
    got_rest = [swap(x, "tm", 1) for x in rest]
    late_fix = kernel_call(
        lambda *refs: late_body(rows, *refs),
        "late",
        near(got_first, got_second, edge, got_cross, got_late),
        [lines(4)],
        weight=WEIGHT,
    )[0]
    beyond = kernel_call(beyond_body, "beyond", near(*coeffs, got_cross), [field])[0]
    terms, known = kernel_call(
        terms_body,
        "terms",
        near(got_cross, got_late, beyond, own, got, late_fix, *got_rest),
        [((4, levels, rows, cols), "near"), field],
    )
    pair = ((2, levels, rows, cols), "near")
    keep, give, sums = kernel_call(
        dots_body, "dots", near(terms, got_send, got_rest[-1], obs_sums), [pair, field, ((2, 128), "near")]
    )
    total = sums + leaders(sums, 0, 2) + leaders(sums, 1, 0) + leaders(sums, 1, 2)
    distance = 2
    while distance < tiles:
        total = total + leaders(total, distance, 0)
        distance *= 2
    got_dir = swap(give, "tm", 1)
    other = swap(total, "tm", 1)
    total = jnp.where(lax.axis_index("tm") % 2 == 1, total, other)
    new_m, new_i, new_o = kernel_call(
        update_body,
        "update",
        near(mult, incr, dual, dir_obs, keep, known, got_dir, total),
        [(mult.shape, "far"), (mult.shape, "far"), (obs_dual.shape, "far")],
    )
    return new_m[None], new_i[None], new_o


def scan_path(multiplier, increment, obs_dual, local, moved, held, back, fix, dir_obs, obs_sums):
    rows = local.shape[1]
    fix = jnp.moveaxis(fix, 0, 1)
    at = jnp.array([0, 1, rows - 2, rows - 1])
    moved = moved.at[:, at].add(fix[:, :4])
    res_incr = -(held - back.at[:, at].add(fix[:, 4:8]))
    res_model = local + shifted(moved, 1)
    dir_model, dir_incr = scanned(res_model, 1), scanned(res_incr, -1)
    numer = jnp.sum(res_model * dir_model) + jnp.sum(res_incr * dir_incr) + jnp.sum(obs_sums[0])
    denom = jnp.sum(dir_model**2) + jnp.sum(dir_incr**2) + jnp.sum(obs_sums[1])
    sums = reduced(reduced(jnp.stack([numer, denom]), "tm"), "tile")
    step = sums[0] / sums[1]
    return (
        multiplier + step * dir_model[None],
        increment + step * dir_incr[None],
        obs_dual + step * dir_obs,
    )


def solution(mesh):
    grid = P(("groups", "tm"), None, "tile", None)
    line = P(("groups", "tm"), "tile")
    return jax.shard_map(
        shards,
        mesh=mesh,
        in_specs=(grid, grid, line, grid, line, grid, line, grid, grid, grid, line, line),
        out_specs=(grid, grid, line),
        check_vma=False,
    )
```

```python
import jax
import jax.numpy as jnp
from jax import lax
from jax.experimental import pallas as pl
from jax.experimental.pallas import tpu as pltpu
from jax.sharding import PartitionSpec as P

F32 = jnp.float32
VMEM = pltpu.VMEM
GRANT = 24 * 1024 * 1024
WEIGHT = 2600000000
PARTS = 2


def kernel_call(body, name, inputs, outputs, scratch=(), weight=1):
    arrays, in_specs = [], []
    for array, home in inputs:
        if home == "far":
            in_specs.append(pl.BlockSpec(memory_space=pltpu.HBM))
            array = pltpu.with_memory_space_constraint(array, pltpu.HBM)
        else:
            in_specs.append(pl.BlockSpec(memory_space=VMEM))
            array = pltpu.with_memory_space_constraint(array, VMEM)
        arrays.append(array)
    out_shape, out_specs = [], []
    for shape, home, *dtype in outputs:
        dtype = dtype[0] if dtype else F32
        out_specs.append(pl.BlockSpec(memory_space=VMEM))
        out_shape.append(
            VMEM(shape, dtype) if home == "near" else jax.ShapeDtypeStruct(shape, dtype)
        )
    return pl.pallas_call(
        body,
        name=name,
        out_shape=out_shape,
        in_specs=in_specs,
        out_specs=out_specs,
        scratch_shapes=list(scratch),
        cost_estimate=pl.CostEstimate(flops=weight, bytes_accessed=1, transcendentals=0),
        compiler_params=pltpu.CompilerParams(vmem_limit_bytes=GRANT),
    )(*arrays)


def lanes(row):
    total = row[:, 0:128]
    for col in range(128, row.shape[1], 128):
        total = total + row[:, col : col + 128]
    return total


def iotas(shape):
    return (
        lax.broadcasted_iota(jnp.int32, shape, 0),
        lax.broadcasted_iota(jnp.int32, shape, 1),
    )


def up(field, axis):
    return pltpu.roll(field, field.shape[axis] - 1, axis)


def down(field, axis):
    return pltpu.roll(field, 1, axis)


def taps(a, b, c):
    i, y = iotas(a.shape)
    rows, cols = a.shape
    return (
        1.0 - 4.0 * c,
        jnp.where(i < rows - 1, c - a, 0.0),
        jnp.where(i > 0, c + a, 0.0),
        jnp.where(y < cols - 1, c - b, 0.0),
        jnp.where(y > 0, c + b, 0.0),
    )


def forward(state, coeffs):
    mid, east, west, north, south = coeffs
    return (
        mid * state
        + east * up(state, 0)
        + west * down(state, 0)
        + north * up(state, 1)
        + south * down(state, 1)
    )


def adjoint(state, coeffs):
    mid, east, west, north, south = coeffs
    return (
        mid * state
        + down(east * state, 0)
        + up(west * state, 0)
        + down(north * state, 1)
        + up(south * state, 1)
    )


EDGE = ("mid_low", "mid_high", "north_low", "north_high", "south_low", "south_high")
EDGE += ("west_low", "west_next", "east_high", "east_next", "east_low", "west_high")


def begin_body(count, *refs):
    sources, targets = refs[:count], refs[count : 2 * count]
    once_ref, high_ref, low_ref, edge_ref, sems = refs[2 * count :]
    s_ref, a_ref, b_ref, c_ref = targets[:4]
    levels, rows, _ = s_ref.shape
    last = rows - 1
    cut = levels // PARTS
    parts = [
        [
            pltpu.make_async_copy(
                sources[n].at[pl.ds(part * cut, cut)],
                targets[n].at[pl.ds(part * cut, cut)],
                sems.at[part * 4 + n],
            )
            for n in range(4)
        ]
        for part in range(PARTS)
    ]
    rest = [
        pltpu.make_async_copy(sources[n], targets[n], sems.at[4 * (PARTS - 1) + n])
        for n in range(4, count)
    ]
    for copy in sum(parts, []) + rest:
        copy.start()
    for lev in range(levels):
        if lev % cut == 0:
            for copy in parts[lev // cut]:
                copy.wait()
        s, a, b, c = s_ref[lev], a_ref[lev], b_ref[lev], c_ref[lev]
        coeffs = taps(a, b, c)
        once = forward(s, coeffs)
        once_ref[lev] = once
        mid, east, west, north, south = coeffs
        at = pl.ds(lev, 1)
        open_east = c[last : last + 1] - a[last : last + 1]
        open_west = c[0:1] + a[0:1]
        high_ref[0, at] = s[last : last + 1]
        high_ref[1, at] = once[last : last + 1]
        high_ref[2, at] = open_east
        high_ref[3, at] = b[last : last + 1]
        high_ref[4, at] = c[last : last + 1]
        low_ref[0, at] = s[0:1]
        low_ref[1, at] = once[0:1]
        low_ref[2, at] = open_west
        low_ref[3, at] = b[0:1]
        low_ref[4, at] = c[0:1]
        rows_of = {
            "mid_low": mid[0:1],
            "mid_high": mid[last : last + 1],
            "north_low": north[0:1],
            "north_high": north[last : last + 1],
            "south_low": south[0:1],
            "south_high": south[last : last + 1],
            "west_low": open_west,
            "west_next": west[1:2],
            "east_high": open_east,
            "east_next": east[last - 1 : last],
            "east_low": east[0:1],
            "west_high": west[last : last + 1],
        }
        for n, key in enumerate(EDGE):
            edge_ref[n, at] = rows_of[key]
    for copy in rest:
        copy.wait()


def forward_body(a_ref, b_ref, c_ref, once_ref, moved_ref):
    for lev in range(a_ref.shape[0]):
        coeffs = taps(a_ref[lev], b_ref[lev], c_ref[lev])
        moved_ref[lev] = forward(once_ref[lev], coeffs)


def adjoint_body(a_ref, b_ref, c_ref, later_ref, back_ref):
    for lev in range(a_ref.shape[0]):
        coeffs = taps(a_ref[lev], b_ref[lev], c_ref[lev])
        back_ref[lev] = adjoint(adjoint(later_ref[lev], coeffs), coeffs)


def outer_products(k, later):
    def once(side, at, beside):
        mid, north, south = k["mid_" + side], k["north_" + side], k["south_" + side]
        return mid * at + beside + down(north * at, 1) + up(south * at, 1)

    west, east = k["west_low"], k["east_high"]
    return (
        (west * later[0], west * once("low", later[0], k["west_next"] * later[1])),
        (east * later[3], east * once("high", later[3], k["east_next"] * later[2])),
    )


def rims_body(four, edge_ref, later_ref, high_ref, low_ref, first_ref, second_ref):
    position, peers = lax.axis_index("tm"), lax.axis_size("tm")
    odd = lax.rem(lax.axis_index("tile"), 2)
    k = {key: edge_ref[n] for n, key in enumerate(EDGE)}
    levels, rows, _ = later_ref.shape
    later = [
        jnp.concatenate([later_ref[lev, row : row + 1] for lev in range(levels)], 0)
        for row in (0, 1, rows - 2, rows - 1)
    ]
    products = outer_products(k, later)
    zero = jnp.zeros(later[0].shape, F32)
    sent = []
    for ref, product, outer, inside, beside in (
        (low_ref, products[0], later[0], later[1], k["west_next"]),
        (high_ref, products[1], later[3], later[2], k["east_next"]),
    ):
        out = [ref[0], ref[1], ref[2], *product, zero]
        if four:
            second, final = position == 1, position == peers - 1
            out[0] = jnp.where(final, outer, out[0])
            out[1] = jnp.where(final, inside, out[1])
            out[3] = jnp.where(second, ref[3], out[3])
            out[4] = jnp.where(second, ref[4], out[4])
            out[5] = jnp.where(second, beside, zero)
        sent.append(out)
    for n, (low, high) in enumerate(zip(*sent)):
        first_ref[n] = jnp.where(odd == 0, high, low)
        second_ref[n] = jnp.where(odd == 0, low, high)


def sides(first, second):
    tile, tiles = lax.axis_index("tile"), lax.axis_size("tile")
    odd = lax.rem(tile, 2)
    below, above = jnp.where(odd == 0, second, first), jnp.where(odd == 0, first, second)
    return jnp.where(tile > 0, below, 0.0), jnp.where(tile < tiles - 1, above, 0.0)


def own_sides(first, second):
    odd = lax.rem(lax.axis_index("tile"), 2)
    return jnp.where(odd == 0, second, first), jnp.where(odd == 0, first, second)


def back_fix(k, product, stepped, own_product, toward):
    def across(x, side):
        mid, north, south = k["mid_" + side], k["north_" + side], k["south_" + side]
        return mid * x + down(north * x, 1) + up(south * x, 1)

    return (
        across(product[0], "low") + (stepped[0] + toward[0] * own_product[0]),
        k["east_low"] * product[0],
        k["west_high"] * product[1],
        across(product[1], "high") + (stepped[1] + toward[1] * own_product[1]),
    )


def edges_of(first_ref, second_ref, got_first_ref, got_second_ref, edge_ref):
    k = {key: edge_ref[n] for n, key in enumerate(EDGE)}
    state, stepped, toward, product, product_stepped = (
        sides(got_first_ref[n], got_second_ref[n]) for n in range(5)
    )
    own_state = own_sides(first_ref[0], second_ref[0])
    own_product = own_sides(first_ref[3], second_ref[3])

    def along(x, side):
        mid, north, south = k["mid_" + side], k["north_" + side], k["south_" + side]
        return mid * x + north * up(x, 1) + south * down(x, 1)

    new_low, new_high = k["west_low"] * state[0], k["east_high"] * state[1]
    moved = (
        along(new_low, "low") + k["west_low"] * (stepped[0] + toward[0] * own_state[0]),
        k["west_next"] * new_low,
        k["east_next"] * new_high,
        along(new_high, "high") + k["east_high"] * (stepped[1] + toward[1] * own_state[1]),
    )
    back = back_fix(k, product, product_stepped, own_product, toward)
    return moved, back, (state[0], stepped[0], state[1], stepped[1])


def edges_body(*refs):
    *in_refs, fix_ref = refs
    moved, back, _ = edges_of(*in_refs)
    wanted = lax.axis_index("tm") < lax.axis_size("tm") - 1
    for n in range(4):
        fix_ref[n] = moved[n]
        fix_ref[4 + n] = jnp.where(wanted, back[n], 0.0)


def late_body(rows, got_first_ref, got_second_ref, edge_ref, cross_ref, late_ref, fix_ref):
    k = {key: edge_ref[n] for n, key in enumerate(EDGE)}
    levels, cols = edge_ref.shape[1:]
    _, y = iotas((levels, cols))
    toward, drift, diffuse, beside = (
        sides(got_first_ref[n], got_second_ref[n]) for n in range(2, 6)
    )
    product, stepped, own = [], [], []
    for side in range(2):
        near_by, far_off = late_ref[2 * side], late_ref[2 * side + 1]
        b, c = drift[side], diffuse[side]
        north, south = jnp.where(y < cols - 1, c - b, 0.0), jnp.where(y > 0, c + b, 0.0)
        once = (1.0 - 4.0 * c) * near_by + beside[side] * far_off
        once = once + down(north * near_by, 1) + up(south * near_by, 1)
        product.append(toward[side] * near_by)
        stepped.append(toward[side] * once)
        row = side * (rows - 1)
        outer = [cross_ref[lev * rows + row : lev * rows + row + 1] for lev in range(levels)]
        own.append(k[("west_low", "east_high")[side]] * jnp.concatenate(outer, 0))
    for n, fix in enumerate(back_fix(k, product, stepped, own, toward)):
        fix_ref[n] = fix


def beyond_body(a_ref, b_ref, c_ref, cross_ref, back_ref):
    levels, rows, _ = a_ref.shape
    for lev in range(levels):
        coeffs = taps(a_ref[lev], b_ref[lev], c_ref[lev])
        cross = cross_ref[lev * rows : (lev + 1) * rows]
        back_ref[lev] = adjoint(adjoint(cross, coeffs), coeffs)


def thirds(x):
    one = x.astype(jnp.bfloat16)
    rest = x - one.astype(F32)
    two = rest.astype(jnp.bfloat16)
    return one, two, (rest - two.astype(F32)).astype(jnp.bfloat16)


def slot_masks(cell, lines, cols):
    slots = cell.shape[1]
    at_line = iotas((lines, slots))[0] == cell // cols
    at_col = iotas((cols, slots))[0] == lax.rem(cell, cols)
    return at_line, jnp.where(at_col, 1.0, 0.0).astype(jnp.bfloat16)


def spread_body(
    incr_ref, mult_ref, rhs_ref, err_ref, cell_ref, dual_ref, valid_ref, local_ref, held_ref
):
    levels, rows, cols = incr_ref.shape
    lines = levels * rows
    at_line, at_col = slot_masks(cell_ref[...], lines, cols)
    weights = thirds(jnp.where(at_line, valid_ref[...] * dual_ref[...], 0.0))
    spread = lax.dot_general(
        jnp.concatenate(weights, 0), at_col, (((1,), (1,)), ((), ())), preferred_element_type=F32
    )
    ht = spread[:lines] + spread[lines : 2 * lines] + spread[2 * lines :]
    mult = mult_ref[...]
    held_ref[...] = mult + ht.reshape(levels, rows, cols)
    local_ref[...] = rhs_ref[...] - (err_ref[...] * mult + incr_ref[...])


def gather_body(
    incr_ref, cell_ref, dual_ref, want_ref, var_ref, valid_ref, dir_ref, sums_ref
):
    levels, rows, cols = incr_ref.shape
    lines = levels * rows
    at_line, at_col = slot_masks(cell_ref[...], lines, cols)
    fields = thirds(incr_ref[...].reshape(lines, cols))
    picked = jnp.dot(jnp.concatenate(fields, 0), at_col, preferred_element_type=F32)
    picked = picked[:lines] + picked[lines : 2 * lines] + picked[2 * lines :]
    valid, var = valid_ref[...], var_ref[...]
    hx = jnp.sum(jnp.where(at_line, picked, 0.0), axis=0, keepdims=True) * valid
    res = valid * (want_ref[...] - (var * dual_ref[...] + hx))
    direction = res / var
    dir_ref[...] = direction
    sums_ref[0] = res * direction
    sums_ref[1] = direction * direction


def corrected(field, fix):
    rows = field.shape[0]
    i, _ = iotas(field.shape)
    for n, row in enumerate((0, 1, rows - 2, rows - 1)):
        field = field + jnp.where(i == row, fix[n], 0.0)
    return field


def fixes(ref, start, lev):
    return [ref[start + n, pl.ds(lev, 1)] for n in range(4)]


def minus(rows):
    return [-x for x in rows]


def share_body(
    first_ref, second_ref, got_first_ref, got_second_ref, edge_ref,
    local_ref, moved_ref, held_ref, back_ref, own_ref, urgent_ref, late_ref,
):
    position = lax.axis_index("tm")
    first, low_pair = lax.rem(position, 2) == 0, position < 2
    fix_moved, fix_back, beyond = edges_of(
        first_ref, second_ref, got_first_ref, got_second_ref, edge_ref
    )
    for n in range(4):
        late_ref[n] = jnp.where(low_pair, fix_moved[n], beyond[n])
    for lev in range(local_ref.shape[0]):
        back = corrected(back_ref[lev], [x[lev : lev + 1] for x in fix_back])
        moved = corrected(moved_ref[lev], [x[lev : lev + 1] for x in fix_moved])
        local = local_ref[lev]
        residual = held_ref[lev] - jnp.where(first, back, 0.0)
        own_ref[0, lev] = local
        own_ref[1, lev] = moved
        own_ref[2, lev] = residual
        urgent_ref[lev] = jnp.where(low_pair, local + moved, residual)


def sends_body(own_ref, got_ref, send_ref):
    low_pair = lax.axis_index("tm") < 2
    for lev in range(own_ref.shape[1]):
        mine = jnp.where(low_pair, own_ref[0, lev], own_ref[2, lev])
        send_ref[lev] = mine + got_ref[lev]


def rest_body(own_ref, obs_ref, *out_refs):
    levels = own_ref.shape[1]
    low_pair = lax.axis_index("tm") < 2
    blocks = [(ref, n) for ref in out_refs for n in range(ref.shape[0])]
    for lev in range(levels):
        ref, n = blocks[lev]
        ref[n] = own_ref[0, lev]
        ref, n = blocks[levels + lev]
        ref[n] = jnp.where(low_pair, own_ref[2, lev], own_ref[1, lev])
    ref, n = blocks[2 * levels]
    ref[n] = jnp.zeros(ref.shape[1:], F32)
    for i in range(2):
        ref[n, i : i + 1, 0:128] = lanes(obs_ref[i])


def terms_body(cross_ref, late_ref, beyond_ref, own_ref, got_ref, fix_ref, *refs):
    low_pair = lax.axis_index("tm") < 2
    _, levels, rows, _ = own_ref.shape
    *rest_refs, terms_ref, known_ref = refs
    blocks = [(ref, n) for ref in rest_refs for n in range(ref.shape[0])]
    for lev in range(levels):
        got = got_ref[lev]
        local, residual = own_ref[0, lev], own_ref[2, lev]
        back = corrected(beyond_ref[lev], fixes(fix_ref, 0, lev))
        moved = corrected(cross_ref[lev * rows : (lev + 1) * rows], fixes(late_ref, 0, lev))
        rest0, rest1 = (ref[n] for ref, n in (blocks[lev], blocks[levels + lev]))
        terms_ref[0, lev] = jnp.where(low_pair, rest0, residual)
        terms_ref[1, lev] = jnp.where(low_pair, local, residual) + got
        terms_ref[2, lev] = jnp.where(low_pair, residual - back, rest0 + moved)
        terms_ref[3, lev] = jnp.where(low_pair, rest1, local + rest1)
        known_ref[lev] = jnp.where(low_pair, local, residual + got)


def dots_body(terms_ref, got_ref, rest_ref, obs_ref, keep_ref, give_ref, sums_ref):
    _, levels, rows, cols = terms_ref.shape
    low_pair = lax.axis_index("tm") < 2
    numer, denom = jnp.zeros((8, 128), F32), jnp.zeros((8, 128), F32)

    def folded(x):
        total = None
        for r in range(0, rows, 8):
            part = lanes(x[r : r + 8])
            total = part if total is None else total + part
        return total

    for lev in range(levels):
        y0, one, z0, z1 = (terms_ref[n, lev] for n in range(4))
        two = got_ref[lev] + z0
        three = two + z1
        numer = numer + folded(y0 * y0 + (one - y0) * one + z0 * two + z1 * three)
        denom = denom + folded(y0 * y0 + one * one + two * two + three * three)
        keep_ref[0, lev] = jnp.where(low_pair, one, three)
        keep_ref[1, lev] = jnp.where(low_pair, two, y0)
        give_ref[lev] = jnp.where(low_pair, three, two)
    for n, total in enumerate((numer, denom)):
        obs = lanes(obs_ref[n]) + rest_ref[rest_ref.shape[0] - 1, n : n + 1, 0:128]
        sums_ref[n : n + 1] = jnp.sum(total, axis=0, keepdims=True) + obs


def update_body(
    mult_ref, incr_ref, dual_ref, dir_ref, keep_ref, known_ref, got_ref, sums_ref,
    new_m_ref, new_i_ref, new_o_ref,
):
    position = lax.axis_index("tm")
    leads, low_pair = lax.rem(position, 2) == 1, position < 2
    total = jnp.sum(sums_ref[...], axis=1, keepdims=True)
    step = total[0:1] / total[1:2]
    for lev in range(mult_ref.shape[0]):
        known, got = known_ref[lev], got_ref[lev]
        model = jnp.where(leads, keep_ref[0, lev], jnp.where(low_pair, known, got))
        back = jnp.where(leads, keep_ref[1, lev], jnp.where(low_pair, got, known))
        new_m_ref[lev] = mult_ref[lev] + step * model
        new_i_ref[lev] = incr_ref[lev] - step * back
    new_o_ref[...] = dual_ref[...] + step * dir_ref[...]


def exchange(value, partner):
    groups, tiles, peers = (lax.axis_size(x) for x in ("groups", "tile", "tm"))
    pairs = []
    for g in range(groups):
        for t in range(tiles):
            for k in range(peers):
                to_g, to_t, to_k = partner(g, t, k)
                target = (to_g * tiles + to_t) * peers + to_k
                pairs.append(((g * tiles + t) * peers + k, target))
    return lax.ppermute(value, ("groups", "tile", "tm"), pairs)


def swap(value, axis, distance):
    return lax.ppermute(value, axis, [(i, i ^ distance) for i in range(lax.axis_size(axis))])


def aside(g, t, k):
    return (g ^ 1, t, k) if lax.axis_size("groups") % 2 == 0 else (g, t ^ 1, k)


def leaders(value, tile, tm):
    return exchange(
        value, lambda g, t, k: (g, t ^ tile, k ^ tm) if k % 2 else aside(g, t, k)
    )


def next_pair(g, t, k):
    if 0 < k < lax.axis_size("tm") - 1:
        return g, t, (k - 1 if k % 2 == 0 else k + 1)
    return aside(g, t, k)


def second_side(g, t, k):
    if 0 < t < lax.axis_size("tile") - 1:
        return g, (t - 1 if t % 2 == 0 else t + 1), k
    return g, t, k ^ 1


def shifted(value, steps):
    count = lax.axis_size("tm")
    pairs = [(i, i + steps) for i in range(count) if 0 <= i + steps < count]
    return lax.ppermute(value, "tm", pairs)


def scanned(value, direction):
    reach = 1
    while reach < lax.axis_size("tm"):
        value = value + shifted(value, direction * reach)
        reach *= 2
    return value


def reduced(value, axis):
    distance = 1
    while distance < lax.axis_size(axis):
        value = value + swap(value, axis, distance)
        distance *= 2
    return value


def near(*arrays):
    return [(x, "near") for x in arrays]


def shards(
    multiplier, increment, obs_dual, rhs_model, rhs_obs, model_err, obs_err,
    drift_east, drift_north, diffusion, obs_cell, obs_count,
):
    tiles, peers = lax.axis_size("tile"), lax.axis_size("tm")
    levels, rows, cols = multiplier.shape[1:]
    field = ((levels, rows, cols), "near")
    lines = lambda n: ((n, levels, cols), "near")

    inner = swap(multiplier[0], "tm", 1)
    arguments = [increment[0], drift_east[0], drift_north[0], diffusion[0], multiplier[0]]
    arguments += [rhs_model[0], model_err[0], obs_cell, obs_dual, rhs_obs, obs_err]
    count = len(arguments)
    *here, once, high, low, edge = kernel_call(
        lambda *refs: begin_body(count, *refs),
        "begin",
        [(x, "far") for x in arguments],
        [(x.shape, "near", x.dtype) for x in arguments]
        + [field, lines(5), lines(5), lines(len(EDGE))],
        [pltpu.SemaphoreType.DMA((count + 4 * (PARTS - 1),))],
    )
    incr, *coeffs = here[:4]
    mult, rhs, err, cell, dual, want, var = here[4:]
    four = peers == 4
    if four:
        later = inner
    else:
        later = jnp.where(lax.axis_index("tm") % 2 == 0, inner, exchange(mult, next_pair))
    first, second = kernel_call(
        lambda *refs: rims_body(four, *refs),
        "rims",
        near(edge, later, high, low),
        [lines(6), lines(6)],
    )
    got_first = swap(first, "tile", 1)
    got_second = exchange(second, second_side)
    valid = (lax.broadcasted_iota(jnp.int32, obs_cell.shape, 1) < obs_count).astype(F32)
    local, held = kernel_call(
        spread_body, "spread", near(incr, mult, rhs, err, cell, dual, valid), [field] * 2
    )
    once, first = lax.optimization_barrier((once, first))
    moved = kernel_call(forward_body, "forward", near(*coeffs, once), [field])[0]
    rims = near(first, second, got_first, got_second, edge)
    if not four:
        fix = kernel_call(edges_body, "edges", rims, [lines(8)])[0]
        later = jnp.where(lax.axis_index("tm") == peers - 1, 0.0, later)
        back = kernel_call(adjoint_body, "adjoint", near(*coeffs, later), [field])[0]
        dir_obs, obs_sums = kernel_call(
            gather_body,
            "gather",
            near(incr, cell, dual, want, var, valid),
            [(obs_dual.shape, "near"), ((2, *obs_dual.shape), "near")],
        )
        return scan_path(
            multiplier, increment, obs_dual, local, moved, held, back, fix, dir_obs, obs_sums
        )
    cross = jnp.where(lax.axis_index("tm") < 2, moved, inner).reshape(levels * rows, cols)
    got_cross = leaders(jnp.pad(cross, ((0, rows), (0, 0))), 0, 2)
    back = kernel_call(adjoint_body, "adjoint", near(*coeffs, inner), [field])[0]
    own, urgent, late = kernel_call(
        share_body,
        "share",
        rims + near(local, moved, held, back),
        [((3, levels, rows, cols), "near"), field, lines(4)],
    )
    got_late = leaders(late, 0, 2)
    got = swap(urgent, "tm", 1)
    send = kernel_call(sends_body, "sends", near(own, got), [field])[0]
    send, own, cell = lax.optimization_barrier((send, own, cell))
    got_send = leaders(send, 0, 2)
    dir_obs, obs_sums = kernel_call(
        gather_body,
        "gather",
        near(incr, cell, dual, want, var, valid),
        [(obs_dual.shape, "near"), ((2, *obs_dual.shape), "near")],
    )
    parts = [-(-(2 * levels + 1) // 3)] * 2
    parts.append(2 * levels + 1 - sum(parts))
    rest = kernel_call(
        rest_body, "rest", near(own, obs_sums), [((n, rows, cols), "near") for n in parts]
    )
    got_rest = [swap(x, "tm", 1) for x in rest]
    late_fix = kernel_call(
        lambda *refs: late_body(rows, *refs),
        "late",
        near(got_first, got_second, edge, got_cross, got_late),
        [lines(4)],
        weight=WEIGHT,
    )[0]
    beyond = kernel_call(beyond_body, "beyond", near(*coeffs, got_cross), [field])[0]
    terms, known = kernel_call(
        terms_body,
        "terms",
        near(got_cross, got_late, beyond, own, got, late_fix, *got_rest),
        [((4, levels, rows, cols), "near"), field],
    )
    pair = ((2, levels, rows, cols), "near")
    keep, give, sums = kernel_call(
        dots_body, "dots", near(terms, got_send, got_rest[-1], obs_sums), [pair, field, ((2, 128), "near")]
    )
    total = sums + leaders(sums, 0, 2) + leaders(sums, 1, 0) + leaders(sums, 1, 2)
    distance = 2
    while distance < tiles:
        total = total + leaders(total, distance, 0)
        distance *= 2
    got_dir = swap(give, "tm", 1)
    other = swap(total, "tm", 1)
    total = jnp.where(lax.axis_index("tm") % 2 == 1, total, other)
    new_m, new_i, new_o = kernel_call(
        update_body,
        "update",
        near(mult, incr, dual, dir_obs, keep, known, got_dir, total),
        [(mult.shape, "far"), (mult.shape, "far"), (obs_dual.shape, "far")],
    )
    return new_m[None], new_i[None], new_o


def scan_path(multiplier, increment, obs_dual, local, moved, held, back, fix, dir_obs, obs_sums):
    rows = local.shape[1]
    fix = jnp.moveaxis(fix, 0, 1)
    at = jnp.array([0, 1, rows - 2, rows - 1])
    moved = moved.at[:, at].add(fix[:, :4])
    res_incr = -(held - back.at[:, at].add(fix[:, 4:8]))
    res_model = local + shifted(moved, 1)
    dir_model, dir_incr = scanned(res_model, 1), scanned(res_incr, -1)
    numer = jnp.sum(res_model * dir_model) + jnp.sum(res_incr * dir_incr) + jnp.sum(obs_sums[0])
    denom = jnp.sum(dir_model**2) + jnp.sum(dir_incr**2) + jnp.sum(obs_sums[1])
    sums = reduced(reduced(jnp.stack([numer, denom]), "tm"), "tile")
    step = sums[0] / sums[1]
    return (
        multiplier + step * dir_model[None],
        increment + step * dir_incr[None],
        obs_dual + step * dir_obs,
    )


def solution(mesh):
    grid = P(("groups", "tm"), None, "tile", None)
    line = P(("groups", "tm"), "tile")
    return jax.shard_map(
        shards,
        mesh=mesh,
        in_specs=(grid, grid, line, grid, line, grid, line, grid, grid, grid, line, line),
        out_specs=(grid, grid, line),
        check_vma=False,
    )
```

```python
import jax
import jax.numpy as jnp
from jax import lax
from jax.experimental import pallas as pl
from jax.experimental.pallas import tpu as pltpu
from jax.sharding import PartitionSpec as P

F32 = jnp.float32
VMEM = pltpu.VMEM
GRANT = 24 * 1024 * 1024
WEIGHT = 2600000000
PARTS = 2


def kernel_call(body, name, inputs, outputs, scratch=(), weight=1):
    arrays, in_specs = [], []
    for array, home in inputs:
        if home == "far":
            in_specs.append(pl.BlockSpec(memory_space=pltpu.HBM))
            array = pltpu.with_memory_space_constraint(array, pltpu.HBM)
        else:
            in_specs.append(pl.BlockSpec(memory_space=VMEM))
            array = pltpu.with_memory_space_constraint(array, VMEM)
        arrays.append(array)
    out_shape, out_specs = [], []
    for shape, home, *dtype in outputs:
        dtype = dtype[0] if dtype else F32
        out_specs.append(pl.BlockSpec(memory_space=VMEM))
        out_shape.append(
            VMEM(shape, dtype) if home == "near" else jax.ShapeDtypeStruct(shape, dtype)
        )
    return pl.pallas_call(
        body,
        name=name,
        out_shape=out_shape,
        in_specs=in_specs,
        out_specs=out_specs,
        scratch_shapes=list(scratch),
        cost_estimate=pl.CostEstimate(flops=weight, bytes_accessed=1, transcendentals=0),
        compiler_params=pltpu.CompilerParams(vmem_limit_bytes=GRANT),
    )(*arrays)


def lanes(row):
    total = row[:, 0:128]
    for col in range(128, row.shape[1], 128):
        total = total + row[:, col : col + 128]
    return total


def iotas(shape):
    return (
        lax.broadcasted_iota(jnp.int32, shape, 0),
        lax.broadcasted_iota(jnp.int32, shape, 1),
    )


def up(field, axis):
    return pltpu.roll(field, field.shape[axis] - 1, axis)


def down(field, axis):
    return pltpu.roll(field, 1, axis)


def taps(a, b, c):
    i, y = iotas(a.shape)
    rows, cols = a.shape
    return (
        1.0 - 4.0 * c,
        jnp.where(i < rows - 1, c - a, 0.0),
        jnp.where(i > 0, c + a, 0.0),
        jnp.where(y < cols - 1, c - b, 0.0),
        jnp.where(y > 0, c + b, 0.0),
    )


def forward(state, coeffs):
    mid, east, west, north, south = coeffs
    return (
        mid * state
        + east * up(state, 0)
        + west * down(state, 0)
        + north * up(state, 1)
        + south * down(state, 1)
    )


def adjoint(state, coeffs):
    mid, east, west, north, south = coeffs
    return (
        mid * state
        + down(east * state, 0)
        + up(west * state, 0)
        + down(north * state, 1)
        + up(south * state, 1)
    )


EDGE = ("mid_low", "mid_high", "north_low", "north_high", "south_low", "south_high")
EDGE += ("west_low", "west_next", "east_high", "east_next", "east_low", "west_high")


def begin_body(count, *refs):
    sources, targets = refs[:count], refs[count : 2 * count]
    once_ref, high_ref, low_ref, edge_ref, sems = refs[2 * count :]
    s_ref, a_ref, b_ref, c_ref = targets[:4]
    levels, rows, _ = s_ref.shape
    last = rows - 1
    cut = levels // PARTS
    parts = [
        [
            pltpu.make_async_copy(
                sources[n].at[pl.ds(part * cut, cut)],
                targets[n].at[pl.ds(part * cut, cut)],
                sems.at[part * 4 + n],
            )
            for n in range(4)
        ]
        for part in range(PARTS)
    ]
    rest = [
        pltpu.make_async_copy(sources[n], targets[n], sems.at[4 * (PARTS - 1) + n])
        for n in range(4, count)
    ]
    for copy in sum(parts, []) + rest:
        copy.start()
    for lev in range(levels):
        if lev % cut == 0:
            for copy in parts[lev // cut]:
                copy.wait()
        s, a, b, c = s_ref[lev], a_ref[lev], b_ref[lev], c_ref[lev]
        coeffs = taps(a, b, c)
        once = forward(s, coeffs)
        once_ref[lev] = once
        mid, east, west, north, south = coeffs
        at = pl.ds(lev, 1)
        open_east = c[last : last + 1] - a[last : last + 1]
        open_west = c[0:1] + a[0:1]
        high_ref[0, at] = s[last : last + 1]
        high_ref[1, at] = once[last : last + 1]
        high_ref[2, at] = open_east
        high_ref[3, at] = b[last : last + 1]
        high_ref[4, at] = c[last : last + 1]
        low_ref[0, at] = s[0:1]
        low_ref[1, at] = once[0:1]
        low_ref[2, at] = open_west
        low_ref[3, at] = b[0:1]
        low_ref[4, at] = c[0:1]
        rows_of = {
            "mid_low": mid[0:1],
            "mid_high": mid[last : last + 1],
            "north_low": north[0:1],
            "north_high": north[last : last + 1],
            "south_low": south[0:1],
            "south_high": south[last : last + 1],
            "west_low": open_west,
            "west_next": west[1:2],
            "east_high": open_east,
            "east_next": east[last - 1 : last],
            "east_low": east[0:1],
            "west_high": west[last : last + 1],
        }
        for n, key in enumerate(EDGE):
            edge_ref[n, at] = rows_of[key]
    for copy in rest:
        copy.wait()


def forward_body(a_ref, b_ref, c_ref, once_ref, moved_ref):
    for lev in range(a_ref.shape[0]):
        coeffs = taps(a_ref[lev], b_ref[lev], c_ref[lev])
        moved_ref[lev] = forward(once_ref[lev], coeffs)


def adjoint_body(a_ref, b_ref, c_ref, later_ref, back_ref):
    for lev in range(a_ref.shape[0]):
        coeffs = taps(a_ref[lev], b_ref[lev], c_ref[lev])
        back_ref[lev] = adjoint(adjoint(later_ref[lev], coeffs), coeffs)


def outer_products(k, later):
    def once(side, at, beside):
        mid, north, south = k["mid_" + side], k["north_" + side], k["south_" + side]
        return mid * at + beside + down(north * at, 1) + up(south * at, 1)

    west, east = k["west_low"], k["east_high"]
    return (
        (west * later[0], west * once("low", later[0], k["west_next"] * later[1])),
        (east * later[3], east * once("high", later[3], k["east_next"] * later[2])),
    )


def rims_body(four, edge_ref, later_ref, high_ref, low_ref, first_ref, second_ref):
    position, peers = lax.axis_index("tm"), lax.axis_size("tm")
    odd = lax.rem(lax.axis_index("tile") + 1, 2)
    k = {key: edge_ref[n] for n, key in enumerate(EDGE)}
    levels, rows, _ = later_ref.shape
    later = [
        jnp.concatenate([later_ref[lev, row : row + 1] for lev in range(levels)], 0)
        for row in (0, 1, rows - 2, rows - 1)
    ]
    products = outer_products(k, later)
    zero = jnp.zeros(later[0].shape, F32)
    sent = []
    for ref, product, outer, inside, beside in (
        (low_ref, products[0], later[0], later[1], k["west_next"]),
        (high_ref, products[1], later[3], later[2], k["east_next"]),
    ):
        out = [ref[0], ref[1], ref[2], *product, zero]
        if four:
            second, final = position == 1, position == peers - 1
            out[0] = jnp.where(final, outer, out[0])
            out[1] = jnp.where(final, inside, out[1])
            out[3] = jnp.where(second, ref[3], out[3])
            out[4] = jnp.where(second, ref[4], out[4])
            out[5] = jnp.where(second, beside, zero)
        sent.append(out)
    for n, (low, high) in enumerate(zip(*sent)):
        first_ref[n] = jnp.where(odd == 0, high, low)
        second_ref[n] = jnp.where(odd == 0, low, high)


def sides(first, second):
    tile, tiles = lax.axis_index("tile"), lax.axis_size("tile")
    odd = lax.rem(tile + 1, 2)
    below, above = jnp.where(odd == 0, second, first), jnp.where(odd == 0, first, second)
    return jnp.where(tile > 0, below, 0.0), jnp.where(tile < tiles - 1, above, 0.0)


def own_sides(first, second):
    odd = lax.rem(lax.axis_index("tile") + 1, 2)
    return jnp.where(odd == 0, second, first), jnp.where(odd == 0, first, second)


def back_fix(k, product, stepped, own_product, toward):
    def across(x, side):
        mid, north, south = k["mid_" + side], k["north_" + side], k["south_" + side]
        return mid * x + down(north * x, 1) + up(south * x, 1)

    return (
        across(product[0], "low") + (stepped[0] + toward[0] * own_product[0]),
        k["east_low"] * product[0],
        k["west_high"] * product[1],
        across(product[1], "high") + (stepped[1] + toward[1] * own_product[1]),
    )


def edges_of(first_ref, second_ref, got_first_ref, got_second_ref, edge_ref):
    k = {key: edge_ref[n] for n, key in enumerate(EDGE)}
    state, stepped, toward, product, product_stepped = (
        sides(got_first_ref[n], got_second_ref[n]) for n in range(5)
    )
    own_state = own_sides(first_ref[0], second_ref[0])
    own_product = own_sides(first_ref[3], second_ref[3])

    def along(x, side):
        mid, north, south = k["mid_" + side], k["north_" + side], k["south_" + side]
        return mid * x + north * up(x, 1) + south * down(x, 1)

    new_low, new_high = k["west_low"] * state[0], k["east_high"] * state[1]
    moved = (
        along(new_low, "low") + k["west_low"] * (stepped[0] + toward[0] * own_state[0]),
        k["west_next"] * new_low,
        k["east_next"] * new_high,
        along(new_high, "high") + k["east_high"] * (stepped[1] + toward[1] * own_state[1]),
    )
    back = back_fix(k, product, product_stepped, own_product, toward)
    return moved, back, (state[0], stepped[0], state[1], stepped[1])


def edges_body(*refs):
    *in_refs, fix_ref = refs
    moved, back, _ = edges_of(*in_refs)
    wanted = lax.axis_index("tm") < lax.axis_size("tm") - 1
    for n in range(4):
        fix_ref[n] = moved[n]
        fix_ref[4 + n] = jnp.where(wanted, back[n], 0.0)


def late_body(rows, got_first_ref, got_second_ref, edge_ref, cross_ref, late_ref, fix_ref):
    k = {key: edge_ref[n] for n, key in enumerate(EDGE)}
    levels, cols = edge_ref.shape[1:]
    _, y = iotas((levels, cols))
    toward, drift, diffuse, beside = (
        sides(got_first_ref[n], got_second_ref[n]) for n in range(2, 6)
    )
    product, stepped, own = [], [], []
    for side in range(2):
        near_by, far_off = late_ref[2 * side], late_ref[2 * side + 1]
        b, c = drift[side], diffuse[side]
        north, south = jnp.where(y < cols - 1, c - b, 0.0), jnp.where(y > 0, c + b, 0.0)
        once = (1.0 - 4.0 * c) * near_by + beside[side] * far_off
        once = once + down(north * near_by, 1) + up(south * near_by, 1)
        product.append(toward[side] * near_by)
        stepped.append(toward[side] * once)
        row = side * (rows - 1)
        outer = [cross_ref[lev * rows + row : lev * rows + row + 1] for lev in range(levels)]
        own.append(k[("west_low", "east_high")[side]] * jnp.concatenate(outer, 0))
    for n, fix in enumerate(back_fix(k, product, stepped, own, toward)):
        fix_ref[n] = fix


def beyond_body(a_ref, b_ref, c_ref, cross_ref, back_ref):
    levels, rows, _ = a_ref.shape
    for lev in range(levels):
        coeffs = taps(a_ref[lev], b_ref[lev], c_ref[lev])
        cross = cross_ref[lev * rows : (lev + 1) * rows]
        back_ref[lev] = adjoint(adjoint(cross, coeffs), coeffs)


def thirds(x):
    one = x.astype(jnp.bfloat16)
    rest = x - one.astype(F32)
    two = rest.astype(jnp.bfloat16)
    return one, two, (rest - two.astype(F32)).astype(jnp.bfloat16)


def slot_masks(cell, lines, cols):
    slots = cell.shape[1]
    at_line = iotas((lines, slots))[0] == cell // cols
    at_col = iotas((cols, slots))[0] == lax.rem(cell, cols)
    return at_line, jnp.where(at_col, 1.0, 0.0).astype(jnp.bfloat16)


def spread_body(
    incr_ref, mult_ref, rhs_ref, err_ref, cell_ref, dual_ref, valid_ref, local_ref, held_ref
):
    levels, rows, cols = incr_ref.shape
    lines = levels * rows
    at_line, at_col = slot_masks(cell_ref[...], lines, cols)
    weights = thirds(jnp.where(at_line, valid_ref[...] * dual_ref[...], 0.0))
    spread = lax.dot_general(
        jnp.concatenate(weights, 0), at_col, (((1,), (1,)), ((), ())), preferred_element_type=F32
    )
    ht = spread[:lines] + spread[lines : 2 * lines] + spread[2 * lines :]
    mult = mult_ref[...]
    held_ref[...] = mult + ht.reshape(levels, rows, cols)
    local_ref[...] = rhs_ref[...] - (err_ref[...] * mult + incr_ref[...])


def gather_body(
    incr_ref, cell_ref, dual_ref, want_ref, var_ref, valid_ref, dir_ref, sums_ref
):
    levels, rows, cols = incr_ref.shape
    lines = levels * rows
    at_line, at_col = slot_masks(cell_ref[...], lines, cols)
    fields = thirds(incr_ref[...].reshape(lines, cols))
    picked = jnp.dot(jnp.concatenate(fields, 0), at_col, preferred_element_type=F32)
    picked = picked[:lines] + picked[lines : 2 * lines] + picked[2 * lines :]
    valid, var = valid_ref[...], var_ref[...]
    hx = jnp.sum(jnp.where(at_line, picked, 0.0), axis=0, keepdims=True) * valid
    res = valid * (want_ref[...] - (var * dual_ref[...] + hx))
    direction = res / var
    dir_ref[...] = direction
    sums_ref[0] = res * direction
    sums_ref[1] = direction * direction


def corrected(field, fix):
    rows = field.shape[0]
    i, _ = iotas(field.shape)
    for n, row in enumerate((0, 1, rows - 2, rows - 1)):
        field = field + jnp.where(i == row, fix[n], 0.0)
    return field


def fixes(ref, start, lev):
    return [ref[start + n, pl.ds(lev, 1)] for n in range(4)]


def share_body(
    first_ref, second_ref, got_first_ref, got_second_ref, edge_ref,
    local_ref, moved_ref, held_ref, back_ref, own_ref, urgent_ref, late_ref,
):
    position = lax.axis_index("tm")
    first, low_pair = lax.rem(position, 2) == 0, position < 2
    fix_moved, fix_back, beyond = edges_of(
        first_ref, second_ref, got_first_ref, got_second_ref, edge_ref
    )
    for n in range(4):
        late_ref[n] = jnp.where(low_pair, fix_moved[n], beyond[n])
    for lev in range(local_ref.shape[0]):
        back = corrected(back_ref[lev], [x[lev : lev + 1] for x in fix_back])
        moved = corrected(moved_ref[lev], [x[lev : lev + 1] for x in fix_moved])
        local = local_ref[lev]
        residual = held_ref[lev] - jnp.where(first, back, 0.0)
        own_ref[0, lev] = local
        own_ref[1, lev] = moved
        own_ref[2, lev] = residual
        urgent_ref[lev] = jnp.where(low_pair, local + moved, residual)


def sends_body(own_ref, got_ref, send_ref):
    low_pair = lax.axis_index("tm") < 2
    for lev in range(own_ref.shape[1]):
        mine = jnp.where(low_pair, own_ref[0, lev], own_ref[2, lev])
        send_ref[lev] = mine + got_ref[lev]


def rest_body(own_ref, obs_ref, *out_refs):
    levels = own_ref.shape[1]
    low_pair = lax.axis_index("tm") < 2
    blocks = [(ref, n) for ref in out_refs for n in range(ref.shape[0])]
    for lev in range(levels):
        ref, n = blocks[lev]
        ref[n] = own_ref[0, lev]
        ref, n = blocks[levels + lev]
        ref[n] = jnp.where(low_pair, own_ref[2, lev], own_ref[1, lev])
    ref, n = blocks[2 * levels]
    ref[n] = jnp.zeros(ref.shape[1:], F32)
    for i in range(2):
        ref[n, i : i + 1, 0:128] = lanes(obs_ref[i])


def terms_body(cross_ref, late_ref, beyond_ref, own_ref, got_ref, fix_ref, *refs):
    low_pair = lax.axis_index("tm") < 2
    _, levels, rows, _ = own_ref.shape
    *rest_refs, terms_ref, known_ref = refs
    blocks = [(ref, n) for ref in rest_refs for n in range(ref.shape[0])]
    for lev in range(levels):
        got = got_ref[lev]
        local, residual = own_ref[0, lev], own_ref[2, lev]
        back = corrected(beyond_ref[lev], fixes(fix_ref, 0, lev))
        moved = corrected(cross_ref[lev * rows : (lev + 1) * rows], fixes(late_ref, 0, lev))
        rest0, rest1 = (ref[n] for ref, n in (blocks[lev], blocks[levels + lev]))
        terms_ref[0, lev] = jnp.where(low_pair, rest0, residual)
        terms_ref[1, lev] = jnp.where(low_pair, local, residual) + got
        terms_ref[2, lev] = jnp.where(low_pair, residual - back, rest0 + moved)
        terms_ref[3, lev] = jnp.where(low_pair, rest1, local + rest1)
        known_ref[lev] = jnp.where(low_pair, local, residual + got)


def dots_body(terms_ref, got_ref, rest_ref, obs_ref, keep_ref, give_ref, sums_ref):
    _, levels, rows, cols = terms_ref.shape
    low_pair = lax.axis_index("tm") < 2
    numer, denom = jnp.zeros((8, 128), F32), jnp.zeros((8, 128), F32)

    def folded(x):
        total = None
        for r in range(0, rows, 8):
            part = lanes(x[r : r + 8])
            total = part if total is None else total + part
        return total

    for lev in range(levels):
        y0, one, z0, z1 = (terms_ref[n, lev] for n in range(4))
        two = got_ref[lev] + z0
        three = two + z1
        numer = numer + folded(y0 * y0 + (one - y0) * one + z0 * two + z1 * three)
        denom = denom + folded(y0 * y0 + one * one + two * two + three * three)
        keep_ref[0, lev] = jnp.where(low_pair, one, three)
        keep_ref[1, lev] = jnp.where(low_pair, two, y0)
        give_ref[lev] = jnp.where(low_pair, three, two)
    for n, total in enumerate((numer, denom)):
        obs = lanes(obs_ref[n]) + rest_ref[rest_ref.shape[0] - 1, n : n + 1, 0:128]
        sums_ref[n : n + 1] = jnp.sum(total, axis=0, keepdims=True) + obs


def update_body(
    mult_ref, incr_ref, dual_ref, dir_ref, keep_ref, known_ref, got_ref, sums_ref,
    new_m_ref, new_i_ref, new_o_ref,
):
    position = lax.axis_index("tm")
    leads, low_pair = lax.rem(position, 2) == 1, position < 2
    total = jnp.sum(sums_ref[...], axis=1, keepdims=True)
    step = total[0:1] / total[1:2]
    for lev in range(mult_ref.shape[0]):
        known, got = known_ref[lev], got_ref[lev]
        model = jnp.where(leads, keep_ref[0, lev], jnp.where(low_pair, known, got))
        back = jnp.where(leads, keep_ref[1, lev], jnp.where(low_pair, got, known))
        new_m_ref[lev] = mult_ref[lev] + step * model
        new_i_ref[lev] = incr_ref[lev] - step * back
    new_o_ref[...] = dual_ref[...] + step * dir_ref[...]


def exchange(value, partner):
    groups, tiles, peers = (lax.axis_size(x) for x in ("groups", "tile", "tm"))
    pairs = []
    for g in range(groups):
        for t in range(tiles):
            for k in range(peers):
                to_g, to_t, to_k = partner(g, t, k)
                target = (to_g * tiles + to_t) * peers + to_k
                pairs.append(((g * tiles + t) * peers + k, target))
    return lax.ppermute(value, ("groups", "tile", "tm"), pairs)


def swap(value, axis, distance):
    return lax.ppermute(value, axis, [(i, i ^ distance) for i in range(lax.axis_size(axis))])


def aside(g, t, k):
    return (g ^ 1, t, k) if lax.axis_size("groups") % 2 == 0 else (g, t ^ 1, k)


def leaders(value, tile, tm):
    return exchange(
        value, lambda g, t, k: (g, t ^ tile, k ^ tm) if k % 2 else aside(g, t, k)
    )


def next_pair(g, t, k):
    if 0 < k < lax.axis_size("tm") - 1:
        return g, t, (k - 1 if k % 2 == 0 else k + 1)
    return aside(g, t, k)


def second_side(g, t, k):
    if 0 < t < lax.axis_size("tile") - 1:
        return g, (t - 1 if t % 2 == 0 else t + 1), k
    return g, t, k ^ 1


def shifted(value, steps):
    count = lax.axis_size("tm")
    pairs = [(i, i + steps) for i in range(count) if 0 <= i + steps < count]
    return lax.ppermute(value, "tm", pairs)


def scanned(value, direction):
    reach = 1
    while reach < lax.axis_size("tm"):
        value = value + shifted(value, direction * reach)
        reach *= 2
    return value


def reduced(value, axis):
    distance = 1
    while distance < lax.axis_size(axis):
        value = value + swap(value, axis, distance)
        distance *= 2
    return value


def near(*arrays):
    return [(x, "near") for x in arrays]


def shards(
    multiplier, increment, obs_dual, rhs_model, rhs_obs, model_err, obs_err,
    drift_east, drift_north, diffusion, obs_cell, obs_count,
):
    tiles, peers = lax.axis_size("tile"), lax.axis_size("tm")
    levels, rows, cols = multiplier.shape[1:]
    field = ((levels, rows, cols), "near")
    lines = lambda n: ((n, levels, cols), "near")

    inner = swap(multiplier[0], "tm", 1)
    arguments = [increment[0], drift_east[0], drift_north[0], diffusion[0], multiplier[0]]
    arguments += [rhs_model[0], model_err[0], obs_cell, obs_dual, rhs_obs, obs_err]
    count = len(arguments)
    *here, once, high, low, edge = kernel_call(
        lambda *refs: begin_body(count, *refs),
        "begin",
        [(x, "far") for x in arguments],
        [(x.shape, "near", x.dtype) for x in arguments]
        + [field, lines(5), lines(5), lines(len(EDGE))],
        [pltpu.SemaphoreType.DMA((count + 4 * (PARTS - 1),))],
    )
    incr, *coeffs = here[:4]
    mult, rhs, err, cell, dual, want, var = here[4:]
    four = peers == 4
    if four:
        later = inner
    else:
        later = jnp.where(lax.axis_index("tm") % 2 == 0, inner, exchange(mult, next_pair))
    first, second = kernel_call(
        lambda *refs: rims_body(four, *refs),
        "rims",
        near(edge, later, high, low),
        [lines(6), lines(6)],
    )
    got_front = exchange(second, lambda g, t, k: (g, t ^ 1, k) if t % 4 < 2 else (g, t, k ^ 1))
    once, second = lax.optimization_barrier((once, second))
    moved = kernel_call(forward_body, "forward", near(*coeffs, once), [field])[0]
    moved, first, second, incr = lax.optimization_barrier((moved, first, second, incr))
    got_first = exchange(first, second_side)
    got_back = exchange(second, lambda g, t, k: (g, t, k ^ 1) if t % 4 < 2 else (g, t ^ 1, k))
    got_second = jnp.where(lax.axis_index("tile") % 4 < 2, got_front, got_back)
    valid = (lax.broadcasted_iota(jnp.int32, obs_cell.shape, 1) < obs_count).astype(F32)
    local, held = kernel_call(
        spread_body, "spread", near(incr, mult, rhs, err, cell, dual, valid), [field] * 2
    )
    rims = near(first, second, got_first, got_second, edge)
    if not four:
        fix = kernel_call(edges_body, "edges", rims, [lines(8)])[0]
        later = jnp.where(lax.axis_index("tm") == peers - 1, 0.0, later)
        back = kernel_call(adjoint_body, "adjoint", near(*coeffs, later), [field])[0]
        dir_obs, obs_sums = kernel_call(
            gather_body,
            "gather",
            near(incr, cell, dual, want, var, valid),
            [(obs_dual.shape, "near"), ((2, *obs_dual.shape), "near")],
        )
        return scan_path(
            multiplier, increment, obs_dual, local, moved, held, back, fix, dir_obs, obs_sums
        )
    cross = jnp.where(lax.axis_index("tm") < 2, moved, inner).reshape(levels * rows, cols)
    got_cross = leaders(jnp.pad(cross, ((0, rows), (0, 0))), 0, 2)
    back = kernel_call(adjoint_body, "adjoint", near(*coeffs, inner), [field])[0]
    own, urgent, late = kernel_call(
        share_body,
        "share",
        rims + near(local, moved, held, back),
        [((3, levels, rows, cols), "near"), field, lines(4)],
    )
    got_late = leaders(late, 0, 2)
    got = swap(urgent, "tm", 1)
    send = kernel_call(sends_body, "sends", near(own, got), [field])[0]
    send, own, cell = lax.optimization_barrier((send, own, cell))
    got_send = leaders(send, 0, 2)
    dir_obs, obs_sums = kernel_call(
        gather_body,
        "gather",
        near(incr, cell, dual, want, var, valid),
        [(obs_dual.shape, "near"), ((2, *obs_dual.shape), "near")],
    )
    parts = [-(-(2 * levels + 1) // 3)] * 2
    parts.append(2 * levels + 1 - sum(parts))
    rest = kernel_call(
        rest_body, "rest", near(own, obs_sums), [((n, rows, cols), "near") for n in parts]
    )
    got_rest = [swap(x, "tm", 1) for x in rest]
    late_fix = kernel_call(
        lambda *refs: late_body(rows, *refs),
        "late",
        near(got_first, got_second, edge, got_cross, got_late),
        [lines(4)],
        weight=WEIGHT,
    )[0]
    beyond = kernel_call(beyond_body, "beyond", near(*coeffs, got_cross), [field])[0]
    terms, known = kernel_call(
        terms_body,
        "terms",
        near(got_cross, got_late, beyond, own, got, late_fix, *got_rest),
        [((4, levels, rows, cols), "near"), field],
    )
    pair = ((2, levels, rows, cols), "near")
    keep, give, sums = kernel_call(
        dots_body, "dots", near(terms, got_send, got_rest[-1], obs_sums), [pair, field, ((2, 128), "near")]
    )
    total = sums + leaders(sums, 0, 2) + leaders(sums, 1, 0) + leaders(sums, 1, 2)
    distance = 2
    while distance < tiles:
        total = total + leaders(total, distance, 0)
        distance *= 2
    got_dir = swap(give, "tm", 1)
    other = swap(total, "tm", 1)
    total = jnp.where(lax.axis_index("tm") % 2 == 1, total, other)
    new_m, new_i, new_o = kernel_call(
        update_body,
        "update",
        near(mult, incr, dual, dir_obs, keep, known, got_dir, total),
        [(mult.shape, "far"), (mult.shape, "far"), (obs_dual.shape, "far")],
    )
    return new_m[None], new_i[None], new_o


def scan_path(multiplier, increment, obs_dual, local, moved, held, back, fix, dir_obs, obs_sums):
    rows = local.shape[1]
    fix = jnp.moveaxis(fix, 0, 1)
    at = jnp.array([0, 1, rows - 2, rows - 1])
    moved = moved.at[:, at].add(fix[:, :4])
    res_incr = -(held - back.at[:, at].add(fix[:, 4:8]))
    res_model = local + shifted(moved, 1)
    dir_model, dir_incr = scanned(res_model, 1), scanned(res_incr, -1)
    numer = jnp.sum(res_model * dir_model) + jnp.sum(res_incr * dir_incr) + jnp.sum(obs_sums[0])
    denom = jnp.sum(dir_model**2) + jnp.sum(dir_incr**2) + jnp.sum(obs_sums[1])
    sums = reduced(reduced(jnp.stack([numer, denom]), "tm"), "tile")
    step = sums[0] / sums[1]
    return (
        multiplier + step * dir_model[None],
        increment + step * dir_incr[None],
        obs_dual + step * dir_obs,
    )


def solution(mesh):
    grid = P(("groups", "tm"), None, "tile", None)
    line = P(("groups", "tm"), "tile")
    return jax.shard_map(
        shards,
        mesh=mesh,
        in_specs=(grid, grid, line, grid, line, grid, line, grid, grid, grid, line, line),
        out_specs=(grid, grid, line),
        check_vma=False,
    )
```

```python
import jax
import jax.numpy as jnp
from jax import lax
from jax.experimental import pallas as pl
from jax.experimental.pallas import tpu as pltpu
from jax.sharding import PartitionSpec as P

F32 = jnp.float32
VMEM = pltpu.VMEM
GRANT = 24 * 1024 * 1024
WEIGHT = 2600000000
PARTS = 2


def kernel_call(body, name, inputs, outputs, scratch=(), weight=1):
    arrays, in_specs = [], []
    for array, home in inputs:
        if home == "far":
            in_specs.append(pl.BlockSpec(memory_space=pltpu.HBM))
            array = pltpu.with_memory_space_constraint(array, pltpu.HBM)
        else:
            in_specs.append(pl.BlockSpec(memory_space=VMEM))
            array = pltpu.with_memory_space_constraint(array, VMEM)
        arrays.append(array)
    out_shape, out_specs = [], []
    for shape, home, *dtype in outputs:
        dtype = dtype[0] if dtype else F32
        out_specs.append(pl.BlockSpec(memory_space=VMEM))
        out_shape.append(
            VMEM(shape, dtype) if home == "near" else jax.ShapeDtypeStruct(shape, dtype)
        )
    return pl.pallas_call(
        body,
        name=name,
        out_shape=out_shape,
        in_specs=in_specs,
        out_specs=out_specs,
        scratch_shapes=list(scratch),
        cost_estimate=pl.CostEstimate(flops=weight, bytes_accessed=1, transcendentals=0),
        compiler_params=pltpu.CompilerParams(vmem_limit_bytes=GRANT),
    )(*arrays)


def lanes(row):
    total = row[:, 0:128]
    for col in range(128, row.shape[1], 128):
        total = total + row[:, col : col + 128]
    return total


def iotas(shape):
    return (
        lax.broadcasted_iota(jnp.int32, shape, 0),
        lax.broadcasted_iota(jnp.int32, shape, 1),
    )


def up(field, axis):
    return pltpu.roll(field, field.shape[axis] - 1, axis)


def down(field, axis):
    return pltpu.roll(field, 1, axis)


def taps(a, b, c):
    i, y = iotas(a.shape)
    rows, cols = a.shape
    return (
        1.0 - 4.0 * c,
        jnp.where(i < rows - 1, c - a, 0.0),
        jnp.where(i > 0, c + a, 0.0),
        jnp.where(y < cols - 1, c - b, 0.0),
        jnp.where(y > 0, c + b, 0.0),
    )


def forward(state, coeffs):
    mid, east, west, north, south = coeffs
    return (
        mid * state
        + east * up(state, 0)
        + west * down(state, 0)
        + north * up(state, 1)
        + south * down(state, 1)
    )


def adjoint(state, coeffs):
    mid, east, west, north, south = coeffs
    return (
        mid * state
        + down(east * state, 0)
        + up(west * state, 0)
        + down(north * state, 1)
        + up(south * state, 1)
    )


EDGE = ("mid_low", "mid_high", "north_low", "north_high", "south_low", "south_high")
EDGE += ("west_low", "west_next", "east_high", "east_next", "east_low", "west_high")


def begin_body(count, *refs):
    sources, targets = refs[:count], refs[count : 2 * count]
    once_ref, high_ref, low_ref, edge_ref, sems = refs[2 * count :]
    s_ref, a_ref, b_ref, c_ref = targets[:4]
    levels, rows, _ = s_ref.shape
    last = rows - 1
    cut = levels // PARTS
    parts = [
        [
            pltpu.make_async_copy(
                sources[n].at[pl.ds(part * cut, cut)],
                targets[n].at[pl.ds(part * cut, cut)],
                sems.at[part * 4 + n],
            )
            for n in range(4)
        ]
        for part in range(PARTS)
    ]
    rest = [
        pltpu.make_async_copy(sources[n], targets[n], sems.at[4 * (PARTS - 1) + n])
        for n in range(4, count)
    ]
    for copy in sum(parts, []) + rest:
        copy.start()
    for lev in range(levels):
        if lev % cut == 0:
            for copy in parts[lev // cut]:
                copy.wait()
        s, a, b, c = s_ref[lev], a_ref[lev], b_ref[lev], c_ref[lev]
        coeffs = taps(a, b, c)
        once = forward(s, coeffs)
        once_ref[lev] = once
        mid, east, west, north, south = coeffs
        at = pl.ds(lev, 1)
        open_east = c[last : last + 1] - a[last : last + 1]
        open_west = c[0:1] + a[0:1]
        high_ref[0, at] = s[last : last + 1]
        high_ref[1, at] = once[last : last + 1]
        high_ref[2, at] = open_east
        high_ref[3, at] = b[last : last + 1]
        high_ref[4, at] = c[last : last + 1]
        low_ref[0, at] = s[0:1]
        low_ref[1, at] = once[0:1]
        low_ref[2, at] = open_west
        low_ref[3, at] = b[0:1]
        low_ref[4, at] = c[0:1]
        rows_of = {
            "mid_low": mid[0:1],
            "mid_high": mid[last : last + 1],
            "north_low": north[0:1],
            "north_high": north[last : last + 1],
            "south_low": south[0:1],
            "south_high": south[last : last + 1],
            "west_low": open_west,
            "west_next": west[1:2],
            "east_high": open_east,
            "east_next": east[last - 1 : last],
            "east_low": east[0:1],
            "west_high": west[last : last + 1],
        }
        for n, key in enumerate(EDGE):
            edge_ref[n, at] = rows_of[key]
    for copy in rest:
        copy.wait()


def forward_body(a_ref, b_ref, c_ref, once_ref, moved_ref):
    for lev in range(a_ref.shape[0]):
        coeffs = taps(a_ref[lev], b_ref[lev], c_ref[lev])
        moved_ref[lev] = forward(once_ref[lev], coeffs)


def adjoint_body(a_ref, b_ref, c_ref, later_ref, back_ref):
    for lev in range(a_ref.shape[0]):
        coeffs = taps(a_ref[lev], b_ref[lev], c_ref[lev])
        back_ref[lev] = adjoint(adjoint(later_ref[lev], coeffs), coeffs)


def outer_products(k, later):
    def once(side, at, beside):
        mid, north, south = k["mid_" + side], k["north_" + side], k["south_" + side]
        return mid * at + beside + down(north * at, 1) + up(south * at, 1)

    west, east = k["west_low"], k["east_high"]
    return (
        (west * later[0], west * once("low", later[0], k["west_next"] * later[1])),
        (east * later[3], east * once("high", later[3], k["east_next"] * later[2])),
    )


def rims_body(four, edge_ref, later_ref, high_ref, low_ref, first_ref, second_ref):
    position, peers = lax.axis_index("tm"), lax.axis_size("tm")
    odd = lax.rem(lax.axis_index("tile") + 1, 2)
    k = {key: edge_ref[n] for n, key in enumerate(EDGE)}
    levels, rows, _ = later_ref.shape
    later = [
        jnp.concatenate([later_ref[lev, row : row + 1] for lev in range(levels)], 0)
        for row in (0, 1, rows - 2, rows - 1)
    ]
    products = outer_products(k, later)
    zero = jnp.zeros(later[0].shape, F32)
    sent = []
    for ref, product, outer, inside, beside in (
        (low_ref, products[0], later[0], later[1], k["west_next"]),
        (high_ref, products[1], later[3], later[2], k["east_next"]),
    ):
        out = [ref[0], ref[1], ref[2], *product, zero]
        if four:
            second, final = position == 1, position == peers - 1
            out[0] = jnp.where(final, outer, out[0])
            out[1] = jnp.where(final, inside, out[1])
            out[3] = jnp.where(second, ref[3], out[3])
            out[4] = jnp.where(second, ref[4], out[4])
            out[5] = jnp.where(second, beside, zero)
        sent.append(out)
    for n, (low, high) in enumerate(zip(*sent)):
        first_ref[n] = jnp.where(odd == 0, high, low)
        second_ref[n] = jnp.where(odd == 0, low, high)


def sides(first, second):
    tile, tiles = lax.axis_index("tile"), lax.axis_size("tile")
    odd = lax.rem(tile + 1, 2)
    below, above = jnp.where(odd == 0, second, first), jnp.where(odd == 0, first, second)
    return jnp.where(tile > 0, below, 0.0), jnp.where(tile < tiles - 1, above, 0.0)


def own_sides(first, second):
    odd = lax.rem(lax.axis_index("tile") + 1, 2)
    return jnp.where(odd == 0, second, first), jnp.where(odd == 0, first, second)


def back_fix(k, product, stepped, own_product, toward):
    def across(x, side):
        mid, north, south = k["mid_" + side], k["north_" + side], k["south_" + side]
        return mid * x + down(north * x, 1) + up(south * x, 1)

    return (
        across(product[0], "low") + (stepped[0] + toward[0] * own_product[0]),
        k["east_low"] * product[0],
        k["west_high"] * product[1],
        across(product[1], "high") + (stepped[1] + toward[1] * own_product[1]),
    )


def edges_of(first_ref, second_ref, got_first_ref, got_second_ref, edge_ref):
    k = {key: edge_ref[n] for n, key in enumerate(EDGE)}
    state, stepped, toward, product, product_stepped = (
        sides(got_first_ref[n], got_second_ref[n]) for n in range(5)
    )
    own_state = own_sides(first_ref[0], second_ref[0])
    own_product = own_sides(first_ref[3], second_ref[3])

    def along(x, side):
        mid, north, south = k["mid_" + side], k["north_" + side], k["south_" + side]
        return mid * x + north * up(x, 1) + south * down(x, 1)

    new_low, new_high = k["west_low"] * state[0], k["east_high"] * state[1]
    moved = (
        along(new_low, "low") + k["west_low"] * (stepped[0] + toward[0] * own_state[0]),
        k["west_next"] * new_low,
        k["east_next"] * new_high,
        along(new_high, "high") + k["east_high"] * (stepped[1] + toward[1] * own_state[1]),
    )
    back = back_fix(k, product, product_stepped, own_product, toward)
    return moved, back, (state[0], stepped[0], state[1], stepped[1])


def edges_body(*refs):
    *in_refs, fix_ref = refs
    moved, back, _ = edges_of(*in_refs)
    wanted = lax.axis_index("tm") < lax.axis_size("tm") - 1
    for n in range(4):
        fix_ref[n] = moved[n]
        fix_ref[4 + n] = jnp.where(wanted, back[n], 0.0)


def late_body(rows, got_first_ref, got_second_ref, edge_ref, cross_ref, late_ref, fix_ref):
    k = {key: edge_ref[n] for n, key in enumerate(EDGE)}
    levels, cols = edge_ref.shape[1:]
    _, y = iotas((levels, cols))
    toward, drift, diffuse, beside = (
        sides(got_first_ref[n], got_second_ref[n]) for n in range(2, 6)
    )
    product, stepped, own = [], [], []
    for side in range(2):
        near_by, far_off = late_ref[2 * side], late_ref[2 * side + 1]
        b, c = drift[side], diffuse[side]
        north, south = jnp.where(y < cols - 1, c - b, 0.0), jnp.where(y > 0, c + b, 0.0)
        once = (1.0 - 4.0 * c) * near_by + beside[side] * far_off
        once = once + down(north * near_by, 1) + up(south * near_by, 1)
        product.append(toward[side] * near_by)
        stepped.append(toward[side] * once)
        row = side * (rows - 1)
        outer = [cross_ref[lev * rows + row : lev * rows + row + 1] for lev in range(levels)]
        own.append(k[("west_low", "east_high")[side]] * jnp.concatenate(outer, 0))
    for n, fix in enumerate(back_fix(k, product, stepped, own, toward)):
        fix_ref[n] = fix


def beyond_body(a_ref, b_ref, c_ref, cross_ref, back_ref):
    levels, rows, _ = a_ref.shape
    for lev in range(levels):
        coeffs = taps(a_ref[lev], b_ref[lev], c_ref[lev])
        cross = cross_ref[lev * rows : (lev + 1) * rows]
        back_ref[lev] = adjoint(adjoint(cross, coeffs), coeffs)


def thirds(x):
    one = x.astype(jnp.bfloat16)
    rest = x - one.astype(F32)
    two = rest.astype(jnp.bfloat16)
    return one, two, (rest - two.astype(F32)).astype(jnp.bfloat16)


def slot_masks(cell, lines, cols):
    slots = cell.shape[1]
    at_line = iotas((lines, slots))[0] == cell // cols
    at_col = iotas((cols, slots))[0] == lax.rem(cell, cols)
    return at_line, jnp.where(at_col, 1.0, 0.0).astype(jnp.bfloat16)


def spread_body(
    incr_ref, mult_ref, rhs_ref, err_ref, cell_ref, dual_ref, valid_ref, local_ref, held_ref
):
    levels, rows, cols = incr_ref.shape
    lines = levels * rows
    at_line, at_col = slot_masks(cell_ref[...], lines, cols)
    weights = thirds(jnp.where(at_line, valid_ref[...] * dual_ref[...], 0.0))
    spread = lax.dot_general(
        jnp.concatenate(weights, 0), at_col, (((1,), (1,)), ((), ())), preferred_element_type=F32
    )
    ht = spread[:lines] + spread[lines : 2 * lines] + spread[2 * lines :]
    mult = mult_ref[...]
    held_ref[...] = mult + ht.reshape(levels, rows, cols)
    local_ref[...] = rhs_ref[...] - (err_ref[...] * mult + incr_ref[...])


def gather_body(
    incr_ref, cell_ref, dual_ref, want_ref, var_ref, valid_ref, dir_ref, sums_ref
):
    levels, rows, cols = incr_ref.shape
    lines = levels * rows
    at_line, at_col = slot_masks(cell_ref[...], lines, cols)
    fields = thirds(incr_ref[...].reshape(lines, cols))
    picked = jnp.dot(jnp.concatenate(fields, 0), at_col, preferred_element_type=F32)
    picked = picked[:lines] + picked[lines : 2 * lines] + picked[2 * lines :]
    valid, var = valid_ref[...], var_ref[...]
    hx = jnp.sum(jnp.where(at_line, picked, 0.0), axis=0, keepdims=True) * valid
    res = valid * (want_ref[...] - (var * dual_ref[...] + hx))
    direction = res / var
    dir_ref[...] = direction
    sums_ref[0] = res * direction
    sums_ref[1] = direction * direction


def corrected(field, fix):
    rows = field.shape[0]
    i, _ = iotas(field.shape)
    for n, row in enumerate((0, 1, rows - 2, rows - 1)):
        field = field + jnp.where(i == row, fix[n], 0.0)
    return field


def fixes(ref, start, lev):
    return [ref[start + n, pl.ds(lev, 1)] for n in range(4)]


def share_body(
    first_ref, second_ref, got_first_ref, got_second_ref, edge_ref,
    local_ref, moved_ref, held_ref, back_ref, own_ref, urgent_ref, late_ref,
):
    position = lax.axis_index("tm")
    first, low_pair = lax.rem(position, 2) == 0, position < 2
    fix_moved, fix_back, beyond = edges_of(
        first_ref, second_ref, got_first_ref, got_second_ref, edge_ref
    )
    for n in range(4):
        late_ref[n] = jnp.where(low_pair, fix_moved[n], beyond[n])
    for lev in range(local_ref.shape[0]):
        back = corrected(back_ref[lev], [x[lev : lev + 1] for x in fix_back])
        moved = corrected(moved_ref[lev], [x[lev : lev + 1] for x in fix_moved])
        local = local_ref[lev]
        residual = held_ref[lev] - jnp.where(first, back, 0.0)
        own_ref[0, lev] = local
        own_ref[1, lev] = moved
        own_ref[2, lev] = residual
        urgent_ref[lev] = jnp.where(low_pair, local + moved, residual)


def sends_body(own_ref, got_ref, send_ref):
    low_pair = lax.axis_index("tm") < 2
    for lev in range(own_ref.shape[1]):
        mine = jnp.where(low_pair, own_ref[0, lev], own_ref[2, lev])
        send_ref[lev] = mine + got_ref[lev]


def rest_body(own_ref, obs_ref, *out_refs):
    levels = own_ref.shape[1]
    low_pair = lax.axis_index("tm") < 2
    blocks = [(ref, n) for ref in out_refs for n in range(ref.shape[0])]
    for lev in range(levels):
        ref, n = blocks[lev]
        ref[n] = own_ref[0, lev]
        ref, n = blocks[levels + lev]
        ref[n] = jnp.where(low_pair, own_ref[2, lev], own_ref[1, lev])
    ref, n = blocks[2 * levels]
    ref[n] = jnp.zeros(ref.shape[1:], F32)
    for i in range(2):
        ref[n, i : i + 1, 0:128] = lanes(obs_ref[i])


def terms_body(cross_ref, late_ref, beyond_ref, own_ref, got_ref, fix_ref, *refs):
    low_pair = lax.axis_index("tm") < 2
    _, levels, rows, _ = own_ref.shape
    *rest_refs, terms_ref, known_ref = refs
    blocks = [(ref, n) for ref in rest_refs for n in range(ref.shape[0])]
    for lev in range(levels):
        got = got_ref[lev]
        local, residual = own_ref[0, lev], own_ref[2, lev]
        back = corrected(beyond_ref[lev], fixes(fix_ref, 0, lev))
        moved = corrected(cross_ref[lev * rows : (lev + 1) * rows], fixes(late_ref, 0, lev))
        rest0, rest1 = (ref[n] for ref, n in (blocks[lev], blocks[levels + lev]))
        terms_ref[0, lev] = jnp.where(low_pair, rest0, residual)
        terms_ref[1, lev] = jnp.where(low_pair, local, residual) + got
        terms_ref[2, lev] = jnp.where(low_pair, residual - back, rest0 + moved)
        terms_ref[3, lev] = jnp.where(low_pair, rest1, local + rest1)
        known_ref[lev] = jnp.where(low_pair, local, residual + got)


def folded(x):
    total = None
    for r in range(0, x.shape[0], 8):
        part = lanes(x[r : r + 8])
        total = part if total is None else total + part
    return total


def early_body(terms_ref, rest_ref, obs_ref, sums_ref):
    levels, last = terms_ref.shape[1], rest_ref.shape[0] - 1
    numer, denom = jnp.zeros((8, 128), F32), jnp.zeros((8, 128), F32)
    for lev in range(levels):
        y0, one = terms_ref[0, lev], terms_ref[1, lev]
        numer = numer + folded(y0 * y0 + (one - y0) * one)
        denom = denom + folded(y0 * y0 + one * one)
    for n, total in enumerate((numer, denom)):
        obs = lanes(obs_ref[n]) + rest_ref[last, n : n + 1, 0:128]
        sums_ref[n : n + 1] = jnp.sum(total, axis=0, keepdims=True) + obs


def dots_body(terms_ref, got_ref, early_ref, sums_ref):
    numer, denom = jnp.zeros((8, 128), F32), jnp.zeros((8, 128), F32)
    for lev in range(got_ref.shape[0]):
        z0, z1 = terms_ref[2, lev], terms_ref[3, lev]
        two = got_ref[lev] + z0
        three = two + z1
        numer = numer + folded(z0 * two + z1 * three)
        denom = denom + folded(two * two + three * three)
    for n, total in enumerate((numer, denom)):
        sums_ref[n : n + 1] = early_ref[n : n + 1] + jnp.sum(total, axis=0, keepdims=True)


def directions_body(terms_ref, got_ref, keep_ref, give_ref):
    low_pair = lax.axis_index("tm") < 2
    for lev in range(got_ref.shape[0]):
        y0, one, z0, z1 = (terms_ref[n, lev] for n in range(4))
        two = got_ref[lev] + z0
        three = two + z1
        keep_ref[0, lev] = jnp.where(low_pair, one, three)
        keep_ref[1, lev] = jnp.where(low_pair, two, y0)
        give_ref[lev] = jnp.where(low_pair, three, two)


def update_body(
    mult_ref, incr_ref, dual_ref, dir_ref, keep_ref, known_ref, got_ref, sums_ref,
    new_m_ref, new_i_ref, new_o_ref,
):
    position = lax.axis_index("tm")
    leads, low_pair = lax.rem(position, 2) == 1, position < 2
    total = jnp.sum(sums_ref[...], axis=1, keepdims=True)
    step = total[0:1] / total[1:2]
    for lev in range(mult_ref.shape[0]):
        known, got = known_ref[lev], got_ref[lev]
        model = jnp.where(leads, keep_ref[0, lev], jnp.where(low_pair, known, got))
        back = jnp.where(leads, keep_ref[1, lev], jnp.where(low_pair, got, known))
        new_m_ref[lev] = mult_ref[lev] + step * model
        new_i_ref[lev] = incr_ref[lev] - step * back
    new_o_ref[...] = dual_ref[...] + step * dir_ref[...]


def exchange(value, partner):
    groups, tiles, peers = (lax.axis_size(x) for x in ("groups", "tile", "tm"))
    pairs = []
    for g in range(groups):
        for t in range(tiles):
            for k in range(peers):
                to_g, to_t, to_k = partner(g, t, k)
                target = (to_g * tiles + to_t) * peers + to_k
                pairs.append(((g * tiles + t) * peers + k, target))
    return lax.ppermute(value, ("groups", "tile", "tm"), pairs)


def swap(value, axis, distance):
    return lax.ppermute(value, axis, [(i, i ^ distance) for i in range(lax.axis_size(axis))])


def aside(g, t, k):
    return (g ^ 1, t, k) if lax.axis_size("groups") % 2 == 0 else (g, t ^ 1, k)


def leaders(value, tile, tm):
    return exchange(
        value, lambda g, t, k: (g, t ^ tile, k ^ tm) if k % 2 else aside(g, t, k)
    )


def next_pair(g, t, k):
    if 0 < k < lax.axis_size("tm") - 1:
        return g, t, (k - 1 if k % 2 == 0 else k + 1)
    return aside(g, t, k)


def second_side(g, t, k):
    if 0 < t < lax.axis_size("tile") - 1:
        return g, (t - 1 if t % 2 == 0 else t + 1), k
    return g, t, k ^ 1


def shifted(value, steps):
    count = lax.axis_size("tm")
    pairs = [(i, i + steps) for i in range(count) if 0 <= i + steps < count]
    return lax.ppermute(value, "tm", pairs)


def scanned(value, direction):
    reach = 1
    while reach < lax.axis_size("tm"):
        value = value + shifted(value, direction * reach)
        reach *= 2
    return value


def reduced(value, axis):
    distance = 1
    while distance < lax.axis_size(axis):
        value = value + swap(value, axis, distance)
        distance *= 2
    return value


def near(*arrays):
    return [(x, "near") for x in arrays]


def shards(
    multiplier, increment, obs_dual, rhs_model, rhs_obs, model_err, obs_err,
    drift_east, drift_north, diffusion, obs_cell, obs_count,
):
    tiles, peers = lax.axis_size("tile"), lax.axis_size("tm")
    levels, rows, cols = multiplier.shape[1:]
    field = ((levels, rows, cols), "near")
    lines = lambda n: ((n, levels, cols), "near")

    inner = swap(multiplier[0], "tm", 1)
    arguments = [increment[0], drift_east[0], drift_north[0], diffusion[0], multiplier[0]]
    arguments += [rhs_model[0], model_err[0], obs_cell, obs_dual, rhs_obs, obs_err]
    count = len(arguments)
    *here, once, high, low, edge = kernel_call(
        lambda *refs: begin_body(count, *refs),
        "begin",
        [(x, "far") for x in arguments],
        [(x.shape, "near", x.dtype) for x in arguments]
        + [field, lines(5), lines(5), lines(len(EDGE))],
        [pltpu.SemaphoreType.DMA((count + 4 * (PARTS - 1),))],
    )
    incr, *coeffs = here[:4]
    mult, rhs, err, cell, dual, want, var = here[4:]
    four = peers == 4
    if four:
        later = inner
    else:
        later = jnp.where(lax.axis_index("tm") % 2 == 0, inner, exchange(mult, next_pair))
    first, second = kernel_call(
        lambda *refs: rims_body(four, *refs),
        "rims",
        near(edge, later, high, low),
        [lines(6), lines(6)],
    )
    got_front = exchange(second, lambda g, t, k: (g, t ^ 1, k) if t % 4 < 2 else (g, t, k ^ 1))
    once, second = lax.optimization_barrier((once, second))
    moved = kernel_call(forward_body, "forward", near(*coeffs, once), [field])[0]
    moved, first, second, incr = lax.optimization_barrier((moved, first, second, incr))
    got_first = exchange(first, second_side)
    got_back = exchange(second, lambda g, t, k: (g, t, k ^ 1) if t % 4 < 2 else (g, t ^ 1, k))
    got_second = jnp.where(lax.axis_index("tile") % 4 < 2, got_front, got_back)
    valid = (lax.broadcasted_iota(jnp.int32, obs_cell.shape, 1) < obs_count).astype(F32)
    local, held = kernel_call(
        spread_body, "spread", near(incr, mult, rhs, err, cell, dual, valid), [field] * 2
    )
    rims = near(first, second, got_first, got_second, edge)
    if not four:
        fix = kernel_call(edges_body, "edges", rims, [lines(8)])[0]
        later = jnp.where(lax.axis_index("tm") == peers - 1, 0.0, later)
        back = kernel_call(adjoint_body, "adjoint", near(*coeffs, later), [field])[0]
        dir_obs, obs_sums = kernel_call(
            gather_body,
            "gather",
            near(incr, cell, dual, want, var, valid),
            [(obs_dual.shape, "near"), ((2, *obs_dual.shape), "near")],
        )
        return scan_path(
            multiplier, increment, obs_dual, local, moved, held, back, fix, dir_obs, obs_sums
        )
    cross = jnp.where(lax.axis_index("tm") < 2, moved, inner).reshape(levels * rows, cols)
    got_cross = leaders(jnp.pad(cross, ((0, rows), (0, 0))), 0, 2)
    back = kernel_call(adjoint_body, "adjoint", near(*coeffs, inner), [field])[0]
    own, urgent, late = kernel_call(
        share_body,
        "share",
        rims + near(local, moved, held, back),
        [((3, levels, rows, cols), "near"), field, lines(4)],
    )
    got_late = leaders(late, 0, 2)
    got = swap(urgent, "tm", 1)
    send = kernel_call(sends_body, "sends", near(own, got), [field])[0]
    send, own, cell = lax.optimization_barrier((send, own, cell))
    got_send = leaders(send, 0, 2)
    dir_obs, obs_sums = kernel_call(
        gather_body,
        "gather",
        near(incr, cell, dual, want, var, valid),
        [(obs_dual.shape, "near"), ((2, *obs_dual.shape), "near")],
    )
    parts = [-(-(2 * levels + 1) // 3)] * 2
    parts.append(2 * levels + 1 - sum(parts))
    rest = kernel_call(
        rest_body, "rest", near(own, obs_sums), [((n, rows, cols), "near") for n in parts]
    )
    got_rest = [swap(x, "tm", 1) for x in rest]
    late_fix = kernel_call(
        lambda *refs: late_body(rows, *refs),
        "late",
        near(got_first, got_second, edge, got_cross, got_late),
        [lines(4)],
        weight=WEIGHT,
    )[0]
    beyond = kernel_call(beyond_body, "beyond", near(*coeffs, got_cross), [field])[0]
    terms, known = kernel_call(
        terms_body,
        "terms",
        near(got_cross, got_late, beyond, own, got, late_fix, *got_rest),
        [((4, levels, rows, cols), "near"), field],
    )
    pair = ((2, levels, rows, cols), "near")
    line = ((2, 128), "near")
    early = kernel_call(early_body, "early", near(terms, got_rest[-1], obs_sums), [line])[0]
    sums = kernel_call(dots_body, "dots", near(terms, got_send, early), [line])[0]
    terms, got_send, sums = lax.optimization_barrier((terms, got_send, sums))
    keep, give = kernel_call(
        directions_body, "directions", near(terms, got_send), [pair, field]
    )
    total = sums + leaders(sums, 0, 2) + leaders(sums, 1, 0) + leaders(sums, 1, 2)
    distance = 2
    while distance < tiles:
        total = total + leaders(total, distance, 0)
        distance *= 2
    got_dir = swap(give, "tm", 1)
    other = swap(total, "tm", 1)
    total = jnp.where(lax.axis_index("tm") % 2 == 1, total, other)
    new_m, new_i, new_o = kernel_call(
        update_body,
        "update",
        near(mult, incr, dual, dir_obs, keep, known, got_dir, total),
        [(mult.shape, "far"), (mult.shape, "far"), (obs_dual.shape, "far")],
    )
    return new_m[None], new_i[None], new_o


def scan_path(multiplier, increment, obs_dual, local, moved, held, back, fix, dir_obs, obs_sums):
    rows = local.shape[1]
    fix = jnp.moveaxis(fix, 0, 1)
    at = jnp.array([0, 1, rows - 2, rows - 1])
    moved = moved.at[:, at].add(fix[:, :4])
    res_incr = -(held - back.at[:, at].add(fix[:, 4:8]))
    res_model = local + shifted(moved, 1)
    dir_model, dir_incr = scanned(res_model, 1), scanned(res_incr, -1)
    numer = jnp.sum(res_model * dir_model) + jnp.sum(res_incr * dir_incr) + jnp.sum(obs_sums[0])
    denom = jnp.sum(dir_model**2) + jnp.sum(dir_incr**2) + jnp.sum(obs_sums[1])
    sums = reduced(reduced(jnp.stack([numer, denom]), "tm"), "tile")
    step = sums[0] / sums[1]
    return (
        multiplier + step * dir_model[None],
        increment + step * dir_incr[None],
        obs_dual + step * dir_obs,
    )


def solution(mesh):
    grid = P(("groups", "tm"), None, "tile", None)
    line = P(("groups", "tm"), "tile")
    return jax.shard_map(
        shards,
        mesh=mesh,
        in_specs=(grid, grid, line, grid, line, grid, line, grid, grid, grid, line, line),
        out_specs=(grid, grid, line),
        check_vma=False,
    )
```

```python
import jax
import jax.numpy as jnp
from jax import lax
from jax.experimental import pallas as pl
from jax.experimental.pallas import tpu as pltpu
from jax.sharding import PartitionSpec as P

F32 = jnp.float32
VMEM = pltpu.VMEM
GRANT = 24 * 1024 * 1024
WEIGHT = 2600000000
PARTS = 2


def kernel_call(body, name, inputs, outputs, scratch=(), weight=1):
    arrays, in_specs = [], []
    for array, home in inputs:
        if home == "far":
            in_specs.append(pl.BlockSpec(memory_space=pltpu.HBM))
            array = pltpu.with_memory_space_constraint(array, pltpu.HBM)
        else:
            in_specs.append(pl.BlockSpec(memory_space=VMEM))
            array = pltpu.with_memory_space_constraint(array, VMEM)
        arrays.append(array)
    out_shape, out_specs = [], []
    for shape, home, *dtype in outputs:
        dtype = dtype[0] if dtype else F32
        out_specs.append(pl.BlockSpec(memory_space=VMEM))
        out_shape.append(
            VMEM(shape, dtype) if home == "near" else jax.ShapeDtypeStruct(shape, dtype)
        )
    return pl.pallas_call(
        body,
        name=name,
        out_shape=out_shape,
        in_specs=in_specs,
        out_specs=out_specs,
        scratch_shapes=list(scratch),
        cost_estimate=pl.CostEstimate(flops=weight, bytes_accessed=1, transcendentals=0),
        compiler_params=pltpu.CompilerParams(vmem_limit_bytes=GRANT),
    )(*arrays)


def lanes(row):
    total = row[:, 0:128]
    for col in range(128, row.shape[1], 128):
        total = total + row[:, col : col + 128]
    return total


def iotas(shape):
    return (
        lax.broadcasted_iota(jnp.int32, shape, 0),
        lax.broadcasted_iota(jnp.int32, shape, 1),
    )


def up(field, axis):
    return pltpu.roll(field, field.shape[axis] - 1, axis)


def down(field, axis):
    return pltpu.roll(field, 1, axis)


def taps(a, b, c):
    i, y = iotas(a.shape)
    rows, cols = a.shape
    return (
        1.0 - 4.0 * c,
        jnp.where(i < rows - 1, c - a, 0.0),
        jnp.where(i > 0, c + a, 0.0),
        jnp.where(y < cols - 1, c - b, 0.0),
        jnp.where(y > 0, c + b, 0.0),
    )


def forward(state, coeffs):
    mid, east, west, north, south = coeffs
    return (
        mid * state
        + east * up(state, 0)
        + west * down(state, 0)
        + north * up(state, 1)
        + south * down(state, 1)
    )


def adjoint(state, coeffs):
    mid, east, west, north, south = coeffs
    return (
        mid * state
        + down(east * state, 0)
        + up(west * state, 0)
        + down(north * state, 1)
        + up(south * state, 1)
    )


EDGE = ("mid_low", "mid_high", "north_low", "north_high", "south_low", "south_high")
EDGE += ("west_low", "west_next", "east_high", "east_next", "east_low", "west_high")


def begin_body(count, *refs):
    sources, targets = refs[:count], refs[count : 2 * count]
    once_ref, high_ref, low_ref, edge_ref, sems = refs[2 * count :]
    s_ref, a_ref, b_ref, c_ref = targets[:4]
    levels, rows, _ = s_ref.shape
    last = rows - 1
    cut = levels // PARTS
    parts = [
        [
            pltpu.make_async_copy(
                sources[n].at[pl.ds(part * cut, cut)],
                targets[n].at[pl.ds(part * cut, cut)],
                sems.at[part * 4 + n],
            )
            for n in range(4)
        ]
        for part in range(PARTS)
    ]
    rest = [
        pltpu.make_async_copy(sources[n], targets[n], sems.at[4 * (PARTS - 1) + n])
        for n in range(4, count)
    ]
    for copy in sum(parts, []) + rest:
        copy.start()
    for lev in range(levels):
        if lev % cut == 0:
            for copy in parts[lev // cut]:
                copy.wait()
        s, a, b, c = s_ref[lev], a_ref[lev], b_ref[lev], c_ref[lev]
        coeffs = taps(a, b, c)
        once = forward(s, coeffs)
        once_ref[lev] = once
        mid, east, west, north, south = coeffs
        at = pl.ds(lev, 1)
        open_east = c[last : last + 1] - a[last : last + 1]
        open_west = c[0:1] + a[0:1]
        high_ref[0, at] = s[last : last + 1]
        high_ref[1, at] = once[last : last + 1]
        high_ref[2, at] = open_east
        high_ref[3, at] = b[last : last + 1]
        high_ref[4, at] = c[last : last + 1]
        low_ref[0, at] = s[0:1]
        low_ref[1, at] = once[0:1]
        low_ref[2, at] = open_west
        low_ref[3, at] = b[0:1]
        low_ref[4, at] = c[0:1]
        rows_of = {
            "mid_low": mid[0:1],
            "mid_high": mid[last : last + 1],
            "north_low": north[0:1],
            "north_high": north[last : last + 1],
            "south_low": south[0:1],
            "south_high": south[last : last + 1],
            "west_low": open_west,
            "west_next": west[1:2],
            "east_high": open_east,
            "east_next": east[last - 1 : last],
            "east_low": east[0:1],
            "west_high": west[last : last + 1],
        }
        for n, key in enumerate(EDGE):
            edge_ref[n, at] = rows_of[key]
    for copy in rest:
        copy.wait()


def forward_body(a_ref, b_ref, c_ref, once_ref, moved_ref):
    for lev in range(a_ref.shape[0]):
        coeffs = taps(a_ref[lev], b_ref[lev], c_ref[lev])
        moved_ref[lev] = forward(once_ref[lev], coeffs)


def adjoint_body(a_ref, b_ref, c_ref, later_ref, back_ref):
    for lev in range(a_ref.shape[0]):
        coeffs = taps(a_ref[lev], b_ref[lev], c_ref[lev])
        back_ref[lev] = adjoint(adjoint(later_ref[lev], coeffs), coeffs)


def outer_products(k, later):
    def once(side, at, beside):
        mid, north, south = k["mid_" + side], k["north_" + side], k["south_" + side]
        return mid * at + beside + down(north * at, 1) + up(south * at, 1)

    west, east = k["west_low"], k["east_high"]
    return (
        (west * later[0], west * once("low", later[0], k["west_next"] * later[1])),
        (east * later[3], east * once("high", later[3], k["east_next"] * later[2])),
    )


def rims_body(four, edge_ref, later_ref, high_ref, low_ref, first_ref, second_ref):
    position, peers = lax.axis_index("tm"), lax.axis_size("tm")
    odd = lax.rem(lax.axis_index("tile") + 1, 2)
    k = {key: edge_ref[n] for n, key in enumerate(EDGE)}
    levels, rows, _ = later_ref.shape
    later = [
        jnp.concatenate([later_ref[lev, row : row + 1] for lev in range(levels)], 0)
        for row in (0, 1, rows - 2, rows - 1)
    ]
    products = outer_products(k, later)
    zero = jnp.zeros(later[0].shape, F32)
    sent = []
    for ref, product, outer, inside, beside in (
        (low_ref, products[0], later[0], later[1], k["west_next"]),
        (high_ref, products[1], later[3], later[2], k["east_next"]),
    ):
        out = [ref[0], ref[1], ref[2], *product, zero]
        if four:
            second, final = position == 1, position == peers - 1
            out[0] = jnp.where(final, outer, out[0])
            out[1] = jnp.where(final, inside, out[1])
            out[3] = jnp.where(second, ref[3], out[3])
            out[4] = jnp.where(second, ref[4], out[4])
            out[5] = jnp.where(second, beside, zero)
        sent.append(out)
    for n, (low, high) in enumerate(zip(*sent)):
        first_ref[n] = jnp.where(odd == 0, high, low)
        second_ref[n] = jnp.where(odd == 0, low, high)


def sides(first, second):
    tile, tiles = lax.axis_index("tile"), lax.axis_size("tile")
    odd = lax.rem(tile + 1, 2)
    below, above = jnp.where(odd == 0, second, first), jnp.where(odd == 0, first, second)
    return jnp.where(tile > 0, below, 0.0), jnp.where(tile < tiles - 1, above, 0.0)


def own_sides(first, second):
    odd = lax.rem(lax.axis_index("tile") + 1, 2)
    return jnp.where(odd == 0, second, first), jnp.where(odd == 0, first, second)


def back_fix(k, product, stepped, own_product, toward):
    def across(x, side):
        mid, north, south = k["mid_" + side], k["north_" + side], k["south_" + side]
        return mid * x + down(north * x, 1) + up(south * x, 1)

    return (
        across(product[0], "low") + (stepped[0] + toward[0] * own_product[0]),
        k["east_low"] * product[0],
        k["west_high"] * product[1],
        across(product[1], "high") + (stepped[1] + toward[1] * own_product[1]),
    )


def edges_of(first_ref, second_ref, got_first_ref, got_second_ref, edge_ref):
    k = {key: edge_ref[n] for n, key in enumerate(EDGE)}
    state, stepped, toward, product, product_stepped = (
        sides(got_first_ref[n], got_second_ref[n]) for n in range(5)
    )
    own_state = own_sides(first_ref[0], second_ref[0])
    own_product = own_sides(first_ref[3], second_ref[3])

    def along(x, side):
        mid, north, south = k["mid_" + side], k["north_" + side], k["south_" + side]
        return mid * x + north * up(x, 1) + south * down(x, 1)

    new_low, new_high = k["west_low"] * state[0], k["east_high"] * state[1]
    moved = (
        along(new_low, "low") + k["west_low"] * (stepped[0] + toward[0] * own_state[0]),
        k["west_next"] * new_low,
        k["east_next"] * new_high,
        along(new_high, "high") + k["east_high"] * (stepped[1] + toward[1] * own_state[1]),
    )
    back = back_fix(k, product, product_stepped, own_product, toward)
    return moved, back, (state[0], stepped[0], state[1], stepped[1])


def edges_body(*refs):
    *in_refs, fix_ref = refs
    moved, back, _ = edges_of(*in_refs)
    wanted = lax.axis_index("tm") < lax.axis_size("tm") - 1
    for n in range(4):
        fix_ref[n] = moved[n]
        fix_ref[4 + n] = jnp.where(wanted, back[n], 0.0)


def late_body(rows, got_first_ref, got_second_ref, edge_ref, cross_ref, late_ref, fix_ref):
    k = {key: edge_ref[n] for n, key in enumerate(EDGE)}
    levels, cols = edge_ref.shape[1:]
    _, y = iotas((levels, cols))
    toward, drift, diffuse, beside = (
        sides(got_first_ref[n], got_second_ref[n]) for n in range(2, 6)
    )
    product, stepped, own = [], [], []
    for side in range(2):
        near_by, far_off = late_ref[2 * side], late_ref[2 * side + 1]
        b, c = drift[side], diffuse[side]
        north, south = jnp.where(y < cols - 1, c - b, 0.0), jnp.where(y > 0, c + b, 0.0)
        once = (1.0 - 4.0 * c) * near_by + beside[side] * far_off
        once = once + down(north * near_by, 1) + up(south * near_by, 1)
        product.append(toward[side] * near_by)
        stepped.append(toward[side] * once)
        row = side * (rows - 1)
        outer = [cross_ref[lev * rows + row : lev * rows + row + 1] for lev in range(levels)]
        own.append(k[("west_low", "east_high")[side]] * jnp.concatenate(outer, 0))
    for n, fix in enumerate(back_fix(k, product, stepped, own, toward)):
        fix_ref[n] = fix


def beyond_body(a_ref, b_ref, c_ref, cross_ref, back_ref):
    levels, rows, _ = a_ref.shape
    for lev in range(levels):
        coeffs = taps(a_ref[lev], b_ref[lev], c_ref[lev])
        cross = cross_ref[lev * rows : (lev + 1) * rows]
        back_ref[lev] = adjoint(adjoint(cross, coeffs), coeffs)


def thirds(x):
    one = x.astype(jnp.bfloat16)
    rest = x - one.astype(F32)
    two = rest.astype(jnp.bfloat16)
    return one, two, (rest - two.astype(F32)).astype(jnp.bfloat16)


def slot_masks(cell, lines, cols):
    slots = cell.shape[1]
    at_line = iotas((lines, slots))[0] == cell // cols
    at_col = iotas((cols, slots))[0] == lax.rem(cell, cols)
    return at_line, jnp.where(at_col, 1.0, 0.0).astype(jnp.bfloat16)


def spread_body(
    incr_ref, mult_ref, rhs_ref, err_ref, cell_ref, dual_ref, valid_ref, local_ref, held_ref
):
    levels, rows, cols = incr_ref.shape
    lines = levels * rows
    at_line, at_col = slot_masks(cell_ref[...], lines, cols)
    weights = thirds(jnp.where(at_line, valid_ref[...] * dual_ref[...], 0.0))
    spread = lax.dot_general(
        jnp.concatenate(weights, 0), at_col, (((1,), (1,)), ((), ())), preferred_element_type=F32
    )
    ht = spread[:lines] + spread[lines : 2 * lines] + spread[2 * lines :]
    mult = mult_ref[...]
    held_ref[...] = mult + ht.reshape(levels, rows, cols)
    local_ref[...] = rhs_ref[...] - (err_ref[...] * mult + incr_ref[...])


def gather_body(
    incr_ref, cell_ref, dual_ref, want_ref, var_ref, valid_ref, dir_ref, sums_ref
):
    levels, rows, cols = incr_ref.shape
    lines = levels * rows
    at_line, at_col = slot_masks(cell_ref[...], lines, cols)
    fields = thirds(incr_ref[...].reshape(lines, cols))
    picked = jnp.dot(jnp.concatenate(fields, 0), at_col, preferred_element_type=F32)
    picked = picked[:lines] + picked[lines : 2 * lines] + picked[2 * lines :]
    valid, var = valid_ref[...], var_ref[...]
    hx = jnp.sum(jnp.where(at_line, picked, 0.0), axis=0, keepdims=True) * valid
    res = valid * (want_ref[...] - (var * dual_ref[...] + hx))
    direction = res / var
    dir_ref[...] = direction
    sums_ref[0] = res * direction
    sums_ref[1] = direction * direction


def corrected(field, fix):
    rows = field.shape[0]
    i, _ = iotas(field.shape)
    for n, row in enumerate((0, 1, rows - 2, rows - 1)):
        field = field + jnp.where(i == row, fix[n], 0.0)
    return field


def fixes(ref, start, lev):
    return [ref[start + n, pl.ds(lev, 1)] for n in range(4)]


def share_body(
    first_ref, second_ref, got_first_ref, got_second_ref, edge_ref,
    local_ref, moved_ref, held_ref, back_ref, own_ref, urgent_ref, late_ref,
):
    position = lax.axis_index("tm")
    first, low_pair = lax.rem(position, 2) == 0, position < 2
    fix_moved, fix_back, beyond = edges_of(
        first_ref, second_ref, got_first_ref, got_second_ref, edge_ref
    )
    for n in range(4):
        late_ref[n] = jnp.where(low_pair, fix_moved[n], beyond[n])
    for lev in range(local_ref.shape[0]):
        back = corrected(back_ref[lev], [x[lev : lev + 1] for x in fix_back])
        moved = corrected(moved_ref[lev], [x[lev : lev + 1] for x in fix_moved])
        local = local_ref[lev]
        residual = held_ref[lev] - jnp.where(first, back, 0.0)
        own_ref[0, lev] = local
        own_ref[1, lev] = moved
        own_ref[2, lev] = residual
        urgent_ref[lev] = jnp.where(low_pair, local + moved, residual)


def sends_body(own_ref, got_ref, send_ref):
    low_pair = lax.axis_index("tm") < 2
    for lev in range(own_ref.shape[1]):
        mine = jnp.where(low_pair, own_ref[0, lev], own_ref[2, lev])
        send_ref[lev] = mine + got_ref[lev]


def rest_body(own_ref, obs_ref, *out_refs):
    levels = own_ref.shape[1]
    low_pair = lax.axis_index("tm") < 2
    blocks = [(ref, n) for ref in out_refs for n in range(ref.shape[0])]
    for lev in range(levels):
        ref, n = blocks[lev]
        ref[n] = own_ref[0, lev]
        ref, n = blocks[levels + lev]
        ref[n] = jnp.where(low_pair, own_ref[2, lev], own_ref[1, lev])
    ref, n = blocks[2 * levels]
    ref[n] = jnp.zeros(ref.shape[1:], F32)
    for i in range(2):
        ref[n, i : i + 1, 0:128] = lanes(obs_ref[i])


def terms_body(cross_ref, late_ref, beyond_ref, own_ref, got_ref, fix_ref, *refs):
    low_pair = lax.axis_index("tm") < 2
    _, levels, rows, _ = own_ref.shape
    *rest_refs, terms_ref, known_ref = refs
    blocks = [(ref, n) for ref in rest_refs for n in range(ref.shape[0])]
    for lev in range(levels):
        got = got_ref[lev]
        local, residual = own_ref[0, lev], own_ref[2, lev]
        back = corrected(beyond_ref[lev], fixes(fix_ref, 0, lev))
        moved = corrected(cross_ref[lev * rows : (lev + 1) * rows], fixes(late_ref, 0, lev))
        rest0, rest1 = (ref[n] for ref, n in (blocks[lev], blocks[levels + lev]))
        terms_ref[0, lev] = jnp.where(low_pair, rest0, residual)
        terms_ref[1, lev] = jnp.where(low_pair, local, residual) + got
        terms_ref[2, lev] = jnp.where(low_pair, residual - back, rest0 + moved)
        terms_ref[3, lev] = jnp.where(low_pair, rest1, local + rest1)
        known_ref[lev] = jnp.where(low_pair, local, residual + got)


def dots_body(terms_ref, got_ref, rest_ref, obs_ref, keep_ref, give_ref, sums_ref):
    _, levels, rows, cols = terms_ref.shape
    low_pair = lax.axis_index("tm") < 2
    numer, denom = jnp.zeros((8, 128), F32), jnp.zeros((8, 128), F32)

    def folded(x):
        total = None
        for r in range(0, rows, 8):
            part = lanes(x[r : r + 8])
            total = part if total is None else total + part
        return total

    for lev in range(levels):
        y0, one, z0, z1 = (terms_ref[n, lev] for n in range(4))
        two = got_ref[lev] + z0
        three = two + z1
        numer = numer + folded(y0 * y0 + (one - y0) * one + z0 * two + z1 * three)
        denom = denom + folded(y0 * y0 + one * one + two * two + three * three)
        keep_ref[0, lev] = jnp.where(low_pair, one, three)
        keep_ref[1, lev] = jnp.where(low_pair, two, y0)
        give_ref[lev] = jnp.where(low_pair, three, two)
    for n, total in enumerate((numer, denom)):
        obs = lanes(obs_ref[n]) + rest_ref[rest_ref.shape[0] - 1, n : n + 1, 0:128]
        sums_ref[n : n + 1] = jnp.sum(total, axis=0, keepdims=True) + obs


def update_body(
    mult_ref, incr_ref, dual_ref, dir_ref, keep_ref, known_ref, got_ref, sums_ref,
    new_m_ref, new_i_ref, new_o_ref,
):
    position = lax.axis_index("tm")
    leads, low_pair = lax.rem(position, 2) == 1, position < 2
    total = jnp.sum(sums_ref[...], axis=1, keepdims=True)
    step = total[0:1] / total[1:2]
    for lev in range(mult_ref.shape[0]):
        known, got = known_ref[lev], got_ref[lev]
        model = jnp.where(leads, keep_ref[0, lev], jnp.where(low_pair, known, got))
        back = jnp.where(leads, keep_ref[1, lev], jnp.where(low_pair, got, known))
        new_m_ref[lev] = mult_ref[lev] + step * model
        new_i_ref[lev] = incr_ref[lev] - step * back
    new_o_ref[...] = dual_ref[...] + step * dir_ref[...]


def exchange(value, partner):
    groups, tiles, peers = (lax.axis_size(x) for x in ("groups", "tile", "tm"))
    pairs = []
    for g in range(groups):
        for t in range(tiles):
            for k in range(peers):
                to_g, to_t, to_k = partner(g, t, k)
                target = (to_g * tiles + to_t) * peers + to_k
                pairs.append(((g * tiles + t) * peers + k, target))
    return lax.ppermute(value, ("groups", "tile", "tm"), pairs)


def swap(value, axis, distance):
    return lax.ppermute(value, axis, [(i, i ^ distance) for i in range(lax.axis_size(axis))])


def aside(g, t, k):
    return (g ^ 1, t, k) if lax.axis_size("groups") % 2 == 0 else (g, t ^ 1, k)


def leaders(value, tile, tm):
    few = value.shape[0] == 2

    def partner(g, t, k):
        if k % 2:
            return g, t ^ tile, k ^ tm
        return (g, t, k ^ 2) if few else aside(g, t, k)

    return exchange(value, partner)


def next_pair(g, t, k):
    if 0 < k < lax.axis_size("tm") - 1:
        return g, t, (k - 1 if k % 2 == 0 else k + 1)
    return aside(g, t, k)


def second_side(g, t, k):
    if 0 < t < lax.axis_size("tile") - 1:
        return g, (t - 1 if t % 2 == 0 else t + 1), k
    return g, t, k ^ 1


def shifted(value, steps):
    count = lax.axis_size("tm")
    pairs = [(i, i + steps) for i in range(count) if 0 <= i + steps < count]
    return lax.ppermute(value, "tm", pairs)


def scanned(value, direction):
    reach = 1
    while reach < lax.axis_size("tm"):
        value = value + shifted(value, direction * reach)
        reach *= 2
    return value


def reduced(value, axis):
    distance = 1
    while distance < lax.axis_size(axis):
        value = value + swap(value, axis, distance)
        distance *= 2
    return value


def near(*arrays):
    return [(x, "near") for x in arrays]


def shards(
    multiplier, increment, obs_dual, rhs_model, rhs_obs, model_err, obs_err,
    drift_east, drift_north, diffusion, obs_cell, obs_count,
):
    tiles, peers = lax.axis_size("tile"), lax.axis_size("tm")
    levels, rows, cols = multiplier.shape[1:]
    field = ((levels, rows, cols), "near")
    lines = lambda n: ((n, levels, cols), "near")

    inner = swap(multiplier[0], "tm", 1)
    arguments = [increment[0], drift_east[0], drift_north[0], diffusion[0], multiplier[0]]
    arguments += [rhs_model[0], model_err[0], obs_cell, obs_dual, rhs_obs, obs_err]
    count = len(arguments)
    *here, once, high, low, edge = kernel_call(
        lambda *refs: begin_body(count, *refs),
        "begin",
        [(x, "far") for x in arguments],
        [(x.shape, "near", x.dtype) for x in arguments]
        + [field, lines(5), lines(5), lines(len(EDGE))],
        [pltpu.SemaphoreType.DMA((count + 4 * (PARTS - 1),))],
    )
    incr, *coeffs = here[:4]
    mult, rhs, err, cell, dual, want, var = here[4:]
    four = peers == 4
    if four:
        later = inner
    else:
        later = jnp.where(lax.axis_index("tm") % 2 == 0, inner, exchange(mult, next_pair))
    first, second = kernel_call(
        lambda *refs: rims_body(four, *refs),
        "rims",
        near(edge, later, high, low),
        [lines(6), lines(6)],
    )
    got_front = exchange(second, lambda g, t, k: (g, t ^ 1, k) if t % 4 < 2 else (g, t, k ^ 1))
    once, second = lax.optimization_barrier((once, second))
    moved = kernel_call(forward_body, "forward", near(*coeffs, once), [field])[0]
    moved, first, second, incr = lax.optimization_barrier((moved, first, second, incr))
    got_first = exchange(first, second_side)
    got_back = exchange(second, lambda g, t, k: (g, t, k ^ 1) if t % 4 < 2 else (g, t ^ 1, k))
    got_second = jnp.where(lax.axis_index("tile") % 4 < 2, got_front, got_back)
    valid = (lax.broadcasted_iota(jnp.int32, obs_cell.shape, 1) < obs_count).astype(F32)
    local, held = kernel_call(
        spread_body, "spread", near(incr, mult, rhs, err, cell, dual, valid), [field] * 2
    )
    rims = near(first, second, got_first, got_second, edge)
    if not four:
        fix = kernel_call(edges_body, "edges", rims, [lines(8)])[0]
        later = jnp.where(lax.axis_index("tm") == peers - 1, 0.0, later)
        back = kernel_call(adjoint_body, "adjoint", near(*coeffs, later), [field])[0]
        dir_obs, obs_sums = kernel_call(
            gather_body,
            "gather",
            near(incr, cell, dual, want, var, valid),
            [(obs_dual.shape, "near"), ((2, *obs_dual.shape), "near")],
        )
        return scan_path(
            multiplier, increment, obs_dual, local, moved, held, back, fix, dir_obs, obs_sums
        )
    cross = jnp.where(lax.axis_index("tm") < 2, moved, inner).reshape(levels * rows, cols)
    got_cross = leaders(jnp.pad(cross, ((0, rows), (0, 0))), 0, 2)
    back = kernel_call(adjoint_body, "adjoint", near(*coeffs, inner), [field])[0]
    own, urgent, late = kernel_call(
        share_body,
        "share",
        rims + near(local, moved, held, back),
        [((3, levels, rows, cols), "near"), field, lines(4)],
    )
    got_late = leaders(late, 0, 2)
    got = swap(urgent, "tm", 1)
    send = kernel_call(sends_body, "sends", near(own, got), [field])[0]
    send, own, cell = lax.optimization_barrier((send, own, cell))
    got_send = leaders(send, 0, 2)
    dir_obs, obs_sums = kernel_call(
        gather_body,
        "gather",
        near(incr, cell, dual, want, var, valid),
        [(obs_dual.shape, "near"), ((2, *obs_dual.shape), "near")],
    )
    parts = [-(-(2 * levels + 1) // 3)] * 2
    parts.append(2 * levels + 1 - sum(parts))
    rest = kernel_call(
        rest_body, "rest", near(own, obs_sums), [((n, rows, cols), "near") for n in parts]
    )
    got_rest = [swap(x, "tm", 1) for x in rest]
    late_fix = kernel_call(
        lambda *refs: late_body(rows, *refs),
        "late",
        near(got_first, got_second, edge, got_cross, got_late),
        [lines(4)],
        weight=WEIGHT,
    )[0]
    beyond = kernel_call(beyond_body, "beyond", near(*coeffs, got_cross), [field])[0]
    terms, known = kernel_call(
        terms_body,
        "terms",
        near(got_cross, got_late, beyond, own, got, late_fix, *got_rest),
        [((4, levels, rows, cols), "near"), field],
    )
    pair = ((2, levels, rows, cols), "near")
    keep, give, sums = kernel_call(
        dots_body, "dots", near(terms, got_send, got_rest[-1], obs_sums), [pair, field, ((2, 128), "near")]
    )
    total = sums + leaders(sums, 0, 2) + leaders(sums, 1, 0) + leaders(sums, 1, 2)
    distance = 2
    while distance < tiles:
        total = total + leaders(total, distance, 0)
        distance *= 2
    got_dir = swap(give, "tm", 1)
    other = swap(total, "tm", 1)
    total = jnp.where(lax.axis_index("tm") % 2 == 1, total, other)
    new_m, new_i, new_o = kernel_call(
        update_body,
        "update",
        near(mult, incr, dual, dir_obs, keep, known, got_dir, total),
        [(mult.shape, "far"), (mult.shape, "far"), (obs_dual.shape, "far")],
    )
    return new_m[None], new_i[None], new_o


def scan_path(multiplier, increment, obs_dual, local, moved, held, back, fix, dir_obs, obs_sums):
    rows = local.shape[1]
    fix = jnp.moveaxis(fix, 0, 1)
    at = jnp.array([0, 1, rows - 2, rows - 1])
    moved = moved.at[:, at].add(fix[:, :4])
    res_incr = -(held - back.at[:, at].add(fix[:, 4:8]))
    res_model = local + shifted(moved, 1)
    dir_model, dir_incr = scanned(res_model, 1), scanned(res_incr, -1)
    numer = jnp.sum(res_model * dir_model) + jnp.sum(res_incr * dir_incr) + jnp.sum(obs_sums[0])
    denom = jnp.sum(dir_model**2) + jnp.sum(dir_incr**2) + jnp.sum(obs_sums[1])
    sums = reduced(reduced(jnp.stack([numer, denom]), "tm"), "tile")
    step = sums[0] / sums[1]
    return (
        multiplier + step * dir_model[None],
        increment + step * dir_incr[None],
        obs_dual + step * dir_obs,
    )


def solution(mesh):
    grid = P(("groups", "tm"), None, "tile", None)
    line = P(("groups", "tm"), "tile")
    return jax.shard_map(
        shards,
        mesh=mesh,
        in_specs=(grid, grid, line, grid, line, grid, line, grid, grid, grid, line, line),
        out_specs=(grid, grid, line),
        check_vma=False,
    )
```
